32 devices in a mesh: az: 8 (over z, x), rad: 4 (over y, core).
Axes of the slice: x: 2, y: 2, z: 4, core: 2. Of those that a mesh axis runs over, the one named last changes fastest.
Arguments:
- potential: float32 [3, 3, 2048, 512], P(None, None, 'az', 'rad'), may hold values from -6 to 6
- current: float32 [3, 3, 2048, 512], P(None, None, 'az', 'rad'), may hold values from -24 to 24
- material: int32 [3, 2048, 512], P(None, 'az', 'rad'), may hold values from 0 to 7
- nu_table: float32 [8], replicated, may hold values from 0.2 to 2
- sat_table: float32 [8], replicated, may hold values from 0.2 to 3
- panel_flux: float32 [9, 2048], P(None, 'az'), may hold values from -48 to 48
- panel_jitter: int32 [2048], P('az'), may hold values from 0 to 2047
- rotor_offset: int32 [1], replicated, may hold values from 0 to 2047
Outputs:
- updated: float32 [3, 3, 2048, 512], P(None, None, 'az', 'rad')
The draws below stay inside these ranges and needn't reach their ends.
All inputs are finite; a program needn't handle non-finite values.
Results may differ from the reference program's by a relative error of at most 0.000064.
Values sent between devices are 32-bit elements; how exact they have to be, the bound alone decides.
No kernel may reach another device: no remote copies, remote signals or barrier semaphores. Data moves between devices by JAX's collectives and lax.ppermute only.
A program may use at most 64 MiB of HBM per device.

```python
import math
import jax
import jax.numpy as jnp

L = 3
MAT = 8
NA = 2048
NR = 512
NPAN = 2048


def with_ends(array, key, low, largest):
    longest = array.shape.index(max(array.shape))
    spots = []
    for shift in (0, 1):
        where = [jax.random.randint(jax.random.fold_in(key, axis), (), 0, length) for axis, length in enumerate(array.shape)]
        where[longest] = (where[longest] + shift) % array.shape[longest]
        spots.append(tuple(where))
    return array.at[spots[0]].set(low).at[spots[1]].set(largest)


def level_of(key, shape, pieces, low, largest):
    def one(dim, parts):
        heights = jax.random.uniform(jax.random.fold_in(jax.random.fold_in(key, 6), dim), (parts,), jnp.float32, low / len(pieces), largest / len(pieces))
        return jnp.repeat(jnp.exp(heights), shape[dim] // parts).reshape((-1,) + (1,) * (len(shape) - dim - 1))

    loudness = one(*pieces[0])
    for cut in pieces[1:]:
        loudness = loudness * one(*cut)
    return loudness


def bell_draw(rng, dims, scale, bound, split=(), kind=jnp.bfloat16):
    level = level_of(rng, dims, split, -0.22, 0.18) if split else 1.0
    drawn = jax.random.normal(rng, dims, jnp.float32) * scale * level
    return jnp.minimum(jnp.maximum(drawn, -bound), bound).astype(kind)


def setup_inputs(seed: int = 0) -> dict:
    key_list = jax.random.split(jax.random.key(seed), 9)
    potential = bell_draw(key_list[0], (3, L, NA, NR), 1.0, 6.0, ((2, 8), (3, 4)), jnp.float32)
    current = bell_draw(key_list[1], (3, L, NA, NR), 4.0, 24.0, ((2, 8), (3, 4)), jnp.float32)
    material = with_ends(jax.random.randint(key_list[2], (L, NA, NR), 0, MAT), jax.random.fold_in(key_list[2], 1), 0, MAT - 1).astype(jnp.int32)
    nu_table = jnp.clip(jnp.exp(jax.random.uniform(key_list[3], (MAT,), jnp.float32, math.log(0.2), math.log(2.0))), 0.2, 2.0)
    sat_table = jnp.clip(jnp.exp(jax.random.uniform(key_list[4], (MAT,), jnp.float32, math.log(0.2), math.log(3.0))), 0.2, 3.0)
    panel_flux = bell_draw(key_list[5], (3 * L, NPAN), 8.0, 48.0, ((1, 8),), jnp.float32)
    panel_jitter = with_ends(jax.random.randint(key_list[6], (NPAN,), 0, NA), jax.random.fold_in(key_list[6], 1), 0, NA - 1).astype(jnp.int32)
    rotor_offset = jax.random.randint(key_list[7], (1,), 0, NA).astype(jnp.int32)
    return dict(potential=potential, current=current, material=material, nu_table=nu_table, sat_table=sat_table, panel_flux=panel_flux, panel_jitter=panel_jitter, rotor_offset=rotor_offset)


sigma_term = 1.0
neighbour_steps = ((0, 1, 0), (0, -1, 0), (0, 0, 1), (0, 0, -1), (1, 0, 0), (-1, 0, 0))


def lookup(material, values_table):
    result = jnp.zeros(material.shape, values_table.dtype)
    for entry in range(values_table.shape[0]):
        result = result + jnp.where(material == entry, values_table[entry], jnp.zeros((), values_table.dtype))
    return result


def extend_cells(field):
    wrapped = jnp.concatenate([field[:, :, -1:], field, field[:, :, :1]], axis=2)
    return jnp.pad(wrapped, ((0, 0), (0, 0), (0, 0), (1, 1)))


def strength(extended):
    centre = extended[:, :, 1:-1, 1:-1]
    azimuth_diff = extended[:, :, 2:, 1:-1] - centre
    radial_diff = extended[:, :, 1:-1, 2:] - centre
    return jnp.sum(azimuth_diff * azimuth_diff + radial_diff * radial_diff, axis=0, keepdims=True)


def offset_view(field, layer_step, az_step, rad_step):
    return field[:, 1 + layer_step:field.shape[1] - 1 + layer_step, 1 + az_step:field.shape[2] - 1 + az_step, 1 + rad_step:field.shape[3] - 1 + rad_step]


def jacobi_sweep(field, coef, source):
    padded_field = jnp.pad(field, ((0, 0), (1, 1), (0, 0), (0, 0)))
    padded_coef = jnp.pad(coef, ((0, 0), (1, 1), (0, 0), (0, 0)))
    centre = offset_view(padded_coef, 0, 0, 0)
    numerator = source
    denominator = jnp.full_like(centre, sigma_term)
    for layer_step, az_step, rad_step in neighbour_steps:
        face_coef = 0.5 * (centre + offset_view(padded_coef, layer_step, az_step, rad_step))
        numerator = numerator + face_coef * offset_view(padded_field, layer_step, az_step, rad_step)
        denominator = denominator + face_coef
    return numerator / denominator


def reference(potential, current, material, nu_table, sat_table, panel_flux, panel_jitter, rotor_offset):
    position = (rotor_offset[0] + panel_jitter) % NA
    airgap = jax.ops.segment_sum(panel_flux.T, position, num_segments=NA).T.reshape(3, L, NA)
    source = current.at[:, :, :, NR // 2].add(airgap)
    base_reluct = lookup(material, nu_table)[None]
    saturation = lookup(material, sat_table)[None]
    extended = extend_cells(potential)
    flux_sq = strength(extended)
    reluct = base_reluct * (1.0 + saturation * flux_sq / (1.0 + flux_sq))
    reluct_wide = extend_cells(reluct)
    sweep_one = jacobi_sweep(extended, reluct_wide, source)
    return jacobi_sweep(extend_cells(sweep_one), reluct_wide, source)
```

```python
import functools

import jax
import jax.numpy as jnp
from jax import lax
from jax.experimental import pallas as pl
from jax.experimental.pallas import tpu as pltpu
from jax.sharding import PartitionSpec as P

sigma_term = 1.0
halo = 3
low_own, high_own = 6, 5
slot = low_own + high_own
f32 = jnp.float32
VMEM = pl.BlockSpec(memory_space=pltpu.VMEM)
SMEM = pl.BlockSpec(memory_space=pltpu.SMEM)


def params(mib=48):
    return pltpu.CompilerParams(vmem_limit_bytes=mib * 1024 * 1024)


def rim_rows(fields, layers):
    return halo * (fields + layers) + fields


def round_up(n, m):
    return (n + m - 1) // m * m


def slot_base(j, cols):
    per = cols // slot
    return (j // per) * cols + (j % per) * slot


def lookup(material, table):
    values = [table[e] for e in range(table.shape[0])]
    bit = 1
    while len(values) > 1:
        take = (material & bit) != 0
        values = [jnp.where(take, values[i + 1], values[i]) for i in range(0, len(values), 2)]
        bit *= 2
    return values[0]


def half_reluct(base, saturation, flux_sq):
    return (0.5 * base) * (1.0 + saturation * flux_sq / (1.0 + flux_sq))


def sweep_cells(coef, field, source, moves):
    layers = len(coef)
    out = [[None] * layers for _ in field]
    for l in range(layers):
        centre = coef[l]
        total = jnp.full_like(centre, sigma_term)
        num = [source[c][l] for c in range(len(field))]
        for move_coef, move_field in moves:
            w = centre + move_coef(l)
            total = total + w
            for c in range(len(field)):
                num[c] = num[c] + w * move_field(c, l)
        for other in (l + 1, l - 1):
            if 0 <= other < layers:
                w = centre + coef[other]
                total = total + w
                for c in range(len(field)):
                    num[c] = num[c] + w * field[c][other]
            else:
                total = total + centre
        inverse = 1.0 / total
        for c in range(len(field)):
            out[c][l] = num[c] * inverse
    return out


def pack_kernel(
    cycle, off_ref, pot_ref, cur_ref, mat_ref, flux_ref, jit_ref, strips_ref, re_ref, ro_ref, pan_ref, slots_ref
):
    fields, layers = pot_ref.shape[0], mat_ref.shape[0]
    rows, cols = mat_ref.shape[1:]
    total = 2 * fields + layers
    per = cols // slot
    groups = -(-total // per)
    odd = lax.rem(lax.axis_index("rad"), 2) == 1

    panels = flux_ref.shape[1]
    where = jit_ref[...] + off_ref[0]
    where = jnp.where(where >= cycle, where - cycle, where).astype(f32)
    for h in range(panels // 128):
        at = h * (fields + 1)
        pan_ref[at : at + fields, :] = flux_ref[:, h * 128 : (h + 1) * 128]
        pan_ref[at + fields : at + fields + 1, :] = where[:, h * 128 : (h + 1) * 128]

    lane = lax.broadcasted_iota(jnp.int32, (8, cols), 1)

    @pl.loop(0, rows // 8, unroll=2)
    def _(i):
        at = pl.ds(pl.multiple_of(i * 8, 8), 8)
        for g in range(groups):
            acc = None
            for k in range(min(per, total - g * per)):
                j = g * per + k
                if j < fields:
                    x = pot_ref[j, at, :]
                elif j < fields + layers:
                    x = mat_ref[j - fields, at, :].astype(f32)
                else:
                    x = cur_ref[j - fields - layers, at, :]
                x = pltpu.roll(x, (k * slot + high_own) % cols, 1)
                acc = x if acc is None else jnp.where(lane >= k * slot, x, acc)
            slots_ref[g, at, :] = acc

    for g in range(groups):
        strips_ref[g * cols : (g + 1) * cols, :] = slots_ref[g].T
    for j in range(total):
        b = slot_base(j, cols)
        if j < fields + layers:
            left, right, n, to = b + high_own, b + high_own - halo, halo, halo * j
        else:
            left, right, n, to = b + high_own, b + high_own - 1, 1, halo * (fields + layers) + j - fields - layers
        lo, hi = strips_ref[left : left + n, :], strips_ref[right : right + n, :]
        re_ref[to : to + n, :] = jnp.where(odd, lo, hi)
        ro_ref[to : to + n, :] = jnp.where(odd, hi, lo)


def pack(offset, pot, cur, mat, flux, jitter, cycle):
    fields, rows, cols = pot.shape
    layers = mat.shape[0]
    total = 2 * fields + layers
    groups = -(-total // (cols // slot))
    send = round_up(rim_rows(fields, layers), 8)
    panels = flux.shape[1]
    return pl.pallas_call(
        functools.partial(pack_kernel, cycle),
        out_shape=[
            jax.ShapeDtypeStruct((groups * cols, rows), f32),
            jax.ShapeDtypeStruct((send, rows), f32),
            jax.ShapeDtypeStruct((send, rows), f32),
            jax.ShapeDtypeStruct((panels // 128 * (fields + 1), 128), f32),
        ],
        in_specs=[SMEM] + [VMEM] * 5,
        out_specs=[VMEM] * 4,
        scratch_shapes=[pltpu.VMEM((groups, rows, cols), f32)],
        compiler_params=params(),
        cost_estimate=pl.CostEstimate(flops=40_000_000, bytes_accessed=3_000_000, transcendentals=0),
        name="pack_columns",
    )(offset, pot, cur, mat, flux, jitter)


def middle_kernel(
    n_pans, strips_ref, re_ref, ro_ref, pt, pb, ct, cb, mt, mb, *refs
):
    pan_refs, (ext_ref, even_ref, odd_ref, pans_ref, up_ref, down_ref) = refs[:n_pans], refs[n_pans:]
    fields, layers = pt.shape[0], mt.shape[0]
    rows = strips_ref.shape[1]
    cols = pt.shape[2]
    total = 2 * fields + layers
    odd_r = lax.rem(lax.axis_index("rad"), 2) == 1
    odd_a = lax.rem(lax.axis_index("az"), 2) == 1
    scalars = halo * (fields + layers)

    at = 0
    for ref in pan_refs:
        pans_ref[at : at + ref.shape[0], :] = ref[...]
        at += ref.shape[0]

    lane = lax.broadcasted_iota(jnp.int32, (16, 128), 1)
    up = down = None
    for j in range(total):
        b = slot_base(j, cols)
        ext_ref[j, 0:8, :] = strips_ref[b + high_own - 2 : b + high_own + 6, :]
        ext_ref[j, 8:16, :] = strips_ref[b : b + 8, :]
        if j < fields + layers:
            s = halo * j
            ext_ref[j, 0:2, :] = jnp.where(odd_r, re_ref[s + 1 : s + 3, :], ro_ref[s + 1 : s + 3, :])
            ext_ref[j, 13:16, :] = jnp.where(odd_r, ro_ref[s : s + 3, :], re_ref[s : s + 3, :])
        else:
            s = scalars + j - fields - layers
            ext_ref[j, 1:2, :] = jnp.where(odd_r, re_ref[s : s + 1, :], ro_ref[s : s + 1, :])
            ext_ref[j, 13:14, :] = jnp.where(odd_r, ro_ref[s : s + 1, :], re_ref[s : s + 1, :])
        first = pltpu.roll(ext_ref[j, :, 0:128], 4 * j, 1)
        last = pltpu.roll(ext_ref[j, :, rows - 128 : rows], (4 * j + halo) % 128, 1)
        up = first if up is None else jnp.where(lane >= 4 * j, first, up)
        down = last if down is None else jnp.where(lane >= 4 * j, last, down)

    for j in range(fields):
        up_ref[halo * j : halo * j + halo, :] = pt[j, 0:halo, :]
        down_ref[halo * j : halo * j + halo, :] = pb[j, 8 - halo : 8, :]
        up_ref[scalars + j : scalars + j + 1, :] = ct[j, 0:1, :]
        down_ref[scalars + j : scalars + j + 1, :] = cb[j, 7:8, :]
    for l in range(layers):
        s = halo * (fields + l)
        up_ref[s : s + halo, :] = mt[l, 0:halo, :].astype(f32)
        down_ref[s : s + halo, :] = mb[l, 8 - halo : 8, :].astype(f32)
    n = up_ref.shape[0]
    even_ref[0:n, :] = jnp.where(odd_a, up_ref[...], down_ref[...])
    odd_ref[0:n, :] = jnp.where(odd_a, down_ref[...], up_ref[...])
    even_ref[n : n + 16, :] = jnp.where(odd_a, up, down)
    odd_ref[n : n + 16, :] = jnp.where(odd_a, down, up)
    even_ref[n + 16 :, :] = pans_ref[...]
    odd_ref[n + 16 :, :] = pans_ref[...]


def edge_specs(lead, rows, cols):
    last = rows // 8 - 1
    return [
        pl.BlockSpec((lead, 8, cols), lambda i: (0, 0, 0)),
        pl.BlockSpec((lead, 8, cols), lambda i: (0, last, 0)),
    ]


def whole(shape):
    return pl.BlockSpec(shape, lambda i: (0,) * len(shape))


def middle(strips, re_got, ro_got, pot, cur, mat, pans):
    fields, rows, cols = pot.shape
    layers = mat.shape[0]
    total = 2 * fields + layers
    send = round_up(rim_rows(fields, layers), 8)
    pan_rows = sum(p.shape[0] for p in pans)
    out_shape = [
        jax.ShapeDtypeStruct((total, 16, rows), f32),
        jax.ShapeDtypeStruct((send + 16 + pan_rows, cols), f32),
        jax.ShapeDtypeStruct((send + 16 + pan_rows, cols), f32),
        jax.ShapeDtypeStruct((pan_rows, cols), f32),
    ]
    return pl.pallas_call(
        functools.partial(middle_kernel, len(pans)),
        grid=(1,),
        out_shape=out_shape,
        in_specs=[whole(strips.shape), whole(re_got.shape), whole(ro_got.shape)]
        + edge_specs(fields, rows, cols)
        + edge_specs(fields, rows, cols)
        + edge_specs(layers, rows, cols)
        + [whole(p.shape) for p in pans],
        out_specs=[whole(o.shape) for o in out_shape],
        scratch_shapes=[pltpu.VMEM((send, cols), f32), pltpu.VMEM((send, cols), f32)],
        compiler_params=params(),
        cost_estimate=pl.CostEstimate(flops=5_000_000, bytes_accessed=1_000_000, transcendentals=0),
        name="pack_rows",
    )(strips, re_got, ro_got, pot, pot, cur, cur, mat, mat, *pans)


def tile_kernel(nu_ref, sat_ref, pot_hbm, cur_ref, mat_ref, out_ref, pot_ref, coef_ref, one_ref, sem):
    fields, rows, cols = out_ref.shape
    layers = mat_ref.shape[0]
    comps = fields // layers
    copy = pltpu.make_async_copy(pot_hbm, pot_ref.at[:, 8 : 8 + rows, :], sem)
    copy.start()
    blank = jnp.zeros((8, cols), f32)
    for j in range(fields):
        for ref in (pot_ref, one_ref):
            ref[j, 0:8, :] = blank
            ref[j, 8 + rows : 16 + rows, :] = blank
    for l in range(layers):
        coef_ref[l, 0:8, :] = blank
        coef_ref[l, 8 + rows : 16 + rows, :] = blank
    copy.wait()

    def shifted(ref, j, i, step):
        return ref[j, pl.ds(i * 8 + 8 + step, 8), :]

    def right(x):
        return pltpu.roll(x, cols - 1, 1)

    def left(x):
        return pltpu.roll(x, 1, 1)

    @pl.loop(0, rows // 8, unroll=2)
    def _(i):
        own = pl.ds(pl.multiple_of(i * 8, 8), 8)
        for l in range(layers):
            flux_sq = None
            for c in range(comps):
                centre = shifted(pot_ref, c * layers + l, i, 0)
                az = shifted(pot_ref, c * layers + l, i, 1) - centre
                rad = right(centre) - centre
                part = az * az + rad * rad
                flux_sq = part if flux_sq is None else flux_sq + part
            material = mat_ref[l, own, :]
            coef_ref[l, pl.ds(pl.multiple_of(i * 8 + 8, 8), 8), :] = half_reluct(
                lookup(material, nu_ref), lookup(material, sat_ref), flux_sq
            )

    def sweep(field_ref, store):
        @pl.loop(0, rows // 8, unroll=2)
        def _(i):
            own = pl.ds(pl.multiple_of(i * 8, 8), 8)
            coef = [shifted(coef_ref, l, i, 0) for l in range(layers)]
            field = [[shifted(field_ref, c * layers + l, i, 0) for l in range(layers)] for c in range(comps)]
            source = [[cur_ref[c * layers + l, own, :] for l in range(layers)] for c in range(comps)]
            moves = []
            for step in (1, -1):
                moves.append(
                    (
                        lambda l, step=step: shifted(coef_ref, l, i, step),
                        lambda c, l, step=step: shifted(field_ref, c * layers + l, i, step),
                    )
                )
            for turn in (right, left):
                moves.append((lambda l, turn=turn: turn(coef[l]), lambda c, l, turn=turn: turn(field[c][l])))
            new = sweep_cells(coef, field, source, moves)
            for c in range(comps):
                for l in range(layers):
                    store(c * layers + l, i, new[c][l])

    def store_one(j, i, x):
        one_ref[j, pl.ds(pl.multiple_of(i * 8 + 8, 8), 8), :] = x

    def store_two(j, i, x):
        out_ref[j, pl.ds(pl.multiple_of(i * 8, 8), 8), :] = x

    sweep(pot_ref, store_one)
    sweep(one_ref, store_two)


def tile(nu, sat, pot, cur, mat):
    fields, rows, cols = pot.shape
    layers = mat.shape[0]
    return pl.pallas_call(
        tile_kernel,
        out_shape=jax.ShapeDtypeStruct(pot.shape, f32),
        in_specs=[SMEM, SMEM, pl.BlockSpec(memory_space=pl.ANY), VMEM, VMEM],
        out_specs=VMEM,
        scratch_shapes=[
            pltpu.VMEM((fields, rows + 16, cols), f32),
            pltpu.VMEM((layers, rows + 16, cols), f32),
            pltpu.VMEM((fields, rows + 16, cols), f32),
            pltpu.SemaphoreType.DMA,
        ],
        compiler_params=params(),
        cost_estimate=pl.CostEstimate(flops=40_000_000, bytes_accessed=4_000_000, transcendentals=0),
        name="tile",
    )(nu, sat, pot, cur, mat)


def deposit(air_ref, vals_ref, blocks, fields, rows, base, cycle):
    lanes = vals_ref.shape[1]
    vals_ref[...] = jnp.zeros_like(vals_ref)
    for t, (ref, at) in enumerate(blocks):
        vals_ref[0 : fields + 1, t * 128 : (t + 1) * 128] = ref[at : at + fields + 1, :]
    values = vals_ref[...]
    local = vals_ref[fields : fields + 1, :].astype(jnp.int32) - base
    local = jnp.where(local < -1, local + cycle, local)
    local = jnp.where(local > rows, local - cycle, local)
    spot = lax.broadcasted_iota(jnp.int32, (rows, lanes), 0)
    onehot = jnp.where(spot == local, 1.0, 0.0).astype(jnp.bfloat16)
    high = values.astype(jnp.bfloat16)
    rest = values - high.astype(f32)
    mid = rest.astype(jnp.bfloat16)
    low = (rest - mid.astype(f32)).astype(jnp.bfloat16)
    parts = lax.dot_general(
        jnp.concatenate([high, mid, low], axis=0),
        onehot,
        (((1,), (1,)), ((), ())),
        preferred_element_type=f32,
    )
    air_ref[:, 0:rows] = parts[0:16] + parts[16:32] + parts[32:48]
    after = jnp.sum(jnp.where(local == rows, values, 0.0), axis=1, keepdims=True)
    before = jnp.sum(jnp.where((local == -1) | (local == cycle - 1), values, 0.0), axis=1, keepdims=True)
    lane = lax.broadcasted_iota(jnp.int32, (16, 128), 1)
    air_ref[:, rows : rows + 128] = jnp.where(lane == 0, after, jnp.where(lane == 127, before, 0.0))


def rim_kernel(
    cycle, nu_ref, sat_ref, main_ref, even_ref, odd_ref, two_ref, pans_ref, ext_ref, pt, pb, ct, cb, mt, mb,
    out_ref, rows_ref, cols_ref, vals_ref, air_ref, back_ref,
):
    fields, layers = pt.shape[0], mt.shape[0]
    comps = fields // layers
    rows, cols = main_ref.shape[1:]
    total = 2 * fields + layers
    scalars = halo * (fields + layers)
    r, a = lax.axis_index("rad"), lax.axis_index("az")
    size = lax.axis_size("rad")
    odd_a = lax.rem(a, 2) == 1
    send = round_up(rim_rows(fields, layers), 8)

    stator = (r == size // 2) | (r == size // 2 - 1)
    air_ref[...] = jnp.zeros_like(air_ref)

    @pl.when(stator)
    def _():
        n = pans_ref.shape[0]
        blocks = []
        for ref, at in ((pans_ref, 0), (even_ref, send + 16), (odd_ref, send + 16), (two_ref, 0)):
            blocks += [(ref, at + k * (fields + 1)) for k in range(n // (fields + 1))]
        deposit(air_ref, vals_ref, blocks, fields, rows, a * rows, cycle)

    def before(at, n):
        return jnp.where(odd_a, even_ref[at : at + n, :], odd_ref[at : at + n, :])

    def after(at, n):
        return jnp.where(odd_a, odd_ref[at : at + n, :], even_ref[at : at + n, :])

    rows_ref[...] = jnp.zeros_like(rows_ref)
    for j in range(total):
        if j < fields + layers:
            rows_ref[j, 8 - halo : 8, :] = before(halo * j, halo)
            rows_ref[j, 24 : 24 + halo, :] = after(halo * j, halo)
        else:
            s = scalars + j - fields - layers
            rows_ref[j, 7:8, :] = before(s, 1)
            rows_ref[j, 24:25, :] = after(s, 1)
        if j < fields:
            top, bottom = pt[j], pb[j]
        elif j < fields + layers:
            top, bottom = mt[j - fields].astype(f32), mb[j - fields].astype(f32)
        else:
            top, bottom = ct[j - fields - layers], cb[j - fields - layers]
        rows_ref[j, 8:16, :] = top
        rows_ref[j, 16:24, :] = bottom

    def solve(get, axis_az, axis_rad, inside, source):
        pot = [[get(c * layers + l) for l in range(layers)] for c in range(comps)]
        if inside is not None:
            pot = [[jnp.where(inside, x, 0.0) for x in part] for part in pot]
        shape = pot[0][0].shape

        def move(x, axis, step):
            return pltpu.roll(x, (-step) % shape[axis], axis)

        coef = []
        for l in range(layers):
            flux_sq = None
            for c in range(comps):
                az = move(pot[c][l], axis_az, 1) - pot[c][l]
                rad = move(pot[c][l], axis_rad, 1) - pot[c][l]
                part = az * az + rad * rad
                flux_sq = part if flux_sq is None else flux_sq + part
            material = get(fields + l).astype(jnp.int32)
            k = half_reluct(lookup(material, nu_ref), lookup(material, sat_ref), flux_sq)
            coef.append(k if inside is None else jnp.where(inside, k, 0.0))

        moved = {}

        def moves_of(field):
            table = []
            for axis in (axis_az, axis_rad):
                for step in (1, -1):
                    def coef_at(l, axis=axis, step=step):
                        key = (l, axis, step)
                        if key not in moved:
                            moved[key] = move(coef[l], axis, step)
                        return moved[key]

                    table.append((coef_at, lambda c, l, axis=axis, step=step: move(field[c][l], axis, step)))
            return table

        one = sweep_cells(coef, pot, source, moves_of(pot))
        if inside is not None:
            one = [[jnp.where(inside, x, 0.0) for x in part] for part in one]
        return sweep_cells(coef, one, source, moves_of(one))

    source = [[rows_ref[fields + layers + c * layers + l] for l in range(layers)] for c in range(comps)]
    fixed_rows = solve(lambda j: rows_ref[j], 0, 1, None, source)

    lane = lax.broadcasted_iota(jnp.int32, (16, 128), 1)
    corner_before, corner_after = before(send, 16), after(send, 16)
    for j in range(total):
        cols_ref[j, :, 0:rows] = ext_ref[j]
        cols_ref[j, :, rows : rows + 128] = jnp.where(
            lane < 64,
            pltpu.roll(corner_after, (-4 * j) % 128, 1),
            pltpu.roll(corner_before, (128 - halo - 4 * j) % 128, 1),
        )
    column = lax.broadcasted_iota(jnp.int32, (16, rows + 128), 0)
    inside = ((column >= 2) | (r > 0)) & ((column < 13) | (r < size - 1))
    target = jnp.where(r == size // 2, 2, jnp.where(r == size // 2 - 1, 13, -1))
    source = []
    for c in range(comps):
        source.append([])
        for l in range(layers):
            j = c * layers + l
            source[c].append(cols_ref[fields + layers + j] + jnp.where(column == target, air_ref[j : j + 1, :], 0.0))
    fixed_cols = solve(lambda j: cols_ref[j], 1, 0, inside, source)

    for c in range(comps):
        for l in range(layers):
            j = c * layers + l
            back_ref[8 * j : 8 * j + 3, :] = fixed_cols[c][l][10:13, 0:rows]
            back_ref[8 * j + 3 : 8 * j + 5, :] = fixed_cols[c][l][2:4, 0:rows]
    turned = back_ref[...].T

    lane = lax.broadcasted_iota(jnp.int32, (rows, cols), 1)
    edge = (lane < 2) | (lane >= cols - 3)
    for c in range(comps):
        for l in range(layers):
            j = c * layers + l
            main_ref[j, 0:2, :] = fixed_rows[c][l][8:10]
            main_ref[j, rows - 3 : rows, :] = fixed_rows[c][l][21:24]
            out_ref[j] = jnp.where(edge, pltpu.roll(turned, (cols - 3 - 8 * j) % cols, 1), main_ref[j])


def rims(nu, sat, main, even_got, odd_got, two_got, pans, ext, pot, cur, mat, cycle):
    fields, rows, cols = pot.shape
    layers = mat.shape[0]
    total = 2 * fields + layers
    panels = 4 * pans.shape[0] // (fields + 1) * 128
    arrays = (main, even_got, odd_got, two_got, pans, ext)
    return pl.pallas_call(
        functools.partial(rim_kernel, cycle),
        grid=(1,),
        out_shape=jax.ShapeDtypeStruct(pot.shape, f32),
        in_specs=[SMEM, SMEM]
        + [whole(x.shape) for x in arrays]
        + edge_specs(fields, rows, cols)
        + edge_specs(fields, rows, cols)
        + edge_specs(layers, rows, cols),
        out_specs=whole(pot.shape),
        scratch_shapes=[
            pltpu.VMEM((total, 32, cols), f32),
            pltpu.VMEM((total, 16, rows + 128), f32),
            pltpu.VMEM((16, panels), f32),
            pltpu.VMEM((16, rows + 128), f32),
            pltpu.VMEM((128, rows), f32),
        ],
        compiler_params=params(),
        name="rims",
    )(nu, sat, *arrays, pot, pot, cur, cur, mat, mat)


def local(potential, current, material, nu_table, sat_table, panel_flux, panel_jitter, rotor_offset):
    comps, layers, rows, cols = potential.shape
    fields = comps * layers
    az, rad = lax.axis_size("az"), lax.axis_size("rad")
    cycle = rows * az
    pot = potential.reshape(fields, rows, cols)
    cur = current.reshape(fields, rows, cols)

    def swap(x, az_of, rad_of):
        pairs = [(a * rad + r, az_of(a) * rad + rad_of(r)) for a in range(az) for r in range(rad)]
        return lax.ppermute(x, ("az", "rad"), pairs)

    def same(i):
        return i

    def even(i):
        return i ^ 1

    def odd(i, n):
        return (i + 1) % n if i % 2 else (i - 1) % n

    strips, re_send, ro_send, pan = pack(
        rotor_offset, pot, cur, material, panel_flux, panel_jitter.reshape(1, -1), cycle
    )
    re_got = swap(re_send, same, even)
    ro_got = swap(ro_send, same, lambda r: odd(r, rad))
    pans = [pan]
    bit = az // 2
    while bit >= 4:
        held = pans[0] if len(pans) == 1 else jnp.concatenate(pans, axis=0)
        pans = [held, swap(held, lambda a, bit=bit: a ^ bit, same)]
        bit //= 2
    ext, even_send, odd_send, held = middle(strips, re_got, ro_got, pot, cur, material, pans)
    two_got = swap(held, lambda a: a ^ 2, same)
    even_got = swap(even_send, even, same)
    odd_got = swap(odd_send, lambda a: odd(a, az), same)
    main = tile(nu_table, sat_table, pot, cur, material)
    out = rims(
        nu_table, sat_table, main, even_got, odd_got, two_got, held, ext, pot, cur, material, cycle
    )
    return out.reshape(potential.shape)


def solution(mesh):
    placed = (
        P(None, None, "az", "rad"),
        P(None, None, "az", "rad"),
        P(None, "az", "rad"),
        P(),
        P(),
        P(None, "az"),
        P("az"),
        P(),
    )
    return jax.shard_map(
        local, mesh=mesh, in_specs=placed, out_specs=P(None, None, "az", "rad"), check_vma=False
    )
```

```python
import functools

import jax
import jax.numpy as jnp
from jax import lax
from jax.experimental import pallas as pl
from jax.experimental.pallas import tpu as pltpu
from jax.sharding import PartitionSpec as P

sigma_term = 1.0
LIMIT = 60
halo = 3
low_own, high_own = 6, 5
slot = low_own + high_own
f32 = jnp.float32
VMEM = pl.BlockSpec(memory_space=pltpu.VMEM)
SMEM = pl.BlockSpec(memory_space=pltpu.SMEM)
HBM = pl.BlockSpec(memory_space=pltpu.HBM)
ANY = pl.BlockSpec(memory_space=pl.ANY)


def params(mib=48):
    return pltpu.CompilerParams(vmem_limit_bytes=mib * 1024 * 1024)


def layout(fields, layers):
    depth = [halo] * fields + [halo - 1] * layers + [1] * fields
    return [(n, sum(depth[:j])) for j, n in enumerate(depth)]


def rim_rows(fields, layers):
    return halo * fields + (halo - 1) * layers + fields


def slot_base(j, cols):
    per = cols // slot
    return (j // per) * cols + (j % per) * slot


def lookup(material, table):
    values = [table[e] for e in range(table.shape[0])]
    bit = 1
    while len(values) > 1:
        take = (material & bit) != 0
        values = [jnp.where(take, values[i + 1], values[i]) for i in range(0, len(values), 2)]
        bit *= 2
    return values[0]


def half_reluct(base, saturation, flux_sq):
    return (0.5 * base) * (1.0 + saturation * flux_sq / (1.0 + flux_sq))


def sweep_cells(coef, field, source, moves):
    layers = len(coef)
    out = [[None] * layers for _ in field]
    for l in range(layers):
        centre = coef[l]
        total = jnp.full_like(centre, sigma_term)
        num = [source[c][l] for c in range(len(field))]
        for move_coef, move_field in moves:
            w = centre + move_coef(l)
            total = total + w
            for c in range(len(field)):
                num[c] = num[c] + w * move_field(c, l)
        for other in (l + 1, l - 1):
            if 0 <= other < layers:
                w = centre + coef[other]
                total = total + w
                for c in range(len(field)):
                    num[c] = num[c] + w * field[c][other]
            else:
                total = total + centre
        inverse = 1.0 / total
        for c in range(len(field)):
            out[c][l] = num[c] * inverse
    return out


def divisor(n, most):
    return max(d for d in range(1, most + 1) if n % d == 0)


def half_strength(centres, az_next, rad_next):
    total = None
    for centre, az, rad in zip(centres, az_next, rad_next):
        az, rad = az - centre, rad - centre
        part = az * az + rad * rad
        total = part if total is None else total + part
    return total


def edges_kernel(
    cycle, off_ref, pot_hbm, cur_hbm, mat_hbm, flux_hbm, jit_hbm, odd_ref, even_ref, pan_ref,
    up_ref, down_ref, pot_ref, cur_ref, mat_ref, flux_ref, jit_ref, sems
):
    fields, layers = pot_ref.shape[1], mat_ref.shape[1]
    rows = pot_hbm.shape[1]
    pairs = [(flux_hbm, flux_ref), (jit_hbm, jit_ref)]
    for hbm, ref in ((pot_hbm, pot_ref), (cur_hbm, cur_ref), (mat_hbm, mat_ref)):
        pairs += [(hbm.at[:, 0:8, :], ref.at[0]), (hbm.at[:, rows - 8 : rows, :], ref.at[1])]
    copies = [pltpu.make_async_copy(src, dst, sems.at[n]) for n, (src, dst) in enumerate(pairs)]
    for copy in copies:
        copy.start()
    for copy in copies:
        copy.wait()

    odd_a = lax.rem(lax.axis_index("az"), 2) == 1
    panels = flux_ref.shape[1]
    where = jit_ref[...] + off_ref[0]
    where = jnp.where(where >= cycle, where - cycle, where).astype(f32)
    for h in range(panels // 128):
        at = h * (fields + 1)
        pan_ref[at : at + fields, :] = flux_ref[:, h * 128 : (h + 1) * 128]
        pan_ref[at + fields : at + fields + 1, :] = where[:, h * 128 : (h + 1) * 128]
    for j, (n, at) in enumerate(layout(fields, layers)):
        if j < fields:
            ref, k = pot_ref, j
        elif j < fields + layers:
            ref, k = mat_ref, j - fields
        else:
            ref, k = cur_ref, j - fields - layers
        up_ref[at : at + n, :] = ref[0, k, 0:n, :].astype(f32)
        down_ref[at : at + n, :] = ref[1, k, 8 - n : 8, :].astype(f32)
    n = up_ref.shape[0]
    even_ref[0:n, :] = jnp.where(odd_a, up_ref[...], down_ref[...])
    odd_ref[0:n, :] = jnp.where(odd_a, down_ref[...], up_ref[...])
    even_ref[n:, :] = pan_ref[...]
    odd_ref[n:, :] = pan_ref[...]


def edges(offset, pot, cur, mat, flux, jitter, cycle):
    fields, rows, cols = pot.shape
    layers = mat.shape[0]
    send = rim_rows(fields, layers)
    pan_rows = flux.shape[1] // 128 * (fields + 1)
    return pl.pallas_call(
        functools.partial(edges_kernel, cycle),
        out_shape=[
            jax.ShapeDtypeStruct((send + pan_rows, cols), f32),
            jax.ShapeDtypeStruct((send + pan_rows, cols), f32),
            jax.ShapeDtypeStruct((pan_rows, 128), f32),
        ],
        in_specs=[SMEM] + [HBM] * 5,
        out_specs=[VMEM] * 3,
        scratch_shapes=[
            pltpu.VMEM((send, cols), f32),
            pltpu.VMEM((send, cols), f32),
            pltpu.VMEM((2, fields, 8, cols), f32),
            pltpu.VMEM((2, fields, 8, cols), f32),
            pltpu.VMEM((2, layers, 8, cols), jnp.int32),
            pltpu.VMEM(flux.shape, f32),
            pltpu.VMEM(jitter.shape, jnp.int32),
            pltpu.SemaphoreType.DMA((8,)),
        ],
        compiler_params=params(LIMIT),
        cost_estimate=pl.CostEstimate(flops=1_000_000, bytes_accessed=400_000, transcendentals=0),
        name="pack_rows",
    )(offset, pot, cur, mat, flux, jitter)


def columns_kernel(pot_ref, cur_ref, mat_ref, strips_ref, slots_ref):
    fields, layers = pot_ref.shape[0], mat_ref.shape[0]
    rows, cols = mat_ref.shape[1:]
    total = 2 * fields + layers
    per = cols // slot
    groups = -(-total // per)
    lane = lax.broadcasted_iota(jnp.int32, (8, cols), 1)

    @pl.loop(0, rows // 8, unroll=8)
    def _(i):
        at = pl.ds(pl.multiple_of(i * 8, 8), 8)
        for g in range(groups):
            acc = None
            for k in range(min(per, total - g * per)):
                j = g * per + k
                if j < fields:
                    x = pot_ref[j, at, :]
                elif j < fields + layers:
                    x = mat_ref[j - fields, at, :].astype(f32)
                else:
                    x = cur_ref[j - fields - layers, at, :]
                x = pltpu.roll(x, (k * slot + high_own) % cols, 1)
                acc = x if acc is None else jnp.where(lane >= k * slot, x, acc)
            slots_ref[g, at, :] = acc

    for g in range(groups):
        strips_ref[g * cols : (g + 1) * cols, :] = slots_ref[g].T


def columns(pot, cur, mat):
    fields, rows, cols = pot.shape
    total = 2 * fields + mat.shape[0]
    groups = -(-total // (cols // slot))
    return pl.pallas_call(
        columns_kernel,
        out_shape=jax.ShapeDtypeStruct((groups * cols, rows), f32),
        in_specs=[VMEM] * 3,
        out_specs=VMEM,
        scratch_shapes=[pltpu.VMEM((groups, rows, cols), f32)],
        compiler_params=params(),
        cost_estimate=pl.CostEstimate(flops=8_000_000, bytes_accessed=3_000_000, transcendentals=0),
        name="turn_columns",
    )(pot, cur, mat)


def middle_kernel(fields, layers, odd_ref, even_ref, strips_ref, _coef, _air, ro_ref, re_ref, turned_ref, rim_ref):
    cols = even_ref.shape[1]
    send = rim_rows(fields, layers)
    odd_r = lax.rem(lax.axis_index("rad"), 2) == 1
    odd_a = lax.rem(lax.axis_index("az"), 2) == 1

    rim_ref[0:send, :] = jnp.where(odd_a, odd_ref[0:send, :], even_ref[0:send, :])
    rim_ref[64 : 64 + send, :] = jnp.where(odd_a, even_ref[0:send, :], odd_ref[0:send, :])
    turned_ref[...] = rim_ref[...].T

    for j, (n, at) in enumerate(layout(fields, layers)):
        b = slot_base(j, cols) + high_own
        lo, hi = strips_ref[b : b + n, :], strips_ref[b - n : b, :]
        re_ref[at : at + n, :] = jnp.where(odd_r, lo, hi)
        ro_ref[at : at + n, :] = jnp.where(odd_r, hi, lo)
    lo, hi = turned_ref[0:halo, :], turned_ref[cols - halo : cols, :]
    re_ref[send : send + halo, 0:128] = jnp.where(odd_r, lo, hi)
    ro_ref[send : send + halo, 0:128] = jnp.where(odd_r, hi, lo)


def middle(strips, odd_got, even_got, coef, air, fields, layers):
    cols = even_got.shape[1]
    rows = strips.shape[1]
    send = rim_rows(fields, layers)
    arrays = (odd_got, even_got, strips, coef, air)
    return pl.pallas_call(
        functools.partial(middle_kernel, fields, layers),
        out_shape=[
            jax.ShapeDtypeStruct((send + halo, rows), f32),
            jax.ShapeDtypeStruct((send + halo, rows), f32),
            jax.ShapeDtypeStruct((cols, 128), f32),
        ],
        in_specs=[VMEM] * 3 + [ANY] * 2,
        out_specs=[VMEM] * 3,
        scratch_shapes=[pltpu.VMEM((128, cols), f32)],
        compiler_params=params(),
        cost_estimate=pl.CostEstimate(flops=1_000_000, bytes_accessed=600_000, transcendentals=0),
        name="pack_columns",
    )(*arrays)


def block(i):
    return pl.ds(pl.multiple_of(i * 8, 8), 8)


def right(x):
    return pltpu.roll(x, x.shape[1] - 1, 1)


def left(x):
    return pltpu.roll(x, 1, 1)


def reluct_block(nu_ref, sat_ref, coef_ref, load, material, i):
    layers = coef_ref.shape[0]
    comps = 3
    for l in range(layers):
        centres = [load(c * layers + l, 0) for c in range(comps)]
        nexts = [load(c * layers + l, 1) for c in range(comps)]
        flux_sq = half_strength(centres, nexts, [right(x) for x in centres])
        which = material(l)
        coef_ref[l, block(i + 2), :] = half_reluct(lookup(which, nu_ref), lookup(which, sat_ref), flux_sq)


def sweep_block(coef_ref, load, source_at, i, store):
    layers = coef_ref.shape[0]
    comps = 3
    coef = [coef_ref[l, block(i + 2), :] for l in range(layers)]
    field = [[load(c * layers + l, 0) for l in range(layers)] for c in range(comps)]
    source = [[source_at(c * layers + l) for l in range(layers)] for c in range(comps)]
    moves = []
    for step in (1, -1):
        moves.append(
            (
                lambda l, step=step: coef_ref[l, pl.ds(i * 8 + 16 + step, 8), :],
                lambda c, l, step=step: load(c * layers + l, step),
            )
        )
    for turn in (right, left):
        moves.append((lambda l, turn=turn: turn(coef[l]), lambda c, l, turn=turn: turn(field[c][l])))
    new = sweep_cells(coef, field, source, moves)
    for c in range(comps):
        for l in range(layers):
            store(c * layers + l, new[c][l])


def keep(one_ref, i):
    def store(j, x):
        one_ref[j, block(i + 1), :] = x

    return store


def inner_kernel(nu_ref, sat_ref, pot_ref, cur_ref, mat_ref, coef_ref, one_ref):
    rows, cols = mat_ref.shape[1:]
    count = rows // 8
    inner = count - 2
    step = divisor(inner, 10)

    def load_at(i):
        return lambda j, step: pot_ref[j, pl.ds(i * 8 + step, 8), :]

    def reluct_at(i, load):
        reluct_block(nu_ref, sat_ref, coef_ref, load, lambda l: mat_ref[l, block(i), :], i)

    def last_load(j, step):
        x = pot_ref[j, rows - 8 : rows, :]
        return x if step == 0 else pltpu.roll(x, 7, 0)

    reluct_at(0, load_at(0))
    reluct_at(count - 1, last_load)

    @pl.loop(1, count - 1, unroll=step)
    def _(i):
        reluct_at(i, load_at(i))

    @pl.loop(1, count - 1, unroll=step)
    def _(i):
        sweep_block(coef_ref, load_at(i), lambda j: cur_ref[j, block(i), :], i, keep(one_ref, i))


def inner(nu, sat, pot, cur, mat):
    fields, rows, cols = pot.shape
    layers = mat.shape[0]
    return pl.pallas_call(
        inner_kernel,
        out_shape=[
            jax.ShapeDtypeStruct((layers, rows + 32, cols), f32),
            jax.ShapeDtypeStruct((fields, rows + 16, cols), f32),
        ],
        in_specs=[SMEM, SMEM] + [VMEM] * 3,
        out_specs=[VMEM, VMEM],
        compiler_params=params(),
        cost_estimate=pl.CostEstimate(flops=20_000_000, bytes_accessed=4_000_000, transcendentals=0),
        name="inner_rows",
    )(nu, sat, pot, cur, mat)


def outer_kernel(
    nu_ref, sat_ref, pot_ref, cur_ref, mat_ref, odd_ref, even_ref, coef_in, one_in, out_ref, coef_ref, one_ref, edge_ref
):
    fields, rows, cols = out_ref.shape
    layers = mat_ref.shape[0]
    odd_a = lax.rem(lax.axis_index("az"), 2) == 1
    count = rows // 8

    blank = jnp.zeros((8, cols), f32)
    for j, (n, at) in enumerate(layout(fields, layers)):
        if j < fields:
            ref, k = pot_ref, j
        elif j < fields + layers:
            ref, k = mat_ref, j - fields
        else:
            ref, k = cur_ref, j - fields - layers
        edge_ref[0, j, 0:8, :] = blank
        edge_ref[0, j, 8:16, :] = blank
        edge_ref[1, j, 16:24, :] = blank
        edge_ref[1, j, 24:32, :] = blank
        edge_ref[0, j, 16:32, :] = ref[k, 0:16, :].astype(f32)
        edge_ref[1, j, 0:16, :] = ref[k, rows - 16 : rows, :].astype(f32)
        even, odd = even_ref[at : at + n, :], odd_ref[at : at + n, :]
        edge_ref[0, j, 16 - n : 16, :] = jnp.where(odd_a, even, odd)
        edge_ref[1, j, 16 : 16 + n, :] = jnp.where(odd_a, odd, even)
    for l in range(layers):
        coef_ref[l, 0:8, :] = blank
        coef_ref[l, 24 + rows : 32 + rows, :] = blank

    def edge_load(k):
        side, at = k // 2, 8 + 8 * (k % 2)
        return (
            lambda j, step: edge_ref[side, j, at + step : at + step + 8, :],
            (-1, 0, count - 1, count)[k],
        )

    for k in (0, 2, 3):
        load, i = edge_load(k)
        reluct_block(nu_ref, sat_ref, coef_ref, load, lambda l: load(fields + l, 0).astype(jnp.int32), i)
    for k in range(4):
        load, i = edge_load(k)
        sweep_block(coef_ref, load, lambda j: load(fields + layers + j, 0), i, keep(one_ref, i))

    @pl.loop(0, count, unroll=divisor(count, 8))
    def _(i):
        def store(j, x):
            out_ref[j, block(i), :] = x

        sweep_block(
            coef_ref,
            lambda j, step: one_ref[j, pl.ds(i * 8 + 8 + step, 8), :],
            lambda j: cur_ref[j, block(i), :],
            i,
            store,
        )


def outer(nu, sat, pot, cur, mat, odd_got, even_got, coef, one):
    fields, rows, cols = pot.shape
    layers = mat.shape[0]
    total = 2 * fields + layers
    return pl.pallas_call(
        outer_kernel,
        out_shape=[
            jax.ShapeDtypeStruct(pot.shape, f32),
            jax.ShapeDtypeStruct(coef.shape, f32),
            jax.ShapeDtypeStruct(one.shape, f32),
        ],
        in_specs=[SMEM, SMEM] + [VMEM] * 7,
        out_specs=[VMEM] * 3,
        input_output_aliases={7: 1, 8: 2},
        scratch_shapes=[pltpu.VMEM((2, total, 32, cols), f32)],
        compiler_params=params(),
        cost_estimate=pl.CostEstimate(flops=20_000_000, bytes_accessed=4_000_000, transcendentals=0),
        name="outer_rows",
    )(nu, sat, pot, cur, mat, odd_got, even_got, coef, one)[0]


def deposit_kernel(cycle, starts, bases, fields, rows, *refs):
    n = len(starts)
    pan_refs, air_refs, vals_ref = refs[:n], refs[n + 1 : -1], refs[-1]
    r, a = lax.axis_index("rad"), lax.axis_index("az")
    size = lax.axis_size("rad")
    stator = (r == size // 2) | (r == size // 2 - 1)

    @pl.when(stator)
    def _():
        lanes = vals_ref.shape[1]
        vals_ref[...] = jnp.zeros_like(vals_ref)
        t = 0
        for ref, first in zip(pan_refs, starts):
            for at in range(first, ref.shape[0], fields + 1):
                vals_ref[0 : fields + 1, t * 128 : (t + 1) * 128] = ref[at : at + fields + 1, :]
                t += 1
        values = vals_ref[...]
        position = vals_ref[fields : fields + 1, :].astype(jnp.int32)
        high = values.astype(jnp.bfloat16)
        rest = values - high.astype(f32)
        mid = rest.astype(jnp.bfloat16)
        low = (rest - mid.astype(f32)).astype(jnp.bfloat16)
        split = jnp.concatenate([high, mid, low], axis=0)
        spot = lax.broadcasted_iota(jnp.int32, (rows, lanes), 0)
        lane = lax.broadcasted_iota(jnp.int32, (16, 128), 1)
        for air_ref, bit in zip(air_refs, bases):
            local = position - (a ^ bit) * rows
            onehot = jnp.where(spot == local, 1.0, 0.0).astype(jnp.bfloat16)
            parts = lax.dot_general(split, onehot, (((1,), (1,)), ((), ())), preferred_element_type=f32)
            air_ref[0:16, 0:rows] = parts[0:16] + parts[16:32] + parts[32:48]
            after = (local == rows) | (local == rows - cycle)
            before = (local == -1) | (local == cycle - 1)
            after = jnp.sum(jnp.where(after, values, 0.0), axis=1, keepdims=True)
            before = jnp.sum(jnp.where(before, values, 0.0), axis=1, keepdims=True)
            air_ref[16:32, 0:128] = jnp.where(lane == 0, after, jnp.where(lane == 127, before, 0.0))

    @pl.when(jnp.logical_not(stator))
    def _():
        for air_ref in air_refs:
            air_ref[...] = jnp.zeros_like(air_ref)


def deposit(pans, starts, coef, bases, fields, rows, cycle):
    layers = coef.shape[0]
    panels = sum(p.shape[0] - first for p, first in zip(pans, starts)) // (fields + 1) * 128
    return pl.pallas_call(
        functools.partial(deposit_kernel, cycle, starts, bases, fields, rows),
        out_shape=[jax.ShapeDtypeStruct((rim_rows(fields, layers) + halo, rows), f32) for _ in bases],
        in_specs=[VMEM] * len(pans) + [ANY],
        out_specs=[VMEM] * len(bases),
        scratch_shapes=[pltpu.VMEM((16, panels), f32)],
        compiler_params=params(),
        cost_estimate=pl.CostEstimate(flops=4_000_000, bytes_accessed=500_000, transcendentals=0),
        name="airgap",
    )(*pans, coef)


def rim_kernel(n_airs, nu_ref, sat_ref, main_ref, *refs):
    air_refs, (strips_ref, turned_ref, ro_ref, re_ref) = refs[:n_airs], refs[n_airs:-6]
    out_hbm, merged_ref, cols_ref, corner_ref, back_ref, sem = refs[-6:]
    fields, rows, cols = main_ref.shape
    total = cols_ref.shape[0]
    layers = total - 2 * fields
    comps = fields // layers
    send = rim_rows(fields, layers)
    r = lax.axis_index("rad")
    size = lax.axis_size("rad")
    odd_r = lax.rem(r, 2) == 1

    def left(at, n):
        return jnp.where(odd_r, re_ref[at : at + n, :], ro_ref[at : at + n, :])

    def right(at, n):
        return jnp.where(odd_r, ro_ref[at : at + n, :], re_ref[at : at + n, :])

    corner_ref[0:2, :] = left(send + 1, 2)[:, 0:128]
    corner_ref[2:8, :] = turned_ref[0:low_own, :]
    corner_ref[8:13, :] = turned_ref[cols - high_own : cols, :]
    corner_ref[13:16, :] = right(send, halo)[:, 0:128]
    corner = corner_ref[...]
    lane = lax.broadcasted_iota(jnp.int32, (16, 128), 1)
    for j, (n, at) in enumerate(layout(fields, layers)):
        b = slot_base(j, cols)
        cols_ref[j, 0:8, 0:rows] = strips_ref[b + high_own - 2 : b + high_own + 6, :]
        cols_ref[j, 8:16, 0:rows] = strips_ref[b : b + 8, :]
        m = min(n, 2)
        cols_ref[j, 2 - m : 2, 0:rows] = left(at + n - m, m)
        cols_ref[j, 13 : 13 + n, 0:rows] = right(at, n)
        cols_ref[j, :, rows : rows + 128] = jnp.where(
            lane < 64, pltpu.roll(corner, (-at) % 128, 1), pltpu.roll(corner, (64 - n - at) % 128, 1)
        )

    column = lax.broadcasted_iota(jnp.int32, (16, rows + 128), 0)
    inside = ((column >= 2) | (r > 0)) & ((column < 13) | (r < size - 1))
    target = jnp.where(r == size // 2, 2, jnp.where(r == size // 2 - 1, 13, -1))

    def move(x, axis, step):
        return pltpu.roll(x, (-step) % x.shape[axis], axis)

    pot = [[jnp.where(inside, cols_ref[c * layers + l], 0.0) for l in range(layers)] for c in range(comps)]
    source = []
    for c in range(comps):
        source.append([])
        for l in range(layers):
            j = c * layers + l
            air = sum(ref[j : j + 1, :] for ref in air_refs)
            outside = sum(ref[16 + j : 17 + j, 0:128] for ref in air_refs)
            air = jnp.concatenate([air, outside], axis=1)
            source[c].append(cols_ref[fields + layers + j] + jnp.where(column == target, air, 0.0))
    coef = []
    for l in range(layers):
        centres = [pot[c][l] for c in range(comps)]
        flux_sq = half_strength(centres, [move(x, 1, 1) for x in centres], [move(x, 0, 1) for x in centres])
        which = cols_ref[fields + l].astype(jnp.int32)
        k = half_reluct(lookup(which, nu_ref), lookup(which, sat_ref), flux_sq)
        coef.append(jnp.where(inside, k, 0.0))
    moves = [(axis, step) for axis in (1, 0) for step in (1, -1)]
    moved = {(l, m): move(coef[l], *m) for l in range(layers) for m in moves}

    def sweep(field):
        table = [
            (lambda l, m=m: moved[l, m], lambda c, l, m=m: move(field[c][l], *m)) for m in moves
        ]
        return sweep_cells(coef, field, source, table)

    one = [[jnp.where(inside, x, 0.0) for x in part] for part in sweep(pot)]
    fixed = sweep(one)
    for c in range(comps):
        for l in range(layers):
            j = c * layers + l
            back_ref[8 * j : 8 * j + 3, :] = fixed[c][l][10:13, 0:rows]
            back_ref[8 * j + 3 : 8 * j + 5, :] = fixed[c][l][2:4, 0:rows]
    turned = back_ref[...].T

    lane = lax.broadcasted_iota(jnp.int32, (rows, cols), 1)
    edge = (lane < 2) | (lane >= cols - 3)
    for j in range(fields):
        merged_ref[j] = jnp.where(edge, pltpu.roll(turned, (cols - 3 - 8 * j) % cols, 1), main_ref[j])
        pltpu.make_async_copy(merged_ref.at[j], out_hbm.at[j], sem.at[j]).start()
    for j in range(fields):
        pltpu.make_async_copy(merged_ref.at[j], out_hbm.at[j], sem.at[j]).wait()


def rims(nu, sat, main, strips, turned, ro_got, re_got, airs, layers):
    fields, rows, cols = main.shape
    total = 2 * fields + layers
    arrays = (main, *airs, strips, turned, ro_got, re_got)
    return pl.pallas_call(
        functools.partial(rim_kernel, len(airs)),
        out_shape=jax.ShapeDtypeStruct(main.shape, f32),
        in_specs=[SMEM, SMEM] + [VMEM] * len(arrays),
        out_specs=ANY,
        scratch_shapes=[
            pltpu.VMEM(main.shape, f32),
            pltpu.VMEM((total, 16, rows + 128), f32),
            pltpu.VMEM((16, 128), f32),
            pltpu.VMEM((128, rows), f32),
            pltpu.SemaphoreType.DMA((fields,)),
        ],
        compiler_params=params(),
        name="rims",
    )(nu, sat, *arrays)


def local(potential, current, material, nu_table, sat_table, panel_flux, panel_jitter, rotor_offset):
    comps, layers, rows, cols = potential.shape
    fields = comps * layers
    az, rad = lax.axis_size("az"), lax.axis_size("rad")
    cycle = rows * az
    pot = potential.reshape(fields, rows, cols)
    cur = current.reshape(fields, rows, cols)

    def swap(x, az_of, rad_of):
        pairs = [(a * rad + r, az_of(a) * rad + rad_of(r)) for a in range(az) for r in range(rad)]
        return lax.ppermute(x, ("az", "rad"), pairs)

    def same(i):
        return i

    def even(i):
        return i ^ 1

    def odd(i, n):
        return (i + 1) % n if i % 2 else (i - 1) % n

    odd_send, even_send, pan = edges(
        rotor_offset, pot, cur, material, panel_flux, panel_jitter.reshape(1, -1), cycle
    )
    odd_got = swap(odd_send, lambda a: odd(a, az), same)
    even_got = swap(even_send, even, same)
    two_got = swap(pan, lambda a: a ^ 2, same)
    strips = columns(pot, cur, material)
    coef, one = inner(nu_table, sat_table, pot, cur, material)
    at = rim_rows(fields, layers)
    pans, starts = [pan, odd_got, even_got, two_got], [0, at, at, 0]
    if az > 8:
        held, bit = jnp.concatenate([p[first:] for p, first in zip(pans, starts)], axis=0), 8
        while bit < az:
            held = jnp.concatenate([held, swap(held, lambda a, bit=bit: a ^ bit, same)], axis=0)
            bit *= 2
        pans, starts = [held], [0]
    if az > 4:
        air, air_send = deposit(pans, starts, coef, [0, 4], fields, rows, cycle)
        airs = [air, swap(air_send, lambda a: a ^ 4, same)]
    else:
        airs = deposit(pans, starts, coef, [0], fields, rows, cycle)
    ro_send, re_send, turned = middle(strips, odd_got, even_got, coef, airs[0], fields, layers)
    ro_got = swap(ro_send, same, lambda r: odd(r, rad))
    re_got = swap(re_send, same, even)
    main = outer(nu_table, sat_table, pot, cur, material, odd_got, even_got, coef, one)
    out = rims(nu_table, sat_table, main, strips, turned, ro_got, re_got, airs, layers)
    return out.reshape(potential.shape)


def solution(mesh):
    placed = (
        P(None, None, "az", "rad"),
        P(None, None, "az", "rad"),
        P(None, "az", "rad"),
        P(),
        P(),
        P(None, "az"),
        P("az"),
        P(),
    )
    return jax.shard_map(
        local, mesh=mesh, in_specs=placed, out_specs=P(None, None, "az", "rad"), check_vma=False
    )
```

```python
import functools

import jax
import jax.numpy as jnp
from jax import lax
from jax.experimental import pallas as pl
from jax.experimental.pallas import tpu as pltpu
from jax.sharding import PartitionSpec as P

sigma_term = 1.0
LIMIT = 60
EXPAND = 20_000_000_000
halo = 3
low_own, high_own = 6, 5
slot = low_own + high_own
f32 = jnp.float32
VMEM = pl.BlockSpec(memory_space=pltpu.VMEM)
HBM = pl.BlockSpec(memory_space=pltpu.HBM)
ANY = pl.BlockSpec(memory_space=pl.ANY)


def params(mib=48):
    return pltpu.CompilerParams(vmem_limit_bytes=mib * 1024 * 1024)


def layout(fields, layers):
    depth = [halo] * fields + [halo - 1] * layers + [1] * fields
    return [(n, sum(depth[:j])) for j, n in enumerate(depth)]


def rim_rows(fields, layers):
    return halo * fields + (halo - 1) * layers + fields


def slot_base(j, cols):
    per = cols // slot
    return (j // per) * cols + (j % per) * slot


def lookup(material, table_ref, first):
    rows, lanes = material.shape
    values = []
    for e in range(first, first + table_ref.shape[0] // 2):
        row = jnp.broadcast_to(table_ref[e : e + 1, :], (rows, 128))
        values.append(jnp.concatenate([row] * (lanes // 128), axis=1))
    bit = 1
    while len(values) > 1:
        take = (material & bit) != 0
        values = [jnp.where(take, values[i + 1], values[i]) for i in range(0, len(values), 2)]
        bit *= 2
    return values[0]


def half_reluct(table_ref, material, flux_sq):
    base = lookup(material, table_ref, 0)
    saturation = lookup(material, table_ref, table_ref.shape[0] // 2)
    return (0.5 * base) * (1.0 + saturation * flux_sq / (1.0 + flux_sq))


def sweep_cells(coef, field, source, moves):
    layers = len(coef)
    out = [[None] * layers for _ in field]
    for l in range(layers):
        centre = coef[l]
        total = jnp.full_like(centre, sigma_term)
        num = [source[c][l] for c in range(len(field))]
        for move_coef, move_field in moves:
            w = centre + move_coef(l)
            total = total + w
            for c in range(len(field)):
                num[c] = num[c] + w * move_field(c, l)
        for other in (l + 1, l - 1):
            if 0 <= other < layers:
                w = centre + coef[other]
                total = total + w
                for c in range(len(field)):
                    num[c] = num[c] + w * field[c][other]
            else:
                total = total + centre
        inverse = 1.0 / total
        for c in range(len(field)):
            out[c][l] = num[c] * inverse
    return out


def divisor(n, most):
    return max(d for d in range(1, most + 1) if n % d == 0)


def half_strength(centres, az_next, rad_next):
    total = None
    for centre, az, rad in zip(centres, az_next, rad_next):
        az, rad = az - centre, rad - centre
        part = az * az + rad * rad
        total = part if total is None else total + part
    return total


def edges_kernel(
    cycle, off_hbm, nu_hbm, sat_hbm, pot_hbm, cur_hbm, mat_hbm, flux_hbm, jit_hbm, odd_ref, even_ref, pan_ref, table_ref,
    up_ref, down_ref, pot_ref, cur_ref, mat_ref, flux_ref, jit_ref, off_ref, nu_ref, sat_ref, sems
):
    fields, layers = pot_ref.shape[1], mat_ref.shape[1]
    rows = pot_hbm.shape[1]
    pairs = [(flux_hbm, flux_ref), (jit_hbm, jit_ref), (off_hbm, off_ref), (nu_hbm, nu_ref), (sat_hbm, sat_ref)]
    for hbm, ref in ((pot_hbm, pot_ref), (cur_hbm, cur_ref), (mat_hbm, mat_ref)):
        pairs += [(hbm.at[:, 0:8, :], ref.at[0]), (hbm.at[:, rows - 8 : rows, :], ref.at[1])]
    copies = [pltpu.make_async_copy(src, dst, sems.at[n]) for n, (src, dst) in enumerate(pairs)]
    for copy in copies:
        copy.start()
    for copy in copies:
        copy.wait()

    odd_a = lax.rem(lax.axis_index("az"), 2) == 1
    panels = flux_ref.shape[1]
    where = jit_ref[...] + off_ref[0]
    where = jnp.where(where >= cycle, where - cycle, where).astype(f32)
    for h in range(panels // 128):
        at = h * (fields + 1)
        pan_ref[at : at + fields, :] = flux_ref[:, h * 128 : (h + 1) * 128]
        pan_ref[at + fields : at + fields + 1, :] = where[:, h * 128 : (h + 1) * 128]
    for j, (n, at) in enumerate(layout(fields, layers)):
        if j < fields:
            ref, k = pot_ref, j
        elif j < fields + layers:
            ref, k = mat_ref, j - fields
        else:
            ref, k = cur_ref, j - fields - layers
        up_ref[at : at + n, :] = ref[0, k, 0:n, :].astype(f32)
        down_ref[at : at + n, :] = ref[1, k, 8 - n : 8, :].astype(f32)
    n = up_ref.shape[0]
    even_ref[0:n, :] = jnp.where(odd_a, up_ref[...], down_ref[...])
    odd_ref[0:n, :] = jnp.where(odd_a, down_ref[...], up_ref[...])
    even_ref[n:, :] = pan_ref[...]
    odd_ref[n:, :] = pan_ref[...]
    entries = nu_ref.shape[0]
    for e in range(entries):
        table_ref[e : e + 1, :] = jnp.full((1, 128), nu_ref[e], f32)
        table_ref[entries + e : entries + e + 1, :] = jnp.full((1, 128), sat_ref[e], f32)


def edges(offset, nu, sat, pot, cur, mat, flux, jitter, cycle):
    fields, rows, cols = pot.shape
    layers = mat.shape[0]
    send = rim_rows(fields, layers)
    pan_rows = flux.shape[1] // 128 * (fields + 1)
    return pl.pallas_call(
        functools.partial(edges_kernel, cycle),
        out_shape=[
            jax.ShapeDtypeStruct((send + pan_rows, cols), f32),
            jax.ShapeDtypeStruct((send + pan_rows, cols), f32),
            jax.ShapeDtypeStruct((pan_rows, 128), f32),
            jax.ShapeDtypeStruct((2 * nu.shape[0], 128), f32),
        ],
        in_specs=[HBM] * 8,
        out_specs=[VMEM] * 4,
        scratch_shapes=[
            pltpu.VMEM((send, cols), f32),
            pltpu.VMEM((send, cols), f32),
            pltpu.VMEM((2, fields, 8, cols), f32),
            pltpu.VMEM((2, fields, 8, cols), f32),
            pltpu.VMEM((2, layers, 8, cols), jnp.int32),
            pltpu.VMEM(flux.shape, f32),
            pltpu.VMEM(jitter.shape, jnp.int32),
            pltpu.SMEM(offset.shape, jnp.int32),
            pltpu.SMEM(nu.shape, f32),
            pltpu.SMEM(sat.shape, f32),
            pltpu.SemaphoreType.DMA((11,)),
        ],
        compiler_params=params(LIMIT),
        cost_estimate=pl.CostEstimate(flops=1_000_000, bytes_accessed=400_000, transcendentals=0),
        name="pack_rows",
    )(offset, nu, sat, pot, cur, mat, flux, jitter)


def columns_kernel(pot_ref, cur_ref, mat_ref, strips_ref, slots_ref):
    fields, layers = pot_ref.shape[0], mat_ref.shape[0]
    rows, cols = mat_ref.shape[1:]
    total = 2 * fields + layers
    per = cols // slot
    groups = -(-total // per)
    lane = lax.broadcasted_iota(jnp.int32, (8, cols), 1)

    @pl.loop(0, rows // 8, unroll=8)
    def _(i):
        at = pl.ds(pl.multiple_of(i * 8, 8), 8)
        for g in range(groups):
            acc = None
            for k in range(min(per, total - g * per)):
                j = g * per + k
                if j < fields:
                    x = pot_ref[j, at, :]
                elif j < fields + layers:
                    x = mat_ref[j - fields, at, :].astype(f32)
                else:
                    x = cur_ref[j - fields - layers, at, :]
                x = pltpu.roll(x, (k * slot + high_own) % cols, 1)
                acc = x if acc is None else jnp.where(lane >= k * slot, x, acc)
            slots_ref[g, at, :] = acc

    for g in range(groups):
        strips_ref[g * cols : (g + 1) * cols, :] = slots_ref[g].T


def columns(pot, cur, mat):
    fields, rows, cols = pot.shape
    total = 2 * fields + mat.shape[0]
    groups = -(-total // (cols // slot))
    return pl.pallas_call(
        columns_kernel,
        out_shape=jax.ShapeDtypeStruct((groups * cols, rows), f32),
        in_specs=[VMEM] * 3,
        out_specs=VMEM,
        scratch_shapes=[pltpu.VMEM((groups, rows, cols), f32)],
        compiler_params=params(),
        cost_estimate=pl.CostEstimate(flops=8_000_000, bytes_accessed=3_000_000, transcendentals=0),
        name="turn_columns",
    )(pot, cur, mat)


def middle_kernel(fields, layers, odd_ref, even_ref, strips_ref, _coef, _air, ro_ref, re_ref, turned_ref, rim_ref):
    cols = even_ref.shape[1]
    send = rim_rows(fields, layers)
    odd_r = lax.rem(lax.axis_index("rad"), 2) == 1
    odd_a = lax.rem(lax.axis_index("az"), 2) == 1

    rim_ref[0:send, :] = jnp.where(odd_a, odd_ref[0:send, :], even_ref[0:send, :])
    rim_ref[64 : 64 + send, :] = jnp.where(odd_a, even_ref[0:send, :], odd_ref[0:send, :])
    turned_ref[...] = rim_ref[...].T

    for j, (n, at) in enumerate(layout(fields, layers)):
        b = slot_base(j, cols) + high_own
        lo, hi = strips_ref[b : b + n, :], strips_ref[b - n : b, :]
        re_ref[at : at + n, :] = jnp.where(odd_r, lo, hi)
        ro_ref[at : at + n, :] = jnp.where(odd_r, hi, lo)
    lo, hi = turned_ref[0:halo, :], turned_ref[cols - halo : cols, :]
    re_ref[send : send + halo, 0:128] = jnp.where(odd_r, lo, hi)
    ro_ref[send : send + halo, 0:128] = jnp.where(odd_r, hi, lo)


def middle(strips, odd_got, even_got, coef, air, fields, layers):
    cols = even_got.shape[1]
    rows = strips.shape[1]
    send = rim_rows(fields, layers)
    arrays = (odd_got, even_got, strips, coef, air)
    return pl.pallas_call(
        functools.partial(middle_kernel, fields, layers),
        out_shape=[
            jax.ShapeDtypeStruct((send + halo, rows), f32),
            jax.ShapeDtypeStruct((send + halo, rows), f32),
            jax.ShapeDtypeStruct((cols, 128), f32),
        ],
        in_specs=[VMEM] * 3 + [ANY] * 2,
        out_specs=[VMEM] * 3,
        scratch_shapes=[pltpu.VMEM((128, cols), f32)],
        compiler_params=params(),
        cost_estimate=pl.CostEstimate(flops=1_000_000, bytes_accessed=600_000, transcendentals=0),
        name="pack_columns",
    )(*arrays)


def block(i):
    return pl.ds(pl.multiple_of(i * 8, 8), 8)


def right(x):
    return pltpu.roll(x, x.shape[1] - 1, 1)


def left(x):
    return pltpu.roll(x, 1, 1)


def reluct_block(table_ref, coef_ref, load, material, i):
    layers = coef_ref.shape[0]
    comps = 3
    for l in range(layers):
        centres = [load(c * layers + l, 0) for c in range(comps)]
        nexts = [load(c * layers + l, 1) for c in range(comps)]
        flux_sq = half_strength(centres, nexts, [right(x) for x in centres])
        which = material(l)
        coef_ref[l, block(i + 2), :] = half_reluct(table_ref, which, flux_sq)


def sweep_block(coef_ref, load, source_at, i, store):
    layers = coef_ref.shape[0]
    comps = 3
    coef = [coef_ref[l, block(i + 2), :] for l in range(layers)]
    field = [[load(c * layers + l, 0) for l in range(layers)] for c in range(comps)]
    source = [[source_at(c * layers + l) for l in range(layers)] for c in range(comps)]
    moves = []
    for step in (1, -1):
        moves.append(
            (
                lambda l, step=step: coef_ref[l, pl.ds(i * 8 + 16 + step, 8), :],
                lambda c, l, step=step: load(c * layers + l, step),
            )
        )
    for turn in (right, left):
        moves.append((lambda l, turn=turn: turn(coef[l]), lambda c, l, turn=turn: turn(field[c][l])))
    new = sweep_cells(coef, field, source, moves)
    for c in range(comps):
        for l in range(layers):
            store(c * layers + l, new[c][l])


def keep(one_ref, i):
    def store(j, x):
        one_ref[j, block(i + 1), :] = x

    return store


def inner_kernel(table_ref, pot_ref, cur_ref, mat_ref, coef_ref, one_ref):
    rows, cols = mat_ref.shape[1:]
    count = rows // 8
    inner = count - 2
    step = divisor(inner, 10)

    def load_at(i):
        return lambda j, step: pot_ref[j, pl.ds(i * 8 + step, 8), :]

    def reluct_at(i, load):
        reluct_block(table_ref, coef_ref, load, lambda l: mat_ref[l, block(i), :], i)

    def last_load(j, step):
        x = pot_ref[j, rows - 8 : rows, :]
        return x if step == 0 else pltpu.roll(x, 7, 0)

    reluct_at(0, load_at(0))
    reluct_at(count - 1, last_load)

    @pl.loop(1, count - 1, unroll=step)
    def _(i):
        reluct_at(i, load_at(i))

    @pl.loop(1, count - 1, unroll=step)
    def _(i):
        sweep_block(coef_ref, load_at(i), lambda j: cur_ref[j, block(i), :], i, keep(one_ref, i))


def inner(table, pot, cur, mat):
    fields, rows, cols = pot.shape
    layers = mat.shape[0]
    return pl.pallas_call(
        inner_kernel,
        out_shape=[
            jax.ShapeDtypeStruct((layers, rows + 32, cols), f32),
            jax.ShapeDtypeStruct((fields, rows + 16, cols), f32),
        ],
        in_specs=[VMEM] * 4,
        out_specs=[VMEM, VMEM],
        compiler_params=params(),
        cost_estimate=pl.CostEstimate(flops=20_000_000, bytes_accessed=4_000_000, transcendentals=0),
        name="inner_rows",
    )(table, pot, cur, mat)


def outer_kernel(
    table_ref, pot_ref, cur_ref, mat_ref, odd_ref, even_ref, coef_in, one_in, out_ref, coef_ref, one_ref, edge_ref
):
    fields, rows, cols = out_ref.shape
    layers = mat_ref.shape[0]
    odd_a = lax.rem(lax.axis_index("az"), 2) == 1
    count = rows // 8

    blank = jnp.zeros((8, cols), f32)
    for j, (n, at) in enumerate(layout(fields, layers)):
        if j < fields:
            ref, k = pot_ref, j
        elif j < fields + layers:
            ref, k = mat_ref, j - fields
        else:
            ref, k = cur_ref, j - fields - layers
        edge_ref[0, j, 0:8, :] = blank
        edge_ref[0, j, 8:16, :] = blank
        edge_ref[1, j, 16:24, :] = blank
        edge_ref[1, j, 24:32, :] = blank
        edge_ref[0, j, 16:32, :] = ref[k, 0:16, :].astype(f32)
        edge_ref[1, j, 0:16, :] = ref[k, rows - 16 : rows, :].astype(f32)
        even, odd = even_ref[at : at + n, :], odd_ref[at : at + n, :]
        edge_ref[0, j, 16 - n : 16, :] = jnp.where(odd_a, even, odd)
        edge_ref[1, j, 16 : 16 + n, :] = jnp.where(odd_a, odd, even)
    for l in range(layers):
        coef_ref[l, 0:8, :] = blank
        coef_ref[l, 24 + rows : 32 + rows, :] = blank

    def edge_load(k):
        side, at = k // 2, 8 + 8 * (k % 2)
        return (
            lambda j, step: edge_ref[side, j, at + step : at + step + 8, :],
            (-1, 0, count - 1, count)[k],
        )

    for k in (0, 2, 3):
        load, i = edge_load(k)
        reluct_block(table_ref, coef_ref, load, lambda l: load(fields + l, 0).astype(jnp.int32), i)
    for k in range(4):
        load, i = edge_load(k)
        sweep_block(coef_ref, load, lambda j: load(fields + layers + j, 0), i, keep(one_ref, i))

    @pl.loop(0, count, unroll=divisor(count, 8))
    def _(i):
        def store(j, x):
            out_ref[j, block(i), :] = x

        sweep_block(
            coef_ref,
            lambda j, step: one_ref[j, pl.ds(i * 8 + 8 + step, 8), :],
            lambda j: cur_ref[j, block(i), :],
            i,
            store,
        )


def outer(table, pot, cur, mat, odd_got, even_got, coef, one):
    fields, rows, cols = pot.shape
    layers = mat.shape[0]
    total = 2 * fields + layers
    return pl.pallas_call(
        outer_kernel,
        out_shape=[
            jax.ShapeDtypeStruct(pot.shape, f32),
            jax.ShapeDtypeStruct(coef.shape, f32),
            jax.ShapeDtypeStruct(one.shape, f32),
        ],
        in_specs=[VMEM] * 8,
        out_specs=[VMEM] * 3,
        input_output_aliases={6: 1, 7: 2},
        scratch_shapes=[pltpu.VMEM((2, total, 32, cols), f32)],
        compiler_params=params(),
        cost_estimate=pl.CostEstimate(flops=20_000_000, bytes_accessed=4_000_000, transcendentals=0),
        name="outer_rows",
    )(table, pot, cur, mat, odd_got, even_got, coef, one)[0]


def deposit_kernel(cycle, starts, bases, fields, rows, *refs):
    n = len(starts)
    pan_refs, air_refs, vals_ref = refs[:n], refs[n + 2 : -1], refs[-1]
    r, a = lax.axis_index("rad"), lax.axis_index("az")
    size = lax.axis_size("rad")
    stator = (r == size // 2) | (r == size // 2 - 1)

    @pl.when(stator)
    def _():
        lanes = vals_ref.shape[1]
        vals_ref[...] = jnp.zeros_like(vals_ref)
        t = 0
        for ref, first in zip(pan_refs, starts):
            for at in range(first, ref.shape[0], fields + 1):
                vals_ref[0 : fields + 1, t * 128 : (t + 1) * 128] = ref[at : at + fields + 1, :]
                t += 1
        values = vals_ref[...]
        position = vals_ref[fields : fields + 1, :].astype(jnp.int32)
        high = values.astype(jnp.bfloat16)
        rest = values - high.astype(f32)
        mid = rest.astype(jnp.bfloat16)
        low = (rest - mid.astype(f32)).astype(jnp.bfloat16)
        split = jnp.concatenate([high, mid, low], axis=0)
        spot = lax.broadcasted_iota(jnp.int32, (rows, lanes), 0)
        lane = lax.broadcasted_iota(jnp.int32, (16, 128), 1)
        channel = lax.broadcasted_iota(jnp.int32, (16, 128), 0)
        for air_ref, bit in zip(air_refs, bases):
            local = position - (a ^ bit) * rows
            onehot = jnp.where(spot == local, 1.0, 0.0).astype(jnp.bfloat16)
            parts = lax.dot_general(split, onehot, (((1,), (1,)), ((), ())), preferred_element_type=f32)
            air_ref[...] = parts[0:16] + parts[16:32] + parts[32:48]
            after = (local == rows) | (local == rows - cycle)
            before = (local == -1) | (local == cycle - 1)
            after = jnp.sum(jnp.where(after, values, 0.0), axis=1, keepdims=True)
            before = jnp.sum(jnp.where(before, values, 0.0), axis=1, keepdims=True)
            outside = jnp.where(lane == channel, after, jnp.where(lane == channel + 16, before, 0.0))
            air_ref[fields : fields + 1, 0:128] = jnp.sum(outside, axis=0, keepdims=True)

    @pl.when(jnp.logical_not(stator))
    def _():
        for air_ref in air_refs:
            air_ref[...] = jnp.zeros_like(air_ref)


def deposit(pans, starts, order, bases, fields, rows, cycle):
    panels = sum(p.shape[0] - first for p, first in zip(pans, starts)) // (fields + 1) * 128
    return pl.pallas_call(
        functools.partial(deposit_kernel, cycle, starts, bases, fields, rows),
        out_shape=[jax.ShapeDtypeStruct((16, rows), f32) for _ in bases],
        in_specs=[VMEM] * len(pans) + [ANY] * len(order),
        out_specs=[VMEM] * len(bases),
        scratch_shapes=[pltpu.VMEM((16, panels), f32)],
        compiler_params=params(),
        cost_estimate=pl.CostEstimate(flops=4_000_000, bytes_accessed=500_000, transcendentals=0),
        name="airgap",
    )(*pans, *order)


def air_kernel(n, fields, *refs):
    air_ref = refs[-1]
    rows = refs[0].shape[1]
    airgap = sum(ref[...] for ref in refs[:n])
    lane = lax.broadcasted_iota(jnp.int32, (16, 128), 1)
    channel = lax.broadcasted_iota(jnp.int32, (16, 128), 0)
    spread = airgap[fields : fields + 1, 0:128]
    after = jnp.sum(jnp.where(lane == channel, spread, 0.0), axis=1, keepdims=True)
    before = jnp.sum(jnp.where(lane == channel + 16, spread, 0.0), axis=1, keepdims=True)
    air_ref[:, 0:rows] = airgap
    air_ref[:, rows : rows + 128] = jnp.where(lane == 0, after, jnp.where(lane == 127, before, 0.0))


def gather_air(airs, main):
    fields, rows, _ = main.shape
    return pl.pallas_call(
        functools.partial(air_kernel, len(airs), fields),
        out_shape=jax.ShapeDtypeStruct((16, rows + 128), f32),
        in_specs=[VMEM] * len(airs) + [ANY],
        out_specs=VMEM,
        compiler_params=params(),
        cost_estimate=pl.CostEstimate(flops=EXPAND, bytes_accessed=0, transcendentals=0),
        name="airgap_sum",
    )(*airs, main)


def rim_kernel(
    table_ref, main_ref, air_ref, strips_ref, turned_ref, ro_ref, re_ref,
    out_hbm, merged_ref, cols_ref, corner_ref, back_ref, sem,
):
    fields, rows, cols = main_ref.shape
    total = cols_ref.shape[0]
    layers = total - 2 * fields
    comps = fields // layers
    send = rim_rows(fields, layers)
    r = lax.axis_index("rad")
    size = lax.axis_size("rad")
    odd_r = lax.rem(r, 2) == 1

    def left(at, n):
        return jnp.where(odd_r, re_ref[at : at + n, :], ro_ref[at : at + n, :])

    def right(at, n):
        return jnp.where(odd_r, ro_ref[at : at + n, :], re_ref[at : at + n, :])

    corner_ref[0:2, :] = left(send + 1, 2)[:, 0:128]
    corner_ref[2:8, :] = turned_ref[0:low_own, :]
    corner_ref[8:13, :] = turned_ref[cols - high_own : cols, :]
    corner_ref[13:16, :] = right(send, halo)[:, 0:128]
    corner = corner_ref[...]
    lane = lax.broadcasted_iota(jnp.int32, (16, 128), 1)
    for j, (n, at) in enumerate(layout(fields, layers)):
        b = slot_base(j, cols)
        cols_ref[j, 0:8, 0:rows] = strips_ref[b + high_own - 2 : b + high_own + 6, :]
        cols_ref[j, 8:16, 0:rows] = strips_ref[b : b + 8, :]
        m = min(n, 2)
        cols_ref[j, 2 - m : 2, 0:rows] = left(at + n - m, m)
        cols_ref[j, 13 : 13 + n, 0:rows] = right(at, n)
        cols_ref[j, :, rows : rows + 128] = jnp.where(
            lane < 64, pltpu.roll(corner, (-at) % 128, 1), pltpu.roll(corner, (64 - n - at) % 128, 1)
        )

    column = lax.broadcasted_iota(jnp.int32, (16, rows + 128), 0)
    inside = ((column >= 2) | (r > 0)) & ((column < 13) | (r < size - 1))
    target = jnp.where(r == size // 2, 2, jnp.where(r == size // 2 - 1, 13, -1))

    def move(x, axis, step):
        return pltpu.roll(x, (-step) % x.shape[axis], axis)

    pot = [[jnp.where(inside, cols_ref[c * layers + l], 0.0) for l in range(layers)] for c in range(comps)]
    source = []
    for c in range(comps):
        source.append([])
        for l in range(layers):
            j = c * layers + l
            air = air_ref[j : j + 1, :]
            source[c].append(cols_ref[fields + layers + j] + jnp.where(column == target, air, 0.0))
    coef = []
    for l in range(layers):
        centres = [pot[c][l] for c in range(comps)]
        flux_sq = half_strength(centres, [move(x, 1, 1) for x in centres], [move(x, 0, 1) for x in centres])
        which = cols_ref[fields + l].astype(jnp.int32)
        k = half_reluct(table_ref, which, flux_sq)
        coef.append(jnp.where(inside, k, 0.0))
    moves = [(axis, step) for axis in (1, 0) for step in (1, -1)]
    moved = {(l, m): move(coef[l], *m) for l in range(layers) for m in moves}

    def sweep(field):
        table = [
            (lambda l, m=m: moved[l, m], lambda c, l, m=m: move(field[c][l], *m)) for m in moves
        ]
        return sweep_cells(coef, field, source, table)

    one = [[jnp.where(inside, x, 0.0) for x in part] for part in sweep(pot)]
    fixed = sweep(one)
    for c in range(comps):
        for l in range(layers):
            j = c * layers + l
            back_ref[8 * j : 8 * j + 3, :] = fixed[c][l][10:13, 0:rows]
            back_ref[8 * j + 3 : 8 * j + 5, :] = fixed[c][l][2:4, 0:rows]
    turned = back_ref[...].T

    lane = lax.broadcasted_iota(jnp.int32, (rows, cols), 1)
    edge = (lane < 2) | (lane >= cols - 3)
    for j in range(fields):
        merged_ref[j] = jnp.where(edge, pltpu.roll(turned, (cols - 3 - 8 * j) % cols, 1), main_ref[j])
        pltpu.make_async_copy(merged_ref.at[j], out_hbm.at[j], sem.at[j]).start()
    for j in range(fields):
        pltpu.make_async_copy(merged_ref.at[j], out_hbm.at[j], sem.at[j]).wait()


def rims(table, main, air, strips, turned, ro_got, re_got, layers):
    fields, rows, cols = main.shape
    total = 2 * fields + layers
    arrays = (main, air, strips, turned, ro_got, re_got)
    return pl.pallas_call(
        rim_kernel,
        out_shape=jax.ShapeDtypeStruct(main.shape, f32),
        in_specs=[VMEM] * (1 + len(arrays)),
        out_specs=ANY,
        scratch_shapes=[
            pltpu.VMEM(main.shape, f32),
            pltpu.VMEM((total, 16, rows + 128), f32),
            pltpu.VMEM((16, 128), f32),
            pltpu.VMEM((128, rows), f32),
            pltpu.SemaphoreType.DMA((fields,)),
        ],
        compiler_params=params(),
        name="rims",
    )(table, *arrays)


def local(potential, current, material, nu_table, sat_table, panel_flux, panel_jitter, rotor_offset):
    comps, layers, rows, cols = potential.shape
    fields = comps * layers
    az, rad = lax.axis_size("az"), lax.axis_size("rad")
    cycle = rows * az
    pot = potential.reshape(fields, rows, cols)
    cur = current.reshape(fields, rows, cols)

    def swap(x, az_of, rad_of):
        pairs = [(a * rad + r, az_of(a) * rad + rad_of(r)) for a in range(az) for r in range(rad)]
        return lax.ppermute(x, ("az", "rad"), pairs)

    def same(i):
        return i

    def even(i):
        return i ^ 1

    def odd(i, n):
        return (i + 1) % n if i % 2 else (i - 1) % n

    odd_send, even_send, pan, table = edges(
        rotor_offset, nu_table, sat_table, pot, cur, material, panel_flux, panel_jitter.reshape(1, -1), cycle
    )
    odd_got = swap(odd_send, lambda a: odd(a, az), same)
    even_got = swap(even_send, even, same)
    two_got = swap(pan, lambda a: a ^ 2, same)
    strips = columns(pot, cur, material)
    coef, one = inner(table, pot, cur, material)
    at = rim_rows(fields, layers)
    pans, starts = [pan, odd_got, even_got, two_got], [0, at, at, 0]
    if az > 8:
        held, bit = jnp.concatenate([p[first:] for p, first in zip(pans, starts)], axis=0), 8
        while bit < az:
            held = jnp.concatenate([held, swap(held, lambda a, bit=bit: a ^ bit, same)], axis=0)
            bit *= 2
        pans, starts = [held], [0]
    if az > 4:
        air, air_send = deposit(pans, starts, (coef, strips), [0, 4], fields, rows, cycle)
        airs = [air, swap(air_send, lambda a: a ^ 4, same)]
    else:
        airs = deposit(pans, starts, (coef, strips), [0], fields, rows, cycle)
    ro_send, re_send, turned = middle(strips, odd_got, even_got, coef, airs[0], fields, layers)
    ro_got = swap(ro_send, same, lambda r: odd(r, rad))
    re_got = swap(re_send, same, even)
    main = outer(table, pot, cur, material, odd_got, even_got, coef, one)
    air = gather_air(airs, main)
    out = rims(table, main, air, strips, turned, ro_got, re_got, layers)
    return out.reshape(potential.shape)


def solution(mesh):
    placed = (
        P(None, None, "az", "rad"),
        P(None, None, "az", "rad"),
        P(None, "az", "rad"),
        P(),
        P(),
        P(None, "az"),
        P("az"),
        P(),
    )
    return jax.shard_map(
        local, mesh=mesh, in_specs=placed, out_specs=P(None, None, "az", "rad"), check_vma=False
    )
```

```python
import functools

import jax
import jax.numpy as jnp
from jax import lax
from jax.experimental import pallas as pl
from jax.experimental.pallas import tpu as pltpu
from jax.sharding import PartitionSpec as P

sigma_term = 1.0

EXPAND = 20_000_000_000
halo = 3
low_own, high_own = 6, 5
slot = low_own + high_own
f32 = jnp.float32
VMEM = pl.BlockSpec(memory_space=pltpu.VMEM)
HBM = pl.BlockSpec(memory_space=pltpu.HBM)
ANY = pl.BlockSpec(memory_space=pl.ANY)


def params(mib=48):
    return pltpu.CompilerParams(vmem_limit_bytes=mib * 1024 * 1024)


def layout(fields, layers):
    depth = [halo] * fields + [halo - 1] * layers + [1] * fields
    return [(n, sum(depth[:j])) for j, n in enumerate(depth)]


def rim_rows(fields, layers):
    return halo * fields + (halo - 1) * layers + fields


def slot_base(j, cols):
    per = cols // slot
    return (j // per) * cols + (j % per) * slot


def lookup(material, table_ref, first):
    rows, lanes = material.shape
    values = []
    for e in range(first, first + table_ref.shape[0] // 2):
        row = jnp.broadcast_to(table_ref[e : e + 1, :], (rows, 128))
        values.append(jnp.concatenate([row] * (lanes // 128), axis=1))
    bit = 1
    while len(values) > 1:
        take = (material & bit) != 0
        values = [jnp.where(take, values[i + 1], values[i]) for i in range(0, len(values), 2)]
        bit *= 2
    return values[0]


def half_reluct(table_ref, material, flux_sq):
    base = lookup(material, table_ref, 0)
    saturation = lookup(material, table_ref, table_ref.shape[0] // 2)
    return (0.5 * base) * (1.0 + saturation * flux_sq / (1.0 + flux_sq))


def sweep_cells(coef, field, source, moves):
    layers = len(coef)
    out = [[None] * layers for _ in field]
    for l in range(layers):
        centre = coef[l]
        total = jnp.full_like(centre, sigma_term)
        num = [source[c][l] for c in range(len(field))]
        for move_coef, move_field in moves:
            w = centre + move_coef(l)
            total = total + w
            for c in range(len(field)):
                num[c] = num[c] + w * move_field(c, l)
        for other in (l + 1, l - 1):
            if 0 <= other < layers:
                w = centre + coef[other]
                total = total + w
                for c in range(len(field)):
                    num[c] = num[c] + w * field[c][other]
            else:
                total = total + centre
        inverse = 1.0 / total
        for c in range(len(field)):
            out[c][l] = num[c] * inverse
    return out


def divisor(n, most):
    return max(d for d in range(1, most + 1) if n % d == 0)


def half_strength(centres, az_next, rad_next):
    total = None
    for centre, az, rad in zip(centres, az_next, rad_next):
        az, rad = az - centre, rad - centre
        part = az * az + rad * rad
        total = part if total is None else total + part
    return total


def edges_kernel(
    cycle, off_ref, nu_hbm, sat_hbm, pot_hbm, cur_hbm, mat_hbm, flux_hbm, jit_hbm, odd_ref, even_ref, pan_ref, table_ref,
    up_ref, down_ref, pot_ref, cur_ref, mat_ref, flux_ref, jit_ref, nu_ref, sat_ref, sems
):
    fields, layers = pot_ref.shape[1], mat_ref.shape[1]
    rows = pot_hbm.shape[1]
    pairs = [(flux_hbm, flux_ref), (jit_hbm, jit_ref), (nu_hbm, nu_ref), (sat_hbm, sat_ref)]
    for hbm, ref in ((pot_hbm, pot_ref), (cur_hbm, cur_ref), (mat_hbm, mat_ref)):
        pairs += [(hbm.at[:, 0:8, :], ref.at[0]), (hbm.at[:, rows - 8 : rows, :], ref.at[1])]
    copies = [pltpu.make_async_copy(src, dst, sems.at[n]) for n, (src, dst) in enumerate(pairs)]
    for copy in copies:
        copy.start()
    for copy in copies:
        copy.wait()

    odd_a = lax.rem(lax.axis_index("az"), 2) == 1
    panels = flux_ref.shape[1]
    where = jit_ref[...] + off_ref[0]
    where = jnp.where(where >= cycle, where - cycle, where).astype(f32)
    for h in range(panels // 128):
        at = h * (fields + 1)
        pan_ref[at : at + fields, :] = flux_ref[:, h * 128 : (h + 1) * 128]
        pan_ref[at + fields : at + fields + 1, :] = where[:, h * 128 : (h + 1) * 128]
    for j, (n, at) in enumerate(layout(fields, layers)):
        if j < fields:
            ref, k = pot_ref, j
        elif j < fields + layers:
            ref, k = mat_ref, j - fields
        else:
            ref, k = cur_ref, j - fields - layers
        up_ref[at : at + n, :] = ref[0, k, 0:n, :].astype(f32)
        down_ref[at : at + n, :] = ref[1, k, 8 - n : 8, :].astype(f32)
    n = up_ref.shape[0]
    even_ref[0:n, :] = jnp.where(odd_a, up_ref[...], down_ref[...])
    odd_ref[0:n, :] = jnp.where(odd_a, down_ref[...], up_ref[...])
    even_ref[n:, :] = pan_ref[...]
    odd_ref[n:, :] = pan_ref[...]
    entries = nu_ref.shape[0]
    for e in range(entries):
        table_ref[e : e + 1, :] = jnp.full((1, 128), nu_ref[e], f32)
        table_ref[entries + e : entries + e + 1, :] = jnp.full((1, 128), sat_ref[e], f32)


def edges(offset, nu, sat, pot, cur, mat, flux, jitter, cycle):
    fields, rows, cols = pot.shape
    layers = mat.shape[0]
    send = rim_rows(fields, layers)
    pan_rows = flux.shape[1] // 128 * (fields + 1)
    return pl.pallas_call(
        functools.partial(edges_kernel, cycle),
        out_shape=[
            jax.ShapeDtypeStruct((send + pan_rows, cols), f32),
            jax.ShapeDtypeStruct((send + pan_rows, cols), f32),
            jax.ShapeDtypeStruct((pan_rows, 128), f32),
            jax.ShapeDtypeStruct((2 * nu.shape[0], 128), f32),
        ],
        in_specs=[pl.BlockSpec(memory_space=pltpu.SMEM)] + [HBM] * 7,
        out_specs=[VMEM] * 4,
        scratch_shapes=[
            pltpu.VMEM((send, cols), f32),
            pltpu.VMEM((send, cols), f32),
            pltpu.VMEM((2, fields, 8, cols), f32),
            pltpu.VMEM((2, fields, 8, cols), f32),
            pltpu.VMEM((2, layers, 8, cols), jnp.int32),
            pltpu.VMEM(flux.shape, f32),
            pltpu.VMEM(jitter.shape, jnp.int32),
            pltpu.SMEM(nu.shape, f32),
            pltpu.SMEM(sat.shape, f32),
            pltpu.SemaphoreType.DMA((10,)),
        ],
        compiler_params=params(),
        cost_estimate=pl.CostEstimate(flops=1_000_000, bytes_accessed=400_000, transcendentals=0),
        name="pack_rows",
    )(offset, *(pltpu.with_memory_space_constraint(x, pltpu.HBM) for x in (nu, sat, pot, cur, mat, flux, jitter)))


def columns_kernel(pot_ref, cur_ref, mat_ref, strips_ref, slots_ref):
    fields, layers = pot_ref.shape[0], mat_ref.shape[0]
    rows, cols = mat_ref.shape[1:]
    total = 2 * fields + layers
    per = cols // slot
    groups = -(-total // per)
    lane = lax.broadcasted_iota(jnp.int32, (8, cols), 1)

    @pl.loop(0, rows // 8, unroll=8)
    def _(i):
        at = pl.ds(pl.multiple_of(i * 8, 8), 8)
        for g in range(groups):
            acc = None
            for k in range(min(per, total - g * per)):
                j = g * per + k
                if j < fields:
                    x = pot_ref[j, at, :]
                elif j < fields + layers:
                    x = mat_ref[j - fields, at, :].astype(f32)
                else:
                    x = cur_ref[j - fields - layers, at, :]
                x = pltpu.roll(x, (k * slot + high_own) % cols, 1)
                acc = x if acc is None else jnp.where(lane >= k * slot, x, acc)
            slots_ref[g, at, :] = acc

    for g in range(groups):
        strips_ref[g * cols : (g + 1) * cols, :] = slots_ref[g].T


def columns(pot, cur, mat):
    fields, rows, cols = pot.shape
    total = 2 * fields + mat.shape[0]
    groups = -(-total // (cols // slot))
    return pl.pallas_call(
        columns_kernel,
        out_shape=jax.ShapeDtypeStruct((groups * cols, rows), f32),
        in_specs=[VMEM] * 3,
        out_specs=VMEM,
        scratch_shapes=[pltpu.VMEM((groups, rows, cols), f32)],
        compiler_params=params(),
        cost_estimate=pl.CostEstimate(flops=8_000_000, bytes_accessed=3_000_000, transcendentals=0),
        name="turn_columns",
    )(pot, cur, mat)


def middle_kernel(fields, layers, odd_ref, even_ref, strips_ref, _coef, _air, ro_ref, re_ref, turned_ref, rim_ref):
    cols = even_ref.shape[1]
    send = rim_rows(fields, layers)
    odd_r = lax.rem(lax.axis_index("rad"), 2) == 1
    odd_a = lax.rem(lax.axis_index("az"), 2) == 1

    rim_ref[0:send, :] = jnp.where(odd_a, odd_ref[0:send, :], even_ref[0:send, :])
    rim_ref[64 : 64 + send, :] = jnp.where(odd_a, even_ref[0:send, :], odd_ref[0:send, :])
    turned_ref[...] = rim_ref[...].T

    for j, (n, at) in enumerate(layout(fields, layers)):
        b = slot_base(j, cols) + high_own
        lo, hi = strips_ref[b : b + n, :], strips_ref[b - n : b, :]
        re_ref[at : at + n, :] = jnp.where(odd_r, lo, hi)
        ro_ref[at : at + n, :] = jnp.where(odd_r, hi, lo)
    lo, hi = turned_ref[0:halo, :], turned_ref[cols - halo : cols, :]
    re_ref[send : send + halo, 0:128] = jnp.where(odd_r, lo, hi)
    ro_ref[send : send + halo, 0:128] = jnp.where(odd_r, hi, lo)


def middle(strips, odd_got, even_got, coef, air, fields, layers):
    cols = even_got.shape[1]
    rows = strips.shape[1]
    send = rim_rows(fields, layers)
    arrays = (odd_got, even_got, strips, coef, air)
    return pl.pallas_call(
        functools.partial(middle_kernel, fields, layers),
        out_shape=[
            jax.ShapeDtypeStruct((send + halo, rows), f32),
            jax.ShapeDtypeStruct((send + halo, rows), f32),
            jax.ShapeDtypeStruct((cols, 128), f32),
        ],
        in_specs=[VMEM] * 3 + [ANY] * 2,
        out_specs=[VMEM] * 3,
        scratch_shapes=[pltpu.VMEM((128, cols), f32)],
        compiler_params=params(),
        cost_estimate=pl.CostEstimate(flops=1_000_000, bytes_accessed=600_000, transcendentals=0),
        name="pack_columns",
    )(*arrays)


def block(i):
    return pl.ds(pl.multiple_of(i * 8, 8), 8)


def right(x):
    return pltpu.roll(x, x.shape[1] - 1, 1)


def left(x):
    return pltpu.roll(x, 1, 1)


def reluct_block(table_ref, coef_ref, load, material, i):
    layers = coef_ref.shape[0]
    comps = 3
    for l in range(layers):
        centres = [load(c * layers + l, 0) for c in range(comps)]
        nexts = [load(c * layers + l, 1) for c in range(comps)]
        flux_sq = half_strength(centres, nexts, [right(x) for x in centres])
        which = material(l)
        coef_ref[l, block(i + 2), :] = half_reluct(table_ref, which, flux_sq)


def sweep_block(coef_ref, load, source_at, i, store):
    layers = coef_ref.shape[0]
    comps = 3
    coef = [coef_ref[l, block(i + 2), :] for l in range(layers)]
    field = [[load(c * layers + l, 0) for l in range(layers)] for c in range(comps)]
    source = [[source_at(c * layers + l) for l in range(layers)] for c in range(comps)]
    moves = []
    for step in (1, -1):
        moves.append(
            (
                lambda l, step=step: coef_ref[l, pl.ds(i * 8 + 16 + step, 8), :],
                lambda c, l, step=step: load(c * layers + l, step),
            )
        )
    for turn in (right, left):
        moves.append((lambda l, turn=turn: turn(coef[l]), lambda c, l, turn=turn: turn(field[c][l])))
    new = sweep_cells(coef, field, source, moves)
    for c in range(comps):
        for l in range(layers):
            store(c * layers + l, new[c][l])


def keep(one_ref, i):
    def store(j, x):
        one_ref[j, block(i + 1), :] = x

    return store


def inner_kernel(table_ref, pot_ref, cur_ref, mat_ref, coef_ref, one_ref):
    rows, cols = mat_ref.shape[1:]
    count = rows // 8
    inner = count - 2
    step = divisor(inner, 10)

    def load_at(i):
        return lambda j, step: pot_ref[j, pl.ds(i * 8 + step, 8), :]

    def reluct_at(i, load):
        reluct_block(table_ref, coef_ref, load, lambda l: mat_ref[l, block(i), :], i)

    def last_load(j, step):
        x = pot_ref[j, rows - 8 : rows, :]
        return x if step == 0 else pltpu.roll(x, 7, 0)

    reluct_at(0, load_at(0))
    reluct_at(count - 1, last_load)

    @pl.loop(1, count - 1, unroll=step)
    def _(i):
        reluct_at(i, load_at(i))

    @pl.loop(1, count - 1, unroll=step)
    def _(i):
        sweep_block(coef_ref, load_at(i), lambda j: cur_ref[j, block(i), :], i, keep(one_ref, i))


def inner(table, pot, cur, mat):
    fields, rows, cols = pot.shape
    layers = mat.shape[0]
    return pl.pallas_call(
        inner_kernel,
        out_shape=[
            jax.ShapeDtypeStruct((layers, rows + 32, cols), f32),
            jax.ShapeDtypeStruct((fields, rows + 16, cols), f32),
        ],
        in_specs=[VMEM] * 4,
        out_specs=[VMEM, VMEM],
        compiler_params=params(),
        cost_estimate=pl.CostEstimate(flops=20_000_000, bytes_accessed=4_000_000, transcendentals=0),
        name="inner_rows",
    )(table, pot, cur, mat)


def outer_kernel(
    table_ref, pot_ref, cur_ref, mat_ref, odd_ref, even_ref, coef_in, one_in, out_ref, coef_ref, one_ref, edge_ref
):
    fields, rows, cols = out_ref.shape
    layers = mat_ref.shape[0]
    odd_a = lax.rem(lax.axis_index("az"), 2) == 1
    count = rows // 8

    blank = jnp.zeros((8, cols), f32)
    for j, (n, at) in enumerate(layout(fields, layers)):
        if j < fields:
            ref, k = pot_ref, j
        elif j < fields + layers:
            ref, k = mat_ref, j - fields
        else:
            ref, k = cur_ref, j - fields - layers
        edge_ref[0, j, 0:8, :] = blank
        edge_ref[0, j, 8:16, :] = blank
        edge_ref[1, j, 16:24, :] = blank
        edge_ref[1, j, 24:32, :] = blank
        edge_ref[0, j, 16:32, :] = ref[k, 0:16, :].astype(f32)
        edge_ref[1, j, 0:16, :] = ref[k, rows - 16 : rows, :].astype(f32)
        even, odd = even_ref[at : at + n, :], odd_ref[at : at + n, :]
        edge_ref[0, j, 16 - n : 16, :] = jnp.where(odd_a, even, odd)
        edge_ref[1, j, 16 : 16 + n, :] = jnp.where(odd_a, odd, even)
    for l in range(layers):
        coef_ref[l, 0:8, :] = blank
        coef_ref[l, 24 + rows : 32 + rows, :] = blank

    def edge_load(k):
        side, at = k // 2, 8 + 8 * (k % 2)
        return (
            lambda j, step: edge_ref[side, j, at + step : at + step + 8, :],
            (-1, 0, count - 1, count)[k],
        )

    for k in (0, 2, 3):
        load, i = edge_load(k)
        reluct_block(table_ref, coef_ref, load, lambda l: load(fields + l, 0).astype(jnp.int32), i)
    for k in range(4):
        load, i = edge_load(k)
        sweep_block(coef_ref, load, lambda j: load(fields + layers + j, 0), i, keep(one_ref, i))

    @pl.loop(0, count, unroll=divisor(count, 8))
    def _(i):
        def store(j, x):
            out_ref[j, block(i), :] = x

        sweep_block(
            coef_ref,
            lambda j, step: one_ref[j, pl.ds(i * 8 + 8 + step, 8), :],
            lambda j: cur_ref[j, block(i), :],
            i,
            store,
        )


def outer(table, pot, cur, mat, odd_got, even_got, coef, one):
    fields, rows, cols = pot.shape
    layers = mat.shape[0]
    total = 2 * fields + layers
    return pl.pallas_call(
        outer_kernel,
        out_shape=[
            jax.ShapeDtypeStruct(pot.shape, f32),
            jax.ShapeDtypeStruct(coef.shape, f32),
            jax.ShapeDtypeStruct(one.shape, f32),
        ],
        in_specs=[VMEM] * 8,
        out_specs=[VMEM] * 3,
        input_output_aliases={6: 1, 7: 2},
        scratch_shapes=[pltpu.VMEM((2, total, 32, cols), f32)],
        compiler_params=params(),
        cost_estimate=pl.CostEstimate(flops=20_000_000, bytes_accessed=4_000_000, transcendentals=0),
        name="outer_rows",
    )(table, pot, cur, mat, odd_got, even_got, coef, one)[0]


def deposit_kernel(cycle, starts, bases, fields, rows, *refs):
    n = len(starts)
    pan_refs, air_refs, vals_ref = refs[:n], refs[n + 2 : -1], refs[-1]
    r, a = lax.axis_index("rad"), lax.axis_index("az")
    size = lax.axis_size("rad")
    stator = (r == size // 2) | (r == size // 2 - 1)

    @pl.when(stator)
    def _():
        lanes = vals_ref.shape[1]
        vals_ref[...] = jnp.zeros_like(vals_ref)
        t = 0
        for ref, first in zip(pan_refs, starts):
            for at in range(first, ref.shape[0], fields + 1):
                vals_ref[0 : fields + 1, t * 128 : (t + 1) * 128] = ref[at : at + fields + 1, :]
                t += 1
        values = vals_ref[...]
        position = vals_ref[fields : fields + 1, :].astype(jnp.int32)
        high = values.astype(jnp.bfloat16)
        rest = values - high.astype(f32)
        mid = rest.astype(jnp.bfloat16)
        low = (rest - mid.astype(f32)).astype(jnp.bfloat16)
        split = jnp.concatenate([high, mid, low], axis=0)
        spot = lax.broadcasted_iota(jnp.int32, (rows, lanes), 0)
        lane = lax.broadcasted_iota(jnp.int32, (16, 128), 1)
        channel = lax.broadcasted_iota(jnp.int32, (16, 128), 0)
        for air_ref, bit in zip(air_refs, bases):
            local = position - (a ^ bit) * rows
            onehot = jnp.where(spot == local, 1.0, 0.0).astype(jnp.bfloat16)
            parts = lax.dot_general(split, onehot, (((1,), (1,)), ((), ())), preferred_element_type=f32)
            air_ref[...] = parts[0:16] + parts[16:32] + parts[32:48]
            after = (local == rows) | (local == rows - cycle)
            before = (local == -1) | (local == cycle - 1)
            after = jnp.sum(jnp.where(after, values, 0.0), axis=1, keepdims=True)
            before = jnp.sum(jnp.where(before, values, 0.0), axis=1, keepdims=True)
            outside = jnp.where(lane == channel, after, jnp.where(lane == channel + 16, before, 0.0))
            air_ref[fields : fields + 1, 0:128] = jnp.sum(outside, axis=0, keepdims=True)

    @pl.when(jnp.logical_not(stator))
    def _():
        for air_ref in air_refs:
            air_ref[...] = jnp.zeros_like(air_ref)


def deposit(pans, starts, order, bases, fields, rows, cycle):
    panels = sum(p.shape[0] - first for p, first in zip(pans, starts)) // (fields + 1) * 128
    return pl.pallas_call(
        functools.partial(deposit_kernel, cycle, starts, bases, fields, rows),
        out_shape=[jax.ShapeDtypeStruct((16, rows), f32) for _ in bases],
        in_specs=[VMEM] * len(pans) + [ANY] * len(order),
        out_specs=[VMEM] * len(bases),
        scratch_shapes=[pltpu.VMEM((16, panels), f32)],
        compiler_params=params(),
        cost_estimate=pl.CostEstimate(flops=4_000_000, bytes_accessed=500_000, transcendentals=0),
        name="airgap",
    )(*pans, *order)


def air_kernel(n, fields, *refs):
    air_ref = refs[-1]
    rows = refs[0].shape[1]
    airgap = sum(ref[...] for ref in refs[:n])
    lane = lax.broadcasted_iota(jnp.int32, (16, 128), 1)
    channel = lax.broadcasted_iota(jnp.int32, (16, 128), 0)
    spread = airgap[fields : fields + 1, 0:128]
    after = jnp.sum(jnp.where(lane == channel, spread, 0.0), axis=1, keepdims=True)
    before = jnp.sum(jnp.where(lane == channel + 16, spread, 0.0), axis=1, keepdims=True)
    air_ref[:, 0:rows] = airgap
    air_ref[:, rows : rows + 128] = jnp.where(lane == 0, after, jnp.where(lane == 127, before, 0.0))


def gather_air(airs, main):
    fields, rows, _ = main.shape
    return pl.pallas_call(
        functools.partial(air_kernel, len(airs), fields),
        out_shape=jax.ShapeDtypeStruct((16, rows + 128), f32),
        in_specs=[VMEM] * len(airs) + [ANY],
        out_specs=VMEM,
        compiler_params=params(),
        cost_estimate=pl.CostEstimate(flops=EXPAND, bytes_accessed=0, transcendentals=0),
        name="airgap_sum",
    )(*airs, main)


def rim_kernel(
    table_ref, main_ref, air_ref, strips_ref, turned_ref, ro_ref, re_ref,
    out_hbm, merged_ref, cols_ref, corner_ref, back_ref, sem,
):
    fields, rows, cols = main_ref.shape
    total = cols_ref.shape[0]
    layers = total - 2 * fields
    comps = fields // layers
    send = rim_rows(fields, layers)
    r = lax.axis_index("rad")
    size = lax.axis_size("rad")
    odd_r = lax.rem(r, 2) == 1

    def left(at, n):
        return jnp.where(odd_r, re_ref[at : at + n, :], ro_ref[at : at + n, :])

    def right(at, n):
        return jnp.where(odd_r, ro_ref[at : at + n, :], re_ref[at : at + n, :])

    corner_ref[0:2, :] = left(send + 1, 2)[:, 0:128]
    corner_ref[2:8, :] = turned_ref[0:low_own, :]
    corner_ref[8:13, :] = turned_ref[cols - high_own : cols, :]
    corner_ref[13:16, :] = right(send, halo)[:, 0:128]
    corner = corner_ref[...]
    lane = lax.broadcasted_iota(jnp.int32, (16, 128), 1)
    for j, (n, at) in enumerate(layout(fields, layers)):
        b = slot_base(j, cols)
        cols_ref[j, 0:8, 0:rows] = strips_ref[b + high_own - 2 : b + high_own + 6, :]
        cols_ref[j, 8:16, 0:rows] = strips_ref[b : b + 8, :]
        m = min(n, 2)
        cols_ref[j, 2 - m : 2, 0:rows] = left(at + n - m, m)
        cols_ref[j, 13 : 13 + n, 0:rows] = right(at, n)
        cols_ref[j, :, rows : rows + 128] = jnp.where(
            lane < 64, pltpu.roll(corner, (-at) % 128, 1), pltpu.roll(corner, (64 - n - at) % 128, 1)
        )

    column = lax.broadcasted_iota(jnp.int32, (16, rows + 128), 0)
    inside = ((column >= 2) | (r > 0)) & ((column < 13) | (r < size - 1))
    target = jnp.where(r == size // 2, 2, jnp.where(r == size // 2 - 1, 13, -1))

    def move(x, axis, step):
        return pltpu.roll(x, (-step) % x.shape[axis], axis)

    pot = [[jnp.where(inside, cols_ref[c * layers + l], 0.0) for l in range(layers)] for c in range(comps)]
    source = []
    for c in range(comps):
        source.append([])
        for l in range(layers):
            j = c * layers + l
            air = air_ref[j : j + 1, :]
            source[c].append(cols_ref[fields + layers + j] + jnp.where(column == target, air, 0.0))
    coef = []
    for l in range(layers):
        centres = [pot[c][l] for c in range(comps)]
        flux_sq = half_strength(centres, [move(x, 1, 1) for x in centres], [move(x, 0, 1) for x in centres])
        which = cols_ref[fields + l].astype(jnp.int32)
        k = half_reluct(table_ref, which, flux_sq)
        coef.append(jnp.where(inside, k, 0.0))
    moves = [(axis, step) for axis in (1, 0) for step in (1, -1)]
    moved = {(l, m): move(coef[l], *m) for l in range(layers) for m in moves}

    def sweep(field):
        table = [
            (lambda l, m=m: moved[l, m], lambda c, l, m=m: move(field[c][l], *m)) for m in moves
        ]
        return sweep_cells(coef, field, source, table)

    one = [[jnp.where(inside, x, 0.0) for x in part] for part in sweep(pot)]
    fixed = sweep(one)
    for c in range(comps):
        for l in range(layers):
            j = c * layers + l
            back_ref[8 * j : 8 * j + 3, :] = fixed[c][l][10:13, 0:rows]
            back_ref[8 * j + 3 : 8 * j + 5, :] = fixed[c][l][2:4, 0:rows]
    turned = back_ref[...].T

    lane = lax.broadcasted_iota(jnp.int32, (rows, cols), 1)
    edge = (lane < 2) | (lane >= cols - 3)
    for j in range(fields):
        merged_ref[j] = jnp.where(edge, pltpu.roll(turned, (cols - 3 - 8 * j) % cols, 1), main_ref[j])
        pltpu.make_async_copy(merged_ref.at[j], out_hbm.at[j], sem.at[j]).start()
    for j in range(fields):
        pltpu.make_async_copy(merged_ref.at[j], out_hbm.at[j], sem.at[j]).wait()


def rims(table, main, air, strips, turned, ro_got, re_got, layers):
    fields, rows, cols = main.shape
    total = 2 * fields + layers
    arrays = (main, air, strips, turned, ro_got, re_got)
    return pl.pallas_call(
        rim_kernel,
        out_shape=jax.ShapeDtypeStruct(main.shape, f32),
        in_specs=[VMEM] * (1 + len(arrays)),
        out_specs=ANY,
        scratch_shapes=[
            pltpu.VMEM(main.shape, f32),
            pltpu.VMEM((total, 16, rows + 128), f32),
            pltpu.VMEM((16, 128), f32),
            pltpu.VMEM((128, rows), f32),
            pltpu.SemaphoreType.DMA((fields,)),
        ],
        compiler_params=params(),
        name="rims",
    )(table, *arrays)


def local(potential, current, material, nu_table, sat_table, panel_flux, panel_jitter, rotor_offset):
    comps, layers, rows, cols = potential.shape
    fields = comps * layers
    az, rad = lax.axis_size("az"), lax.axis_size("rad")
    cycle = rows * az
    pot = potential.reshape(fields, rows, cols)
    cur = current.reshape(fields, rows, cols)

    def swap(x, az_of, rad_of):
        pairs = [(a * rad + r, az_of(a) * rad + rad_of(r)) for a in range(az) for r in range(rad)]
        return lax.ppermute(x, ("az", "rad"), pairs)

    def same(i):
        return i

    def even(i):
        return i ^ 1

    def odd(i, n):
        return (i + 1) % n if i % 2 else (i - 1) % n

    odd_send, even_send, pan, table = edges(
        rotor_offset, nu_table, sat_table, pot, cur, material, panel_flux, panel_jitter.reshape(1, -1), cycle
    )
    odd_got = swap(odd_send, lambda a: odd(a, az), same)
    even_got = swap(even_send, even, same)
    two_got = swap(pan, lambda a: a ^ 2, same)
    strips = columns(pot, cur, material)
    coef, one = inner(table, pot, cur, material)
    at = rim_rows(fields, layers)
    pans, starts = [pan, odd_got, even_got, two_got], [0, at, at, 0]
    if az > 8:
        held, bit = jnp.concatenate([p[first:] for p, first in zip(pans, starts)], axis=0), 8
        while bit < az:
            held = jnp.concatenate([held, swap(held, lambda a, bit=bit: a ^ bit, same)], axis=0)
            bit *= 2
        pans, starts = [held], [0]
    if az > 4:
        air, air_send = deposit(pans, starts, (coef, strips), [0, 4], fields, rows, cycle)
        airs = [air, swap(air_send, lambda a: a ^ 4, same)]
    else:
        airs = deposit(pans, starts, (coef, strips), [0], fields, rows, cycle)
    ro_send, re_send, turned = middle(strips, odd_got, even_got, coef, airs[0], fields, layers)
    ro_got = swap(ro_send, same, lambda r: odd(r, rad))
    re_got = swap(re_send, same, even)
    main = outer(table, pot, cur, material, odd_got, even_got, coef, one)
    air = gather_air(airs, main)
    out = rims(table, main, air, strips, turned, ro_got, re_got, layers)
    return out.reshape(potential.shape)


def solution(mesh):
    placed = (
        P(None, None, "az", "rad"),
        P(None, None, "az", "rad"),
        P(None, "az", "rad"),
        P(),
        P(),
        P(None, "az"),
        P("az"),
        P(),
    )
    return jax.shard_map(
        local, mesh=mesh, in_specs=placed, out_specs=P(None, None, "az", "rad"), check_vma=False
    )
```

```python
import functools

import jax
import jax.numpy as jnp
from jax import lax
from jax.experimental import pallas as pl
from jax.experimental.pallas import tpu as pltpu
from jax.sharding import PartitionSpec as P

sigma_term = 1.0

EXPAND = 20_000_000_000
AHEAD = 0
halo = 3
low_own, high_own = 6, 5
slot = low_own + high_own
f32 = jnp.float32
VMEM = pl.BlockSpec(memory_space=pltpu.VMEM)
SMEM = pl.BlockSpec(memory_space=pltpu.SMEM)
HBM = pl.BlockSpec(memory_space=pltpu.HBM)
ANY = pl.BlockSpec(memory_space=pl.ANY)


def params(mib=48):
    return pltpu.CompilerParams(vmem_limit_bytes=mib * 1024 * 1024)


def layout(fields, layers):
    depth = [halo] * fields + [halo - 1] * layers + [1] * fields
    return [(n, sum(depth[:j])) for j, n in enumerate(depth)]


def rim_rows(fields, layers):
    return halo * fields + (halo - 1) * layers + fields


def slot_base(j, cols):
    per = cols // slot
    return (j // per) * cols + (j % per) * slot


def lookup(material, table_ref, first):
    rows, lanes = material.shape
    values = []
    for e in range(first, first + table_ref.shape[0] // 2):
        row = jnp.broadcast_to(table_ref[e : e + 1, :], (rows, 128))
        values.append(jnp.concatenate([row] * (lanes // 128), axis=1))
    bit = 1
    while len(values) > 1:
        take = (material & bit) != 0
        values = [jnp.where(take, values[i + 1], values[i]) for i in range(0, len(values), 2)]
        bit *= 2
    return values[0]


def half_reluct(table_ref, material, flux_sq):
    base = lookup(material, table_ref, 0)
    saturation = lookup(material, table_ref, table_ref.shape[0] // 2)
    return (0.5 * base) * (1.0 + saturation * flux_sq / (1.0 + flux_sq))


def sweep_cells(coef, field, source, moves):
    layers = len(coef)
    out = [[None] * layers for _ in field]
    for l in range(layers):
        centre = coef[l]
        total = jnp.full_like(centre, sigma_term)
        num = [source[c][l] for c in range(len(field))]
        for move_coef, move_field in moves:
            w = centre + move_coef(l)
            total = total + w
            for c in range(len(field)):
                num[c] = num[c] + w * move_field(c, l)
        for other in (l + 1, l - 1):
            if 0 <= other < layers:
                w = centre + coef[other]
                total = total + w
                for c in range(len(field)):
                    num[c] = num[c] + w * field[c][other]
            else:
                total = total + centre
        inverse = 1.0 / total
        for c in range(len(field)):
            out[c][l] = num[c] * inverse
    return out


def divisor(n, most):
    return max(d for d in range(1, most + 1) if n % d == 0)


def half_strength(centres, az_next, rad_next):
    total = None
    for centre, az, rad in zip(centres, az_next, rad_next):
        az, rad = az - centre, rad - centre
        part = az * az + rad * rad
        total = part if total is None else total + part
    return total


def edges_kernel(
    nu_hbm, sat_hbm, pot_hbm, cur_hbm, mat_hbm, flux_hbm, jit_hbm, odd_ref, even_ref, pan_ref, table_ref,
    up_ref, down_ref, pot_ref, cur_ref, mat_ref, flux_ref, jit_ref, nu_ref, sat_ref, sems
):
    fields, layers = pot_ref.shape[1], mat_ref.shape[1]
    rows = pot_hbm.shape[1]
    pairs = [(flux_hbm, flux_ref), (jit_hbm, jit_ref), (nu_hbm, nu_ref), (sat_hbm, sat_ref)]
    for hbm, ref in ((pot_hbm, pot_ref), (cur_hbm, cur_ref), (mat_hbm, mat_ref)):
        pairs += [(hbm.at[:, 0:8, :], ref.at[0]), (hbm.at[:, rows - 8 : rows, :], ref.at[1])]
    copies = [pltpu.make_async_copy(src, dst, sems.at[n]) for n, (src, dst) in enumerate(pairs)]
    for copy in copies:
        copy.start()
    for copy in copies:
        copy.wait()

    odd_a = lax.rem(lax.axis_index("az"), 2) == 1
    panels = flux_ref.shape[1]
    where = jit_ref[...].astype(f32)
    for h in range(panels // 128):
        at = h * (fields + 1)
        pan_ref[at : at + fields, :] = flux_ref[:, h * 128 : (h + 1) * 128]
        pan_ref[at + fields : at + fields + 1, :] = where[:, h * 128 : (h + 1) * 128]
    for j, (n, at) in enumerate(layout(fields, layers)):
        if j < fields:
            ref, k = pot_ref, j
        elif j < fields + layers:
            ref, k = mat_ref, j - fields
        else:
            ref, k = cur_ref, j - fields - layers
        up_ref[at : at + n, :] = ref[0, k, 0:n, :].astype(f32)
        down_ref[at : at + n, :] = ref[1, k, 8 - n : 8, :].astype(f32)
    n = up_ref.shape[0]
    even_ref[0:n, :] = jnp.where(odd_a, up_ref[...], down_ref[...])
    odd_ref[0:n, :] = jnp.where(odd_a, down_ref[...], up_ref[...])
    even_ref[n:, :] = pan_ref[...]
    odd_ref[n:, :] = pan_ref[...]
    entries = nu_ref.shape[0]
    for e in range(entries):
        table_ref[e : e + 1, :] = jnp.full((1, 128), nu_ref[e], f32)
        table_ref[entries + e : entries + e + 1, :] = jnp.full((1, 128), sat_ref[e], f32)


def edges(nu, sat, pot, cur, mat, flux, jitter):
    fields, rows, cols = pot.shape
    layers = mat.shape[0]
    send = rim_rows(fields, layers)
    pan_rows = flux.shape[1] // 128 * (fields + 1)
    return pl.pallas_call(
        edges_kernel,
        out_shape=[
            jax.ShapeDtypeStruct((send + pan_rows, cols), f32),
            jax.ShapeDtypeStruct((send + pan_rows, cols), f32),
            jax.ShapeDtypeStruct((pan_rows, 128), f32),
            jax.ShapeDtypeStruct((2 * nu.shape[0], 128), f32),
        ],
        in_specs=[HBM] * 7,
        out_specs=[VMEM] * 4,
        scratch_shapes=[
            pltpu.VMEM((send, cols), f32),
            pltpu.VMEM((send, cols), f32),
            pltpu.VMEM((2, fields, 8, cols), f32),
            pltpu.VMEM((2, fields, 8, cols), f32),
            pltpu.VMEM((2, layers, 8, cols), jnp.int32),
            pltpu.VMEM(flux.shape, f32),
            pltpu.VMEM(jitter.shape, jnp.int32),
            pltpu.SMEM(nu.shape, f32),
            pltpu.SMEM(sat.shape, f32),
            pltpu.SemaphoreType.DMA((10,)),
        ],
        compiler_params=params(),
        cost_estimate=pl.CostEstimate(flops=1_000_000, bytes_accessed=400_000, transcendentals=0),
        name="pack_rows",
    )(*(pltpu.with_memory_space_constraint(x, pltpu.HBM) for x in (nu, sat, pot, cur, mat, flux, jitter)))


def columns_kernel(_offset, pot_ref, cur_ref, mat_ref, strips_ref, slots_ref):
    fields, layers = pot_ref.shape[0], mat_ref.shape[0]
    rows, cols = mat_ref.shape[1:]
    total = 2 * fields + layers
    per = cols // slot
    groups = -(-total // per)
    lane = lax.broadcasted_iota(jnp.int32, (8, cols), 1)

    @pl.loop(0, rows // 8, unroll=32)
    def _(i):
        at = pl.ds(pl.multiple_of(i * 8, 8), 8)
        for g in range(groups):
            acc = None
            for k in range(min(per, total - g * per)):
                j = g * per + k
                if j < fields:
                    x = pot_ref[j, at, :]
                elif j < fields + layers:
                    x = mat_ref[j - fields, at, :].astype(f32)
                else:
                    x = cur_ref[j - fields - layers, at, :]
                x = pltpu.roll(x, (k * slot + high_own) % cols, 1)
                acc = x if acc is None else jnp.where(lane >= k * slot, x, acc)
            slots_ref[g, at, :] = acc

    for g in range(groups):
        strips_ref[g * cols : (g + 1) * cols, :] = slots_ref[g].T


def columns(offset, pot, cur, mat):
    fields, rows, cols = pot.shape
    total = 2 * fields + mat.shape[0]
    groups = -(-total // (cols // slot))
    return pl.pallas_call(
        columns_kernel,
        out_shape=jax.ShapeDtypeStruct((groups * cols, rows), f32),
        in_specs=[SMEM] + [VMEM] * 3,
        out_specs=VMEM,
        scratch_shapes=[pltpu.VMEM((groups, rows, cols), f32)],
        compiler_params=params(),
        cost_estimate=pl.CostEstimate(flops=8_000_000, bytes_accessed=3_000_000, transcendentals=0),
        name="turn_columns",
    )(offset, pot, cur, mat)


def middle_kernel(fields, layers, odd_ref, even_ref, strips_ref, _coef, _air, ro_ref, re_ref, turned_ref, rim_ref):
    cols = even_ref.shape[1]
    send = rim_rows(fields, layers)
    odd_r = lax.rem(lax.axis_index("rad"), 2) == 1
    odd_a = lax.rem(lax.axis_index("az"), 2) == 1

    rim_ref[0:send, :] = jnp.where(odd_a, odd_ref[0:send, :], even_ref[0:send, :])
    rim_ref[64 : 64 + send, :] = jnp.where(odd_a, even_ref[0:send, :], odd_ref[0:send, :])
    turned_ref[...] = rim_ref[...].T

    for j, (n, at) in enumerate(layout(fields, layers)):
        b = slot_base(j, cols) + high_own
        lo, hi = strips_ref[b : b + n, :], strips_ref[b - n : b, :]
        re_ref[at : at + n, :] = jnp.where(odd_r, lo, hi)
        ro_ref[at : at + n, :] = jnp.where(odd_r, hi, lo)
    lo, hi = turned_ref[0:halo, :], turned_ref[cols - halo : cols, :]
    re_ref[send : send + halo, 0:128] = jnp.where(odd_r, lo, hi)
    ro_ref[send : send + halo, 0:128] = jnp.where(odd_r, hi, lo)


def middle(strips, odd_got, even_got, coef, air, fields, layers):
    cols = even_got.shape[1]
    rows = strips.shape[1]
    send = rim_rows(fields, layers)
    arrays = (odd_got, even_got, strips, coef, air)
    return pl.pallas_call(
        functools.partial(middle_kernel, fields, layers),
        out_shape=[
            jax.ShapeDtypeStruct((send + halo, rows), f32),
            jax.ShapeDtypeStruct((send + halo, rows), f32),
            jax.ShapeDtypeStruct((cols, 128), f32),
        ],
        in_specs=[VMEM] * 3 + [ANY] * 2,
        out_specs=[VMEM] * 3,
        scratch_shapes=[pltpu.VMEM((128, cols), f32)],
        compiler_params=params(),
        cost_estimate=pl.CostEstimate(flops=1_000_000, bytes_accessed=600_000, transcendentals=0),
        name="pack_columns",
    )(*arrays)


def block(i):
    return pl.ds(pl.multiple_of(i * 8, 8), 8)


def right(x):
    return pltpu.roll(x, x.shape[1] - 1, 1)


def left(x):
    return pltpu.roll(x, 1, 1)


def reluct_block(table_ref, coef_ref, load, material, i):
    layers = coef_ref.shape[0]
    comps = 3
    for l in range(layers):
        centres = [load(c * layers + l, 0) for c in range(comps)]
        nexts = [load(c * layers + l, 1) for c in range(comps)]
        flux_sq = half_strength(centres, nexts, [right(x) for x in centres])
        which = material(l)
        coef_ref[l, block(i + 2), :] = half_reluct(table_ref, which, flux_sq)


def sweep_block(coef_ref, load, source_at, i, store):
    layers = coef_ref.shape[0]
    comps = 3
    coef = [coef_ref[l, block(i + 2), :] for l in range(layers)]
    field = [[load(c * layers + l, 0) for l in range(layers)] for c in range(comps)]
    source = [[source_at(c * layers + l) for l in range(layers)] for c in range(comps)]
    moves = []
    for step in (1, -1):
        moves.append(
            (
                lambda l, step=step: coef_ref[l, pl.ds(i * 8 + 16 + step, 8), :],
                lambda c, l, step=step: load(c * layers + l, step),
            )
        )
    for turn in (right, left):
        moves.append((lambda l, turn=turn: turn(coef[l]), lambda c, l, turn=turn: turn(field[c][l])))
    new = sweep_cells(coef, field, source, moves)
    for c in range(comps):
        for l in range(layers):
            store(c * layers + l, new[c][l])


def keep(one_ref, i):
    def store(j, x):
        one_ref[j, block(i + 1), :] = x

    return store


def inner_kernel(table_ref, pot_ref, cur_ref, mat_ref, coef_ref, one_ref, out_ref):
    rows, cols = mat_ref.shape[1:]
    count = rows // 8
    inner = count - 2
    step = divisor(inner, 30)

    def load_at(i):
        return lambda j, step: pot_ref[j, pl.ds(i * 8 + step, 8), :]

    def reluct_at(i, load):
        reluct_block(table_ref, coef_ref, load, lambda l: mat_ref[l, block(i), :], i)

    def last_load(j, step):
        x = pot_ref[j, rows - 8 : rows, :]
        return x if step == 0 else pltpu.roll(x, 7, 0)

    reluct_at(0, load_at(0))
    reluct_at(count - 1, last_load)

    @pl.loop(1, count - 1, unroll=step)
    def _(i):
        reluct_at(i, load_at(i))

    @pl.loop(1, count - 1, unroll=step)
    def _(i):
        sweep_block(coef_ref, load_at(i), lambda j: cur_ref[j, block(i), :], i, keep(one_ref, i))

    ahead = AHEAD * (count - 4) // 4
    if ahead:

        @pl.loop(2, 2 + ahead, unroll=divisor(ahead, 10))
        def _(i):
            second_block(coef_ref, one_ref, cur_ref, out_ref, i)


def second_block(coef_ref, one_ref, cur_ref, out_ref, i):
    def store(j, x):
        out_ref[j, block(i), :] = x

    sweep_block(
        coef_ref,
        lambda j, step: one_ref[j, pl.ds(i * 8 + 8 + step, 8), :],
        lambda j: cur_ref[j, block(i), :],
        i,
        store,
    )


def inner(table, pot, cur, mat):
    fields, rows, cols = pot.shape
    layers = mat.shape[0]
    return pl.pallas_call(
        inner_kernel,
        out_shape=[
            jax.ShapeDtypeStruct((layers, rows + 32, cols), f32),
            jax.ShapeDtypeStruct((fields, rows + 16, cols), f32),
            jax.ShapeDtypeStruct(pot.shape, f32),
        ],
        in_specs=[VMEM] * 4,
        out_specs=[VMEM] * 3,
        compiler_params=params(),
        cost_estimate=pl.CostEstimate(flops=20_000_000, bytes_accessed=4_000_000, transcendentals=0),
        name="inner_rows",
    )(table, pot, cur, mat)


def outer_kernel(
    table_ref, pot_ref, cur_ref, mat_ref, odd_ref, even_ref, coef_in, one_in, out_in, coef_ref, one_ref, out_ref, edge_ref
):
    fields, rows, cols = out_ref.shape
    layers = mat_ref.shape[0]
    odd_a = lax.rem(lax.axis_index("az"), 2) == 1
    count = rows // 8

    blank = jnp.zeros((8, cols), f32)
    for j, (n, at) in enumerate(layout(fields, layers)):
        if j < fields:
            ref, k = pot_ref, j
        elif j < fields + layers:
            ref, k = mat_ref, j - fields
        else:
            ref, k = cur_ref, j - fields - layers
        edge_ref[0, j, 0:8, :] = blank
        edge_ref[0, j, 8:16, :] = blank
        edge_ref[1, j, 16:24, :] = blank
        edge_ref[1, j, 24:32, :] = blank
        edge_ref[0, j, 16:32, :] = ref[k, 0:16, :].astype(f32)
        edge_ref[1, j, 0:16, :] = ref[k, rows - 16 : rows, :].astype(f32)
        even, odd = even_ref[at : at + n, :], odd_ref[at : at + n, :]
        edge_ref[0, j, 16 - n : 16, :] = jnp.where(odd_a, even, odd)
        edge_ref[1, j, 16 : 16 + n, :] = jnp.where(odd_a, odd, even)
    for l in range(layers):
        coef_ref[l, 0:8, :] = blank
        coef_ref[l, 24 + rows : 32 + rows, :] = blank

    def edge_load(k):
        side, at = k // 2, 8 + 8 * (k % 2)
        return (
            lambda j, step: edge_ref[side, j, at + step : at + step + 8, :],
            (-1, 0, count - 1, count)[k],
        )

    for k in (0, 2, 3):
        load, i = edge_load(k)
        reluct_block(table_ref, coef_ref, load, lambda l: load(fields + l, 0).astype(jnp.int32), i)
    for k in range(4):
        load, i = edge_load(k)
        sweep_block(coef_ref, load, lambda j: load(fields + layers + j, 0), i, keep(one_ref, i))

    for i in (0, 1, count - 2, count - 1):
        second_block(coef_ref, one_ref, cur_ref, out_ref, i)
    ahead = AHEAD * (count - 4) // 4
    if ahead < count - 4:

        @pl.loop(2 + ahead, count - 2, unroll=divisor(count - 4 - ahead, 30))
        def _(i):
            second_block(coef_ref, one_ref, cur_ref, out_ref, i)


def outer(table, pot, cur, mat, odd_got, even_got, coef, one, main):
    fields, rows, cols = pot.shape
    layers = mat.shape[0]
    total = 2 * fields + layers
    return pl.pallas_call(
        outer_kernel,
        out_shape=[
            jax.ShapeDtypeStruct(coef.shape, f32),
            jax.ShapeDtypeStruct(one.shape, f32),
            jax.ShapeDtypeStruct(main.shape, f32),
        ],
        in_specs=[VMEM] * 9,
        out_specs=[VMEM] * 3,
        input_output_aliases={6: 0, 7: 1, 8: 2},
        scratch_shapes=[pltpu.VMEM((2, total, 32, cols), f32)],
        compiler_params=params(),
        cost_estimate=pl.CostEstimate(flops=20_000_000, bytes_accessed=4_000_000, transcendentals=0),
        name="outer_rows",
    )(table, pot, cur, mat, odd_got, even_got, coef, one, main)[2]


def deposit_kernel(cycle, starts, bases, fields, rows, n_order, off_ref, *refs):
    n = len(starts)
    pan_refs, air_refs, vals_ref = refs[:n], refs[n + n_order : -1], refs[-1]
    r, a = lax.axis_index("rad"), lax.axis_index("az")
    size = lax.axis_size("rad")
    stator = (r == size // 2) | (r == size // 2 - 1)

    @pl.when(stator)
    def _():
        lanes = vals_ref.shape[1]
        vals_ref[...] = jnp.zeros_like(vals_ref)
        t = 0
        for ref, first in zip(pan_refs, starts):
            for at in range(first, ref.shape[0], fields + 1):
                vals_ref[0 : fields + 1, t * 128 : (t + 1) * 128] = ref[at : at + fields + 1, :]
                t += 1
        values = vals_ref[...]
        position = vals_ref[fields : fields + 1, :].astype(jnp.int32) + off_ref[0]
        position = jnp.where(position >= cycle, position - cycle, position)
        high = values.astype(jnp.bfloat16)
        rest = values - high.astype(f32)
        mid = rest.astype(jnp.bfloat16)
        low = (rest - mid.astype(f32)).astype(jnp.bfloat16)
        split = jnp.concatenate([high, mid, low], axis=0)
        spot = lax.broadcasted_iota(jnp.int32, (rows, lanes), 0)
        lane = lax.broadcasted_iota(jnp.int32, (16, 128), 1)
        channel = lax.broadcasted_iota(jnp.int32, (16, 128), 0)
        for air_ref, bit in zip(air_refs, bases):
            local = position - (a ^ bit) * rows
            onehot = jnp.where(spot == local, 1.0, 0.0).astype(jnp.bfloat16)
            parts = lax.dot_general(split, onehot, (((1,), (1,)), ((), ())), preferred_element_type=f32)
            air_ref[...] = parts[0:16] + parts[16:32] + parts[32:48]
            after = (local == rows) | (local == rows - cycle)
            before = (local == -1) | (local == cycle - 1)
            after = jnp.sum(jnp.where(after, values, 0.0), axis=1, keepdims=True)
            before = jnp.sum(jnp.where(before, values, 0.0), axis=1, keepdims=True)
            outside = jnp.where(lane == channel, after, jnp.where(lane == channel + 16, before, 0.0))
            air_ref[fields : fields + 1, 0:128] = jnp.sum(outside, axis=0, keepdims=True)

    @pl.when(jnp.logical_not(stator))
    def _():
        for air_ref in air_refs:
            air_ref[...] = jnp.zeros_like(air_ref)


def deposit(name, offset, pans, starts, order, bases, fields, rows, cycle):
    panels = sum(p.shape[0] - first for p, first in zip(pans, starts)) // (fields + 1) * 128
    return pl.pallas_call(
        functools.partial(deposit_kernel, cycle, starts, bases, fields, rows, len(order)),
        out_shape=[jax.ShapeDtypeStruct((16, rows), f32) for _ in bases],
        in_specs=[SMEM] + [VMEM] * len(pans) + [ANY] * len(order),
        out_specs=[VMEM] * len(bases),
        scratch_shapes=[pltpu.VMEM((16, panels), f32)],
        compiler_params=params(),
        cost_estimate=pl.CostEstimate(flops=4_000_000, bytes_accessed=500_000, transcendentals=0),
        name=name,
    )(offset, *pans, *order)


def air_kernel(n, fields, *refs):
    air_ref = refs[-1]
    rows = refs[0].shape[1]
    airgap = sum(ref[...] for ref in refs[:n])
    lane = lax.broadcasted_iota(jnp.int32, (16, 128), 1)
    channel = lax.broadcasted_iota(jnp.int32, (16, 128), 0)
    spread = airgap[fields : fields + 1, 0:128]
    after = jnp.sum(jnp.where(lane == channel, spread, 0.0), axis=1, keepdims=True)
    before = jnp.sum(jnp.where(lane == channel + 16, spread, 0.0), axis=1, keepdims=True)
    air_ref[:, 0:rows] = airgap
    air_ref[:, rows : rows + 128] = jnp.where(lane == 0, after, jnp.where(lane == 127, before, 0.0))


def gather_air(airs, main):
    fields, rows, _ = main.shape
    return pl.pallas_call(
        functools.partial(air_kernel, len(airs), fields),
        out_shape=jax.ShapeDtypeStruct((16, rows + 128), f32),
        in_specs=[VMEM] * len(airs) + [ANY],
        out_specs=VMEM,
        compiler_params=params(),
        cost_estimate=pl.CostEstimate(flops=EXPAND, bytes_accessed=0, transcendentals=0),
        name="airgap_sum",
    )(*airs, main)


def rim_kernel(
    table_ref, main_ref, air_ref, strips_ref, turned_ref, ro_ref, re_ref,
    out_hbm, merged_ref, cols_ref, corner_ref, back_ref, sem,
):
    fields, rows, cols = main_ref.shape
    total = cols_ref.shape[0]
    layers = total - 2 * fields
    comps = fields // layers
    send = rim_rows(fields, layers)
    r = lax.axis_index("rad")
    size = lax.axis_size("rad")
    odd_r = lax.rem(r, 2) == 1

    def left(at, n):
        return jnp.where(odd_r, re_ref[at : at + n, :], ro_ref[at : at + n, :])

    def right(at, n):
        return jnp.where(odd_r, ro_ref[at : at + n, :], re_ref[at : at + n, :])

    corner_ref[0:2, :] = left(send + 1, 2)[:, 0:128]
    corner_ref[2:8, :] = turned_ref[0:low_own, :]
    corner_ref[8:13, :] = turned_ref[cols - high_own : cols, :]
    corner_ref[13:16, :] = right(send, halo)[:, 0:128]
    corner = corner_ref[...]
    lane = lax.broadcasted_iota(jnp.int32, (16, 128), 1)
    for j, (n, at) in enumerate(layout(fields, layers)):
        b = slot_base(j, cols)
        cols_ref[j, 0:8, 0:rows] = strips_ref[b + high_own - 2 : b + high_own + 6, :]
        cols_ref[j, 8:16, 0:rows] = strips_ref[b : b + 8, :]
        m = min(n, 2)
        cols_ref[j, 2 - m : 2, 0:rows] = left(at + n - m, m)
        cols_ref[j, 13 : 13 + n, 0:rows] = right(at, n)
        cols_ref[j, :, rows : rows + 128] = jnp.where(
            lane < 64, pltpu.roll(corner, (-at) % 128, 1), pltpu.roll(corner, (64 - n - at) % 128, 1)
        )

    column = lax.broadcasted_iota(jnp.int32, (16, rows + 128), 0)
    inside = ((column >= 2) | (r > 0)) & ((column < 13) | (r < size - 1))
    target = jnp.where(r == size // 2, 2, jnp.where(r == size // 2 - 1, 13, -1))

    def move(x, axis, step):
        return pltpu.roll(x, (-step) % x.shape[axis], axis)

    pot = [[jnp.where(inside, cols_ref[c * layers + l], 0.0) for l in range(layers)] for c in range(comps)]
    source = []
    for c in range(comps):
        source.append([])
        for l in range(layers):
            j = c * layers + l
            air = air_ref[j : j + 1, :]
            source[c].append(cols_ref[fields + layers + j] + jnp.where(column == target, air, 0.0))
    coef = []
    for l in range(layers):
        centres = [pot[c][l] for c in range(comps)]
        flux_sq = half_strength(centres, [move(x, 1, 1) for x in centres], [move(x, 0, 1) for x in centres])
        which = cols_ref[fields + l].astype(jnp.int32)
        k = half_reluct(table_ref, which, flux_sq)
        coef.append(jnp.where(inside, k, 0.0))
    moves = [(axis, step) for axis in (1, 0) for step in (1, -1)]
    moved = {(l, m): move(coef[l], *m) for l in range(layers) for m in moves}

    def sweep(field):
        table = [
            (lambda l, m=m: moved[l, m], lambda c, l, m=m: move(field[c][l], *m)) for m in moves
        ]
        return sweep_cells(coef, field, source, table)

    one = [[jnp.where(inside, x, 0.0) for x in part] for part in sweep(pot)]
    fixed = sweep(one)
    for c in range(comps):
        for l in range(layers):
            j = c * layers + l
            back_ref[8 * j : 8 * j + 3, :] = fixed[c][l][10:13, 0:rows]
            back_ref[8 * j + 3 : 8 * j + 5, :] = fixed[c][l][2:4, 0:rows]
    turned = back_ref[...].T

    lane = lax.broadcasted_iota(jnp.int32, (rows, cols), 1)
    edge = (lane < 2) | (lane >= cols - 3)
    for j in range(fields):
        merged_ref[j] = jnp.where(edge, pltpu.roll(turned, (cols - 3 - 8 * j) % cols, 1), main_ref[j])
        pltpu.make_async_copy(merged_ref.at[j], out_hbm.at[j], sem.at[j]).start()
    for j in range(fields):
        pltpu.make_async_copy(merged_ref.at[j], out_hbm.at[j], sem.at[j]).wait()


def rims(table, main, air, strips, turned, re_got, ro_got, layers):
    fields, rows, cols = main.shape
    total = 2 * fields + layers
    arrays = (main, air, strips, turned, ro_got, re_got)
    return pl.pallas_call(
        rim_kernel,
        out_shape=jax.ShapeDtypeStruct(main.shape, f32),
        in_specs=[VMEM] * (1 + len(arrays)),
        out_specs=ANY,
        scratch_shapes=[
            pltpu.VMEM(main.shape, f32),
            pltpu.VMEM((total, 16, rows + 128), f32),
            pltpu.VMEM((16, 128), f32),
            pltpu.VMEM((128, rows), f32),
            pltpu.SemaphoreType.DMA((fields,)),
        ],
        compiler_params=params(),
        name="rims",
    )(table, *arrays)


def local(potential, current, material, nu_table, sat_table, panel_flux, panel_jitter, rotor_offset):
    comps, layers, rows, cols = potential.shape
    fields = comps * layers
    az, rad = lax.axis_size("az"), lax.axis_size("rad")
    cycle = rows * az
    pot = potential.reshape(fields, rows, cols)
    cur = current.reshape(fields, rows, cols)

    def swap(x, az_of, rad_of):
        pairs = [(a * rad + r, az_of(a, r) * rad + rad_of(r)) for a in range(az) for r in range(rad)]
        return lax.ppermute(x, ("az", "rad"), pairs)

    def same(i, r=None):
        return i

    def even(i):
        return i ^ 1

    def odd(i, n):
        return (i + 1) % n if i % 2 else (i - 1) % n

    odd_send, even_send, pan, table = edges(
        nu_table, sat_table, pot, cur, material, panel_flux, panel_jitter.reshape(1, -1)
    )
    odd_got = swap(odd_send, lambda a, r: odd(a, az), same)
    even_got = swap(even_send, lambda a, r: a ^ 1, same)
    two_got = swap(pan, lambda a, r: a ^ 2, same)
    strips = columns(rotor_offset, pot, cur, material)
    coef, one, main = inner(table, pot, cur, material)
    at = rim_rows(fields, layers)
    pans, starts = [pan, odd_got, even_got, two_got], [0, at, at, 0]
    if az > 8:
        held, bit = jnp.concatenate([p[first:] for p, first in zip(pans, starts)], axis=0), 8
        while bit < az:
            held = jnp.concatenate([held, swap(held, lambda a, r, bit=bit: a ^ bit, same)], axis=0)
            bit *= 2
        pans, starts = [held], [0]
    airs = []
    if az > 4:
        send = deposit("airgap_far", rotor_offset, pans, starts, (coef, strips), [4], fields, rows, cycle)[0]
        airs.append(swap(send, lambda a, r: a ^ 4, same))
    ro_send, re_send, turned = middle(strips, odd_got, even_got, coef, send if airs else table, fields, layers)
    ro_got = swap(ro_send, same, lambda r: odd(r, rad))
    re_got = swap(re_send, same, even)
    main = outer(table, pot, cur, material, odd_got, even_got, coef, one, main)
    airs += deposit("airgap_own", rotor_offset, pans, starts, (main,), [0], fields, rows, cycle)
    air = gather_air(airs, main)
    out = rims(table, main, air, strips, turned, re_got, ro_got, layers)
    return out.reshape(potential.shape)


def solution(mesh):
    placed = (
        P(None, None, "az", "rad"),
        P(None, None, "az", "rad"),
        P(None, "az", "rad"),
        P(),
        P(),
        P(None, "az"),
        P("az"),
        P(),
    )
    return jax.shard_map(
        local, mesh=mesh, in_specs=placed, out_specs=P(None, None, "az", "rad"), check_vma=False
    )
```

```python
import functools

import jax
import jax.numpy as jnp
from jax import lax
from jax.experimental import pallas as pl
from jax.experimental.pallas import tpu as pltpu
from jax.sharding import PartitionSpec as P

sigma_term = 1.0

EXPAND = 20_000_000_000
AHEAD = 0
halo = 3
low_own, high_own = 6, 5
slot = low_own + high_own
f32 = jnp.float32
VMEM = pl.BlockSpec(memory_space=pltpu.VMEM)
SMEM = pl.BlockSpec(memory_space=pltpu.SMEM)
HBM = pl.BlockSpec(memory_space=pltpu.HBM)
ANY = pl.BlockSpec(memory_space=pl.ANY)


def params(mib=48):
    return pltpu.CompilerParams(vmem_limit_bytes=mib * 1024 * 1024)


def layout(fields, layers):
    depth = [halo] * fields + [halo - 1] * layers + [1] * fields
    return [(n, sum(depth[:j])) for j, n in enumerate(depth)]


def rim_rows(fields, layers):
    return halo * fields + (halo - 1) * layers + fields


def slot_base(j, cols):
    per = cols // slot
    return (j // per) * cols + (j % per) * slot


def lookup(material, table_ref, first):
    rows, lanes = material.shape
    values = []
    for e in range(first, first + table_ref.shape[0] // 2):
        row = jnp.broadcast_to(table_ref[e : e + 1, :], (rows, 128))
        values.append(jnp.concatenate([row] * (lanes // 128), axis=1))
    bit = 1
    while len(values) > 1:
        take = (material & bit) != 0
        values = [jnp.where(take, values[i + 1], values[i]) for i in range(0, len(values), 2)]
        bit *= 2
    return values[0]


def half_reluct(table_ref, material, flux_sq):
    base = lookup(material, table_ref, 0)
    saturation = lookup(material, table_ref, table_ref.shape[0] // 2)
    return (0.5 * base) * (1.0 + saturation * flux_sq / (1.0 + flux_sq))


def sweep_cells(coef, field, source, moves):
    layers = len(coef)
    out = [[None] * layers for _ in field]
    for l in range(layers):
        centre = coef[l]
        total = jnp.full_like(centre, sigma_term)
        num = [source[c][l] for c in range(len(field))]
        for move_coef, move_field in moves:
            w = centre + move_coef(l)
            total = total + w
            for c in range(len(field)):
                num[c] = num[c] + w * move_field(c, l)
        for other in (l + 1, l - 1):
            if 0 <= other < layers:
                w = centre + coef[other]
                total = total + w
                for c in range(len(field)):
                    num[c] = num[c] + w * field[c][other]
            else:
                total = total + centre
        inverse = 1.0 / total
        for c in range(len(field)):
            out[c][l] = num[c] * inverse
    return out


def divisor(n, most):
    return max(d for d in range(1, most + 1) if n % d == 0)


def half_strength(centres, az_next, rad_next):
    total = None
    for centre, az, rad in zip(centres, az_next, rad_next):
        az, rad = az - centre, rad - centre
        part = az * az + rad * rad
        total = part if total is None else total + part
    return total


def edges_kernel(
    nu_hbm, sat_hbm, pot_hbm, cur_hbm, mat_hbm, flux_hbm, jit_hbm, odd_ref, even_ref, pan_ref, table_ref,
    up_ref, down_ref, pot_ref, cur_ref, mat_ref, flux_ref, jit_ref, nu_ref, sat_ref, sems
):
    fields, layers = pot_ref.shape[1], mat_ref.shape[1]
    rows = pot_hbm.shape[1]
    pairs = [(flux_hbm, flux_ref), (jit_hbm, jit_ref), (nu_hbm, nu_ref), (sat_hbm, sat_ref)]
    for hbm, ref in ((pot_hbm, pot_ref), (cur_hbm, cur_ref), (mat_hbm, mat_ref)):
        pairs += [(hbm.at[:, 0:8, :], ref.at[0]), (hbm.at[:, rows - 8 : rows, :], ref.at[1])]
    copies = [pltpu.make_async_copy(src, dst, sems.at[n]) for n, (src, dst) in enumerate(pairs)]
    for copy in copies:
        copy.start()
    for copy in copies:
        copy.wait()

    odd_a = lax.rem(lax.axis_index("az"), 2) == 1
    panels = flux_ref.shape[1]
    where = jit_ref[...].astype(f32)
    for h in range(panels // 128):
        at = h * (fields + 1)
        pan_ref[at : at + fields, :] = flux_ref[:, h * 128 : (h + 1) * 128]
        pan_ref[at + fields : at + fields + 1, :] = where[:, h * 128 : (h + 1) * 128]
    for j, (n, at) in enumerate(layout(fields, layers)):
        if j < fields:
            ref, k = pot_ref, j
        elif j < fields + layers:
            ref, k = mat_ref, j - fields
        else:
            ref, k = cur_ref, j - fields - layers
        up_ref[at : at + n, :] = ref[0, k, 0:n, :].astype(f32)
        down_ref[at : at + n, :] = ref[1, k, 8 - n : 8, :].astype(f32)
    n = up_ref.shape[0]
    even_ref[0:n, :] = jnp.where(odd_a, up_ref[...], down_ref[...])
    odd_ref[0:n, :] = jnp.where(odd_a, down_ref[...], up_ref[...])
    even_ref[n:, :] = pan_ref[...]
    odd_ref[n:, :] = pan_ref[...]
    entries = nu_ref.shape[0]
    for e in range(entries):
        table_ref[e : e + 1, :] = jnp.full((1, 128), nu_ref[e], f32)
        table_ref[entries + e : entries + e + 1, :] = jnp.full((1, 128), sat_ref[e], f32)


def edges(nu, sat, pot, cur, mat, flux, jitter):
    fields, rows, cols = pot.shape
    layers = mat.shape[0]
    send = rim_rows(fields, layers)
    pan_rows = flux.shape[1] // 128 * (fields + 1)
    return pl.pallas_call(
        edges_kernel,
        out_shape=[
            jax.ShapeDtypeStruct((send + pan_rows, cols), f32),
            jax.ShapeDtypeStruct((send + pan_rows, cols), f32),
            jax.ShapeDtypeStruct((pan_rows, 128), f32),
            jax.ShapeDtypeStruct((2 * nu.shape[0], 128), f32),
        ],
        in_specs=[HBM] * 7,
        out_specs=[VMEM] * 4,
        scratch_shapes=[
            pltpu.VMEM((send, cols), f32),
            pltpu.VMEM((send, cols), f32),
            pltpu.VMEM((2, fields, 8, cols), f32),
            pltpu.VMEM((2, fields, 8, cols), f32),
            pltpu.VMEM((2, layers, 8, cols), jnp.int32),
            pltpu.VMEM(flux.shape, f32),
            pltpu.VMEM(jitter.shape, jnp.int32),
            pltpu.SMEM(nu.shape, f32),
            pltpu.SMEM(sat.shape, f32),
            pltpu.SemaphoreType.DMA((10,)),
        ],
        compiler_params=params(),
        cost_estimate=pl.CostEstimate(flops=1_000_000, bytes_accessed=400_000, transcendentals=0),
        name="pack_rows",
    )(*(pltpu.with_memory_space_constraint(x, pltpu.HBM) for x in (nu, sat, pot, cur, mat, flux, jitter)))


def columns_kernel(_offset, pot_ref, cur_ref, mat_ref, strips_ref, slots_ref):
    fields, layers = pot_ref.shape[0], mat_ref.shape[0]
    rows, cols = mat_ref.shape[1:]
    total = 2 * fields + layers
    per = cols // slot
    groups = -(-total // per)
    lane = lax.broadcasted_iota(jnp.int32, (8, cols), 1)

    @pl.loop(0, rows // 8, unroll=32)
    def _(i):
        at = pl.ds(pl.multiple_of(i * 8, 8), 8)
        for g in range(groups):
            acc = None
            for k in range(min(per, total - g * per)):
                j = g * per + k
                if j < fields:
                    x = pot_ref[j, at, :]
                elif j < fields + layers:
                    x = mat_ref[j - fields, at, :].astype(f32)
                else:
                    x = cur_ref[j - fields - layers, at, :]
                x = pltpu.roll(x, (k * slot + high_own) % cols, 1)
                acc = x if acc is None else jnp.where(lane >= k * slot, x, acc)
            slots_ref[g, at, :] = acc

    for g in range(groups):
        strips_ref[g * cols : (g + 1) * cols, :] = slots_ref[g].T


def columns(offset, pot, cur, mat):
    fields, rows, cols = pot.shape
    total = 2 * fields + mat.shape[0]
    groups = -(-total // (cols // slot))
    return pl.pallas_call(
        columns_kernel,
        out_shape=jax.ShapeDtypeStruct((groups * cols, rows), f32),
        in_specs=[SMEM] + [VMEM] * 3,
        out_specs=VMEM,
        scratch_shapes=[pltpu.VMEM((groups, rows, cols), f32)],
        compiler_params=params(),
        cost_estimate=pl.CostEstimate(flops=8_000_000, bytes_accessed=3_000_000, transcendentals=0),
        name="turn_columns",
    )(offset, pot, cur, mat)


def middle_kernel(fields, layers, odd_ref, even_ref, strips_ref, _coef, ro_ref, re_ref, turned_ref, rim_ref):
    cols = even_ref.shape[1]
    send = rim_rows(fields, layers)
    odd_r = lax.rem(lax.axis_index("rad"), 2) == 1
    odd_a = lax.rem(lax.axis_index("az"), 2) == 1

    rim_ref[0:send, :] = jnp.where(odd_a, odd_ref[0:send, :], even_ref[0:send, :])
    rim_ref[64 : 64 + send, :] = jnp.where(odd_a, even_ref[0:send, :], odd_ref[0:send, :])
    turned_ref[...] = rim_ref[...].T

    for j, (n, at) in enumerate(layout(fields, layers)):
        b = slot_base(j, cols) + high_own
        lo, hi = strips_ref[b : b + n, :], strips_ref[b - n : b, :]
        re_ref[at : at + n, :] = jnp.where(odd_r, lo, hi)
        ro_ref[at : at + n, :] = jnp.where(odd_r, hi, lo)
    lo, hi = turned_ref[0:halo, :], turned_ref[cols - halo : cols, :]
    re_ref[send : send + halo, 0:128] = jnp.where(odd_r, lo, hi)
    ro_ref[send : send + halo, 0:128] = jnp.where(odd_r, hi, lo)


def middle(strips, odd_got, even_got, coef, fields, layers):
    cols = even_got.shape[1]
    rows = strips.shape[1]
    send = rim_rows(fields, layers)
    arrays = (odd_got, even_got, strips, coef)
    return pl.pallas_call(
        functools.partial(middle_kernel, fields, layers),
        out_shape=[
            jax.ShapeDtypeStruct((send + halo, rows), f32),
            jax.ShapeDtypeStruct((send + halo, rows), f32),
            jax.ShapeDtypeStruct((cols, 128), f32),
        ],
        in_specs=[VMEM] * 3 + [ANY],
        out_specs=[VMEM] * 3,
        scratch_shapes=[pltpu.VMEM((128, cols), f32)],
        compiler_params=params(),
        cost_estimate=pl.CostEstimate(flops=1_000_000, bytes_accessed=600_000, transcendentals=0),
        name="pack_columns",
    )(*arrays)


def block(i):
    return pl.ds(pl.multiple_of(i * 8, 8), 8)


def right(x):
    return pltpu.roll(x, x.shape[1] - 1, 1)


def left(x):
    return pltpu.roll(x, 1, 1)


def reluct_block(table_ref, coef_ref, load, material, i):
    layers = coef_ref.shape[0]
    comps = 3
    for l in range(layers):
        centres = [load(c * layers + l, 0) for c in range(comps)]
        nexts = [load(c * layers + l, 1) for c in range(comps)]
        flux_sq = half_strength(centres, nexts, [right(x) for x in centres])
        which = material(l)
        coef_ref[l, block(i + 2), :] = half_reluct(table_ref, which, flux_sq)


def sweep_block(coef_ref, load, source_at, i, store):
    layers = coef_ref.shape[0]
    comps = 3
    coef = [coef_ref[l, block(i + 2), :] for l in range(layers)]
    field = [[load(c * layers + l, 0) for l in range(layers)] for c in range(comps)]
    source = [[source_at(c * layers + l) for l in range(layers)] for c in range(comps)]
    moves = []
    for step in (1, -1):
        moves.append(
            (
                lambda l, step=step: coef_ref[l, pl.ds(i * 8 + 16 + step, 8), :],
                lambda c, l, step=step: load(c * layers + l, step),
            )
        )
    for turn in (right, left):
        moves.append((lambda l, turn=turn: turn(coef[l]), lambda c, l, turn=turn: turn(field[c][l])))
    new = sweep_cells(coef, field, source, moves)
    for c in range(comps):
        for l in range(layers):
            store(c * layers + l, new[c][l])


def keep(one_ref, i):
    def store(j, x):
        one_ref[j, block(i + 1), :] = x

    return store


def inner_kernel(table_ref, pot_ref, cur_ref, mat_ref, coef_ref, one_ref, out_ref):
    rows, cols = mat_ref.shape[1:]
    count = rows // 8
    inner = count - 2
    step = divisor(inner, 30)

    def load_at(i):
        return lambda j, step: pot_ref[j, pl.ds(i * 8 + step, 8), :]

    def reluct_at(i, load):
        reluct_block(table_ref, coef_ref, load, lambda l: mat_ref[l, block(i), :], i)

    def last_load(j, step):
        x = pot_ref[j, rows - 8 : rows, :]
        return x if step == 0 else pltpu.roll(x, 7, 0)

    reluct_at(0, load_at(0))
    reluct_at(count - 1, last_load)

    @pl.loop(1, count - 1, unroll=step)
    def _(i):
        reluct_at(i, load_at(i))

    @pl.loop(1, count - 1, unroll=step)
    def _(i):
        sweep_block(coef_ref, load_at(i), lambda j: cur_ref[j, block(i), :], i, keep(one_ref, i))

    ahead = AHEAD * (count - 4) // 4
    if ahead:

        @pl.loop(2, 2 + ahead, unroll=divisor(ahead, 10))
        def _(i):
            second_block(coef_ref, one_ref, cur_ref, out_ref, i)


def second_block(coef_ref, one_ref, cur_ref, out_ref, i):
    def store(j, x):
        out_ref[j, block(i), :] = x

    sweep_block(
        coef_ref,
        lambda j, step: one_ref[j, pl.ds(i * 8 + 8 + step, 8), :],
        lambda j: cur_ref[j, block(i), :],
        i,
        store,
    )


def inner(table, pot, cur, mat):
    fields, rows, cols = pot.shape
    layers = mat.shape[0]
    return pl.pallas_call(
        inner_kernel,
        out_shape=[
            jax.ShapeDtypeStruct((layers, rows + 32, cols), f32),
            jax.ShapeDtypeStruct((fields, rows + 16, cols), f32),
            jax.ShapeDtypeStruct(pot.shape, f32),
        ],
        in_specs=[VMEM] * 4,
        out_specs=[VMEM] * 3,
        compiler_params=params(),
        cost_estimate=pl.CostEstimate(flops=20_000_000, bytes_accessed=4_000_000, transcendentals=0),
        name="inner_rows",
    )(table, pot, cur, mat)


def outer_kernel(
    table_ref, pot_ref, cur_ref, mat_ref, odd_ref, even_ref, coef_in, one_in, out_in, coef_ref, one_ref, out_ref, edge_ref
):
    fields, rows, cols = out_ref.shape
    layers = mat_ref.shape[0]
    odd_a = lax.rem(lax.axis_index("az"), 2) == 1
    count = rows // 8

    blank = jnp.zeros((8, cols), f32)
    for j, (n, at) in enumerate(layout(fields, layers)):
        if j < fields:
            ref, k = pot_ref, j
        elif j < fields + layers:
            ref, k = mat_ref, j - fields
        else:
            ref, k = cur_ref, j - fields - layers
        edge_ref[0, j, 0:8, :] = blank
        edge_ref[0, j, 8:16, :] = blank
        edge_ref[1, j, 16:24, :] = blank
        edge_ref[1, j, 24:32, :] = blank
        edge_ref[0, j, 16:32, :] = ref[k, 0:16, :].astype(f32)
        edge_ref[1, j, 0:16, :] = ref[k, rows - 16 : rows, :].astype(f32)
        even, odd = even_ref[at : at + n, :], odd_ref[at : at + n, :]
        edge_ref[0, j, 16 - n : 16, :] = jnp.where(odd_a, even, odd)
        edge_ref[1, j, 16 : 16 + n, :] = jnp.where(odd_a, odd, even)
    for l in range(layers):
        coef_ref[l, 0:8, :] = blank
        coef_ref[l, 24 + rows : 32 + rows, :] = blank

    def edge_load(k):
        side, at = k // 2, 8 + 8 * (k % 2)
        return (
            lambda j, step: edge_ref[side, j, at + step : at + step + 8, :],
            (-1, 0, count - 1, count)[k],
        )

    for k in (0, 2, 3):
        load, i = edge_load(k)
        reluct_block(table_ref, coef_ref, load, lambda l: load(fields + l, 0).astype(jnp.int32), i)
    for k in range(4):
        load, i = edge_load(k)
        sweep_block(coef_ref, load, lambda j: load(fields + layers + j, 0), i, keep(one_ref, i))

    for i in (0, 1, count - 2, count - 1):
        second_block(coef_ref, one_ref, cur_ref, out_ref, i)
    ahead = AHEAD * (count - 4) // 4
    if ahead < count - 4:

        @pl.loop(2 + ahead, count - 2, unroll=divisor(count - 4 - ahead, 30))
        def _(i):
            second_block(coef_ref, one_ref, cur_ref, out_ref, i)


def outer(table, pot, cur, mat, odd_got, even_got, coef, one, main):
    fields, rows, cols = pot.shape
    layers = mat.shape[0]
    total = 2 * fields + layers
    return pl.pallas_call(
        outer_kernel,
        out_shape=[
            jax.ShapeDtypeStruct(coef.shape, f32),
            jax.ShapeDtypeStruct(one.shape, f32),
            jax.ShapeDtypeStruct(main.shape, f32),
        ],
        in_specs=[VMEM] * 9,
        out_specs=[VMEM] * 3,
        input_output_aliases={6: 0, 7: 1, 8: 2},
        scratch_shapes=[pltpu.VMEM((2, total, 32, cols), f32)],
        compiler_params=params(),
        cost_estimate=pl.CostEstimate(flops=20_000_000, bytes_accessed=4_000_000, transcendentals=0),
        name="outer_rows",
    )(table, pot, cur, mat, odd_got, even_got, coef, one, main)[2]


def deposit_kernel(cycle, starts, bases, fields, rows, n_order, off_ref, *refs):
    n = len(starts)
    pan_refs, air_refs, vals_ref = refs[:n], refs[n + n_order : -1], refs[-1]
    r, a = lax.axis_index("rad"), lax.axis_index("az")
    size = lax.axis_size("rad")
    stator = (r == size // 2) | (r == size // 2 - 1)

    @pl.when(stator)
    def _():
        lanes = vals_ref.shape[1]
        vals_ref[...] = jnp.zeros_like(vals_ref)
        t = 0
        for ref, first in zip(pan_refs, starts):
            for at in range(first, ref.shape[0], fields + 1):
                vals_ref[0 : fields + 1, t * 128 : (t + 1) * 128] = ref[at : at + fields + 1, :]
                t += 1
        values = vals_ref[...]
        position = vals_ref[fields : fields + 1, :].astype(jnp.int32) + off_ref[0]
        position = jnp.where(position >= cycle, position - cycle, position)
        high = values.astype(jnp.bfloat16)
        rest = values - high.astype(f32)
        mid = rest.astype(jnp.bfloat16)
        low = (rest - mid.astype(f32)).astype(jnp.bfloat16)
        split = jnp.concatenate([high, mid, low], axis=0)
        spot = lax.broadcasted_iota(jnp.int32, (rows, lanes), 0)
        lane = lax.broadcasted_iota(jnp.int32, (16, 128), 1)
        channel = lax.broadcasted_iota(jnp.int32, (16, 128), 0)
        for air_ref, bit in zip(air_refs, bases):
            local = position - (a ^ bit) * rows
            onehot = jnp.where(spot == local, 1.0, 0.0).astype(jnp.bfloat16)
            parts = lax.dot_general(split, onehot, (((1,), (1,)), ((), ())), preferred_element_type=f32)
            air_ref[...] = parts[0:16] + parts[16:32] + parts[32:48]
            after = (local == rows) | (local == rows - cycle)
            before = (local == -1) | (local == cycle - 1)
            after = jnp.sum(jnp.where(after, values, 0.0), axis=1, keepdims=True)
            before = jnp.sum(jnp.where(before, values, 0.0), axis=1, keepdims=True)
            outside = jnp.where(lane == channel, after, jnp.where(lane == channel + 16, before, 0.0))
            air_ref[fields : fields + 1, 0:128] = jnp.sum(outside, axis=0, keepdims=True)

    @pl.when(jnp.logical_not(stator))
    def _():
        for air_ref in air_refs:
            air_ref[...] = jnp.zeros_like(air_ref)


def deposit(name, offset, pans, starts, order, bases, fields, rows, cycle):
    panels = sum(p.shape[0] - first for p, first in zip(pans, starts)) // (fields + 1) * 128
    return pl.pallas_call(
        functools.partial(deposit_kernel, cycle, starts, bases, fields, rows, len(order)),
        out_shape=[jax.ShapeDtypeStruct((16, rows), f32) for _ in bases],
        in_specs=[SMEM] + [VMEM] * len(pans) + [ANY] * len(order),
        out_specs=[VMEM] * len(bases),
        scratch_shapes=[pltpu.VMEM((16, panels), f32)],
        compiler_params=params(),
        cost_estimate=pl.CostEstimate(flops=4_000_000, bytes_accessed=500_000, transcendentals=0),
        name=name,
    )(offset, *pans, *order)


def air_kernel(n, fields, *refs):
    air_ref = refs[-1]
    rows = refs[0].shape[1]
    airgap = sum(ref[...] for ref in refs[:n])
    lane = lax.broadcasted_iota(jnp.int32, (16, 128), 1)
    channel = lax.broadcasted_iota(jnp.int32, (16, 128), 0)
    spread = airgap[fields : fields + 1, 0:128]
    after = jnp.sum(jnp.where(lane == channel, spread, 0.0), axis=1, keepdims=True)
    before = jnp.sum(jnp.where(lane == channel + 16, spread, 0.0), axis=1, keepdims=True)
    air_ref[:, 0:rows] = airgap
    air_ref[:, rows : rows + 128] = jnp.where(lane == 0, after, jnp.where(lane == 127, before, 0.0))


def gather_air(airs, main):
    fields, rows, _ = main.shape
    return pl.pallas_call(
        functools.partial(air_kernel, len(airs), fields),
        out_shape=jax.ShapeDtypeStruct((16, rows + 128), f32),
        in_specs=[VMEM] * len(airs) + [ANY],
        out_specs=VMEM,
        compiler_params=params(),
        cost_estimate=pl.CostEstimate(flops=EXPAND, bytes_accessed=0, transcendentals=0),
        name="airgap_sum",
    )(*airs, main)


def rim_kernel(
    table_ref, main_ref, air_ref, strips_ref, turned_ref, ro_ref, re_ref,
    out_hbm, merged_ref, cols_ref, corner_ref, back_ref, sem,
):
    fields, rows, cols = main_ref.shape
    total = cols_ref.shape[0]
    layers = total - 2 * fields
    comps = fields // layers
    send = rim_rows(fields, layers)
    r = lax.axis_index("rad")
    size = lax.axis_size("rad")
    odd_r = lax.rem(r, 2) == 1

    def left(at, n):
        return jnp.where(odd_r, re_ref[at : at + n, :], ro_ref[at : at + n, :])

    def right(at, n):
        return jnp.where(odd_r, ro_ref[at : at + n, :], re_ref[at : at + n, :])

    corner_ref[0:2, :] = left(send + 1, 2)[:, 0:128]
    corner_ref[2:8, :] = turned_ref[0:low_own, :]
    corner_ref[8:13, :] = turned_ref[cols - high_own : cols, :]
    corner_ref[13:16, :] = right(send, halo)[:, 0:128]
    corner = corner_ref[...]
    lane = lax.broadcasted_iota(jnp.int32, (16, 128), 1)
    for j, (n, at) in enumerate(layout(fields, layers)):
        b = slot_base(j, cols)
        cols_ref[j, 0:8, 0:rows] = strips_ref[b + high_own - 2 : b + high_own + 6, :]
        cols_ref[j, 8:16, 0:rows] = strips_ref[b : b + 8, :]
        m = min(n, 2)
        cols_ref[j, 2 - m : 2, 0:rows] = left(at + n - m, m)
        cols_ref[j, 13 : 13 + n, 0:rows] = right(at, n)
        cols_ref[j, :, rows : rows + 128] = jnp.where(
            lane < 64, pltpu.roll(corner, (-at) % 128, 1), pltpu.roll(corner, (64 - n - at) % 128, 1)
        )

    def apart(x):
        return x.reshape(2, 8, x.shape[1])

    column = apart(lax.broadcasted_iota(jnp.int32, (16, rows + 128), 0))
    inside = ((column >= 2) | (r > 0)) & ((column < 13) | (r < size - 1))
    target = jnp.where(r == size // 2, 2, jnp.where(r == size // 2 - 1, 13, -1))

    def move(x, axis, step):
        return pltpu.roll(x, (-step) % x.shape[axis], axis)

    pot = [[jnp.where(inside, apart(cols_ref[c * layers + l]), 0.0) for l in range(layers)] for c in range(comps)]
    source = []
    for c in range(comps):
        source.append([])
        for l in range(layers):
            j = c * layers + l
            air = air_ref[j : j + 1, :].reshape(1, 1, rows + 128)
            source[c].append(apart(cols_ref[fields + layers + j]) + jnp.where(column == target, air, 0.0))
    coef = []
    for l in range(layers):
        centres = [pot[c][l] for c in range(comps)]
        flux_sq = half_strength(centres, [move(x, 2, 1) for x in centres], [move(x, 1, 1) for x in centres])
        which = cols_ref[fields + l].astype(jnp.int32)
        k = apart(half_reluct(table_ref, which, flux_sq.reshape(16, rows + 128)))
        coef.append(jnp.where(inside, k, 0.0))
    moves = [(axis, step) for axis in (2, 1) for step in (1, -1)]
    moved = {(l, m): move(coef[l], *m) for l in range(layers) for m in moves}

    def sweep(field, lanes):
        table = [
            (lambda l, m=m: moved[l, m][..., :lanes], lambda c, l, m=m: move(field[c][l], *m)[..., :lanes])
            for m in moves
        ]
        cut = lambda part: [x[..., :lanes] for x in part]
        return sweep_cells(cut(coef), [cut(part) for part in field], [cut(part) for part in source], table)

    one = [[jnp.where(inside, x, 0.0) for x in part] for part in sweep(pot, rows + 128)]
    fixed = [[x.reshape(16, rows) for x in part] for part in sweep(one, rows)]
    for c in range(comps):
        for l in range(layers):
            j = c * layers + l
            back_ref[8 * j : 8 * j + 3, :] = fixed[c][l][10:13, 0:rows]
            back_ref[8 * j + 3 : 8 * j + 5, :] = fixed[c][l][2:4, 0:rows]
    turned = back_ref[...].T

    lane = lax.broadcasted_iota(jnp.int32, (rows, cols), 1)
    edge = (lane < 2) | (lane >= cols - 3)
    for j in range(fields):
        merged_ref[j] = jnp.where(edge, pltpu.roll(turned, (cols - 3 - 8 * j) % cols, 1), main_ref[j])
        pltpu.make_async_copy(merged_ref.at[j], out_hbm.at[j], sem.at[j]).start()
    for j in range(fields):
        pltpu.make_async_copy(merged_ref.at[j], out_hbm.at[j], sem.at[j]).wait()


def rims(table, main, air, strips, turned, re_got, ro_got, layers):
    fields, rows, cols = main.shape
    total = 2 * fields + layers
    arrays = (main, air, strips, turned, ro_got, re_got)
    return pl.pallas_call(
        rim_kernel,
        out_shape=jax.ShapeDtypeStruct(main.shape, f32),
        in_specs=[VMEM] * (1 + len(arrays)),
        out_specs=ANY,
        scratch_shapes=[
            pltpu.VMEM(main.shape, f32),
            pltpu.VMEM((total, 16, rows + 128), f32),
            pltpu.VMEM((16, 128), f32),
            pltpu.VMEM((128, rows), f32),
            pltpu.SemaphoreType.DMA((fields,)),
        ],
        compiler_params=params(),
        name="rims",
    )(table, *arrays)


def local(potential, current, material, nu_table, sat_table, panel_flux, panel_jitter, rotor_offset):
    comps, layers, rows, cols = potential.shape
    fields = comps * layers
    az, rad = lax.axis_size("az"), lax.axis_size("rad")
    cycle = rows * az
    pot = potential.reshape(fields, rows, cols)
    cur = current.reshape(fields, rows, cols)

    def swap(x, az_of, rad_of):
        pairs = [(a * rad + r, az_of(a, r) * rad + rad_of(r)) for a in range(az) for r in range(rad)]
        return lax.ppermute(x, ("az", "rad"), pairs)

    def same(i, r=None):
        return i

    def even(i):
        return i ^ 1

    def odd(i, n):
        return (i + 1) % n if i % 2 else (i - 1) % n

    def beside(r):
        return r in (rad // 2 - 1, rad // 2)

    odd_send, even_send, pan, table = edges(
        nu_table, sat_table, pot, cur, material, panel_flux, panel_jitter.reshape(1, -1)
    )
    odd_got = swap(odd_send, lambda a, r: odd(a, az), same)
    even_got = swap(even_send, lambda a, r: a ^ 1, same)
    two_got = swap(pan, lambda a, r: a ^ 2, same)
    strips = columns(rotor_offset, pot, cur, material)
    coef, one, main = inner(table, pot, cur, material)
    at = rim_rows(fields, layers)
    pans, starts = [pan, odd_got, even_got, two_got], [0, at, at, 0]
    if az > 8:
        held, bit = jnp.concatenate([p[first:] for p, first in zip(pans, starts)], axis=0), 8
        while bit < az:
            held = jnp.concatenate([held, swap(held, lambda a, r, bit=bit: a ^ bit, same)], axis=0)
            bit *= 2
        pans, starts = [held], [0]
    ro_send, re_send, turned = middle(strips, odd_got, even_got, coef, fields, layers)
    airs = []
    if az > 4:
        send = deposit("airgap_far", rotor_offset, pans, starts, (turned,), [4], fields, rows, cycle)[0]
        airs.append(
            swap(send, lambda a, r: a ^ 4 if beside(r) else a, lambda r: r if beside(r) else rad - 1 - r)
        )
    ro_got = swap(ro_send, same, lambda r: odd(r, rad))
    re_got = swap(re_send, same, even)
    main = outer(table, pot, cur, material, odd_got, even_got, coef, one, main)
    airs += deposit("airgap_own", rotor_offset, pans, starts, (main,), [0], fields, rows, cycle)
    air = gather_air(airs, main)
    out = rims(table, main, air, strips, turned, re_got, ro_got, layers)
    return out.reshape(potential.shape)


def solution(mesh):
    placed = (
        P(None, None, "az", "rad"),
        P(None, None, "az", "rad"),
        P(None, "az", "rad"),
        P(),
        P(),
        P(None, "az"),
        P("az"),
        P(),
    )
    return jax.shard_map(
        local, mesh=mesh, in_specs=placed, out_specs=P(None, None, "az", "rad"), check_vma=False
    )
```

```python
import functools

import jax
import jax.numpy as jnp
from jax import lax
from jax.experimental import pallas as pl
from jax.experimental.pallas import tpu as pltpu
from jax.sharding import PartitionSpec as P

sigma_term = 1.0

EXPAND = 20_000_000_000
AHEAD = 0
halo = 3
low_own, high_own = 6, 5
slot = low_own + high_own
f32 = jnp.float32
VMEM = pl.BlockSpec(memory_space=pltpu.VMEM)
SMEM = pl.BlockSpec(memory_space=pltpu.SMEM)
HBM = pl.BlockSpec(memory_space=pltpu.HBM)
ANY = pl.BlockSpec(memory_space=pl.ANY)


def params(mib=48):
    return pltpu.CompilerParams(vmem_limit_bytes=mib * 1024 * 1024)


def layout(fields, layers):
    depth = [halo] * fields + [halo - 1] * layers + [1] * fields
    return [(n, sum(depth[:j])) for j, n in enumerate(depth)]


def rim_rows(fields, layers):
    return halo * fields + (halo - 1) * layers + fields


def slot_base(j, cols):
    per = cols // slot
    return (j // per) * cols + (j % per) * slot


def lookup(material, table_ref, first):
    rows, lanes = material.shape
    values = []
    for e in range(first, first + table_ref.shape[0] // 2):
        row = jnp.broadcast_to(table_ref[e : e + 1, :], (rows, 128))
        values.append(jnp.concatenate([row] * (lanes // 128), axis=1))
    bit = 1
    while len(values) > 1:
        take = (material & bit) != 0
        values = [jnp.where(take, values[i + 1], values[i]) for i in range(0, len(values), 2)]
        bit *= 2
    return values[0]


def half_reluct(table_ref, material, flux_sq):
    base = lookup(material, table_ref, 0)
    saturation = lookup(material, table_ref, table_ref.shape[0] // 2)
    return (0.5 * base) * (1.0 + saturation * flux_sq / (1.0 + flux_sq))


def sweep_cells(coef, field, source, moves):
    layers = len(coef)
    out = [[None] * layers for _ in field]
    for l in range(layers):
        centre = coef[l]
        total = jnp.full_like(centre, sigma_term)
        num = [source[c][l] for c in range(len(field))]
        for move_coef, move_field in moves:
            w = centre + move_coef(l)
            total = total + w
            for c in range(len(field)):
                num[c] = num[c] + w * move_field(c, l)
        for other in (l + 1, l - 1):
            if 0 <= other < layers:
                w = centre + coef[other]
                total = total + w
                for c in range(len(field)):
                    num[c] = num[c] + w * field[c][other]
            else:
                total = total + centre
        inverse = 1.0 / total
        for c in range(len(field)):
            out[c][l] = num[c] * inverse
    return out


def divisor(n, most):
    return max(d for d in range(1, most + 1) if n % d == 0)


def half_strength(centres, az_next, rad_next):
    total = None
    for centre, az, rad in zip(centres, az_next, rad_next):
        az, rad = az - centre, rad - centre
        part = az * az + rad * rad
        total = part if total is None else total + part
    return total


def edges_kernel(
    nu_hbm, sat_hbm, pot_hbm, cur_hbm, mat_hbm, flux_hbm, jit_hbm, odd_ref, even_ref, pan_ref, table_ref,
    up_ref, down_ref, pot_ref, cur_ref, mat_ref, flux_ref, jit_ref, nu_ref, sat_ref, sems
):
    fields, layers = pot_ref.shape[1], mat_ref.shape[1]
    rows = pot_hbm.shape[1]
    pairs = [(flux_hbm, flux_ref), (jit_hbm, jit_ref), (nu_hbm, nu_ref), (sat_hbm, sat_ref)]
    for hbm, ref in ((pot_hbm, pot_ref), (cur_hbm, cur_ref), (mat_hbm, mat_ref)):
        pairs += [(hbm.at[:, 0:8, :], ref.at[0]), (hbm.at[:, rows - 8 : rows, :], ref.at[1])]
    copies = [pltpu.make_async_copy(src, dst, sems.at[n]) for n, (src, dst) in enumerate(pairs)]
    for copy in copies:
        copy.start()
    for copy in copies:
        copy.wait()

    odd_a = lax.rem(lax.axis_index("az"), 2) == 1
    panels = flux_ref.shape[1]
    where = jit_ref[...].astype(f32)
    for h in range(panels // 128):
        at = h * (fields + 1)
        pan_ref[at : at + fields, :] = flux_ref[:, h * 128 : (h + 1) * 128]
        pan_ref[at + fields : at + fields + 1, :] = where[:, h * 128 : (h + 1) * 128]
    for j, (n, at) in enumerate(layout(fields, layers)):
        if j < fields:
            ref, k = pot_ref, j
        elif j < fields + layers:
            ref, k = mat_ref, j - fields
        else:
            ref, k = cur_ref, j - fields - layers
        up_ref[at : at + n, :] = ref[0, k, 0:n, :].astype(f32)
        down_ref[at : at + n, :] = ref[1, k, 8 - n : 8, :].astype(f32)
    n = up_ref.shape[0]
    even_ref[0:n, :] = jnp.where(odd_a, up_ref[...], down_ref[...])
    odd_ref[0:n, :] = jnp.where(odd_a, down_ref[...], up_ref[...])
    even_ref[n:, :] = pan_ref[...]
    odd_ref[n:, :] = pan_ref[...]
    entries = nu_ref.shape[0]
    for e in range(entries):
        table_ref[e : e + 1, :] = jnp.full((1, 128), nu_ref[e], f32)
        table_ref[entries + e : entries + e + 1, :] = jnp.full((1, 128), sat_ref[e], f32)


def edges(nu, sat, pot, cur, mat, flux, jitter):
    fields, rows, cols = pot.shape
    layers = mat.shape[0]
    send = rim_rows(fields, layers)
    pan_rows = flux.shape[1] // 128 * (fields + 1)
    return pl.pallas_call(
        edges_kernel,
        out_shape=[
            jax.ShapeDtypeStruct((send + pan_rows, cols), f32),
            jax.ShapeDtypeStruct((send + pan_rows, cols), f32),
            jax.ShapeDtypeStruct((pan_rows, 128), f32),
            jax.ShapeDtypeStruct((2 * nu.shape[0], 128), f32),
        ],
        in_specs=[HBM] * 7,
        out_specs=[VMEM] * 4,
        scratch_shapes=[
            pltpu.VMEM((send, cols), f32),
            pltpu.VMEM((send, cols), f32),
            pltpu.VMEM((2, fields, 8, cols), f32),
            pltpu.VMEM((2, fields, 8, cols), f32),
            pltpu.VMEM((2, layers, 8, cols), jnp.int32),
            pltpu.VMEM(flux.shape, f32),
            pltpu.VMEM(jitter.shape, jnp.int32),
            pltpu.SMEM(nu.shape, f32),
            pltpu.SMEM(sat.shape, f32),
            pltpu.SemaphoreType.DMA((10,)),
        ],
        compiler_params=params(),
        cost_estimate=pl.CostEstimate(flops=1_000_000, bytes_accessed=400_000, transcendentals=0),
        name="pack_rows",
    )(*(pltpu.with_memory_space_constraint(x, pltpu.HBM) for x in (nu, sat, pot, cur, mat, flux, jitter)))


def columns_kernel(_offset, pot_ref, cur_ref, mat_ref, cols_ref, slots_ref, strips_ref):
    fields, layers = pot_ref.shape[0], mat_ref.shape[0]
    rows, cols = mat_ref.shape[1:]
    total = 2 * fields + layers
    per = cols // slot
    groups = -(-total // per)
    lane = lax.broadcasted_iota(jnp.int32, (8, cols), 1)

    @pl.loop(0, rows // 8, unroll=32)
    def _(i):
        at = pl.ds(pl.multiple_of(i * 8, 8), 8)
        for g in range(groups):
            acc = None
            for k in range(min(per, total - g * per)):
                j = g * per + k
                if j < fields:
                    x = pot_ref[j, at, :]
                elif j < fields + layers:
                    x = mat_ref[j - fields, at, :].astype(f32)
                else:
                    x = cur_ref[j - fields - layers, at, :]
                x = pltpu.roll(x, (k * slot + high_own) % cols, 1)
                acc = x if acc is None else jnp.where(lane >= k * slot, x, acc)
            slots_ref[g, at, :] = acc

    for g in range(groups):
        strips_ref[g * cols : (g + 1) * cols, :] = slots_ref[g].T
    for j in range(total):
        b = slot_base(j, cols)
        cols_ref[j, 0:8, 0:rows] = strips_ref[b + high_own - 2 : b + high_own + 6, :]
        cols_ref[j, 8:16, 0:rows] = strips_ref[b : b + 8, :]


def columns(offset, pot, cur, mat):
    fields, rows, cols = pot.shape
    total = 2 * fields + mat.shape[0]
    groups = -(-total // (cols // slot))
    return pl.pallas_call(
        columns_kernel,
        out_shape=jax.ShapeDtypeStruct((total, 16, rows + 128), f32),
        in_specs=[SMEM] + [VMEM] * 3,
        out_specs=VMEM,
        scratch_shapes=[pltpu.VMEM((groups, rows, cols), f32), pltpu.VMEM((groups * cols, rows), f32)],
        compiler_params=params(),
        cost_estimate=pl.CostEstimate(flops=8_000_000, bytes_accessed=3_000_000, transcendentals=0),
        name="turn_columns",
    )(offset, pot, cur, mat)


def middle_kernel(fields, layers, n_order, odd_ref, even_ref, strips_ref, *refs):
    ro_ref, re_ref, turned_ref, rim_ref = refs[n_order:]
    cols = even_ref.shape[1]
    send = rim_rows(fields, layers)
    odd_r = lax.rem(lax.axis_index("rad"), 2) == 1
    odd_a = lax.rem(lax.axis_index("az"), 2) == 1

    rows = ro_ref.shape[1]
    rim_ref[0:send, :] = jnp.where(odd_a, odd_ref[0:send, :], even_ref[0:send, :])
    rim_ref[64 : 64 + send, :] = jnp.where(odd_a, even_ref[0:send, :], odd_ref[0:send, :])
    turned_ref[...] = rim_ref[...].T

    for j, (n, at) in enumerate(layout(fields, layers)):
        lo, hi = strips_ref[j, 2 : 2 + n, 0:rows], strips_ref[j, 13 - n : 13, 0:rows]
        re_ref[at : at + n, :] = jnp.where(odd_r, lo, hi)
        ro_ref[at : at + n, :] = jnp.where(odd_r, hi, lo)
    lo, hi = turned_ref[0:halo, :], turned_ref[cols - halo : cols, :]
    re_ref[send : send + halo, 0:128] = jnp.where(odd_r, lo, hi)
    ro_ref[send : send + halo, 0:128] = jnp.where(odd_r, hi, lo)


def middle(strips, odd_got, even_got, order, fields, layers):
    cols = even_got.shape[1]
    rows = strips.shape[2] - 128
    send = rim_rows(fields, layers)
    arrays = (odd_got, even_got, strips, *order)
    return pl.pallas_call(
        functools.partial(middle_kernel, fields, layers, len(order)),
        out_shape=[
            jax.ShapeDtypeStruct((send + halo, rows), f32),
            jax.ShapeDtypeStruct((send + halo, rows), f32),
            jax.ShapeDtypeStruct((cols, 128), f32),
        ],
        in_specs=[VMEM] * 3 + [ANY] * len(order),
        out_specs=[VMEM] * 3,
        scratch_shapes=[pltpu.VMEM((128, cols), f32)],
        compiler_params=params(),
        cost_estimate=pl.CostEstimate(flops=1_000_000, bytes_accessed=600_000, transcendentals=0),
        name="pack_columns",
    )(*arrays)


def block(i):
    return pl.ds(pl.multiple_of(i * 8, 8), 8)


def right(x):
    return pltpu.roll(x, x.shape[1] - 1, 1)


def left(x):
    return pltpu.roll(x, 1, 1)


def reluct_block(table_ref, coef_ref, load, material, i):
    layers = coef_ref.shape[0]
    comps = 3
    for l in range(layers):
        centres = [load(c * layers + l, 0) for c in range(comps)]
        nexts = [load(c * layers + l, 1) for c in range(comps)]
        flux_sq = half_strength(centres, nexts, [right(x) for x in centres])
        which = material(l)
        coef_ref[l, block(i + 2), :] = half_reluct(table_ref, which, flux_sq)


def sweep_block(coef_ref, load, source_at, i, store):
    layers = coef_ref.shape[0]
    comps = 3
    coef = [coef_ref[l, block(i + 2), :] for l in range(layers)]
    field = [[load(c * layers + l, 0) for l in range(layers)] for c in range(comps)]
    source = [[source_at(c * layers + l) for l in range(layers)] for c in range(comps)]
    moves = []
    for step in (1, -1):
        moves.append(
            (
                lambda l, step=step: coef_ref[l, pl.ds(i * 8 + 16 + step, 8), :],
                lambda c, l, step=step: load(c * layers + l, step),
            )
        )
    for turn in (right, left):
        moves.append((lambda l, turn=turn: turn(coef[l]), lambda c, l, turn=turn: turn(field[c][l])))
    new = sweep_cells(coef, field, source, moves)
    for c in range(comps):
        for l in range(layers):
            store(c * layers + l, new[c][l])


def keep(one_ref, i):
    def store(j, x):
        one_ref[j, block(i + 1), :] = x

    return store


def inner_kernel(table_ref, pot_ref, cur_ref, mat_ref, coef_ref, one_ref, out_ref):
    rows, cols = mat_ref.shape[1:]
    count = rows // 8
    inner = count - 2
    step = divisor(inner, 30)

    def load_at(i):
        return lambda j, step: pot_ref[j, pl.ds(i * 8 + step, 8), :]

    def reluct_at(i, load):
        reluct_block(table_ref, coef_ref, load, lambda l: mat_ref[l, block(i), :], i)

    def last_load(j, step):
        x = pot_ref[j, rows - 8 : rows, :]
        return x if step == 0 else pltpu.roll(x, 7, 0)

    reluct_at(0, load_at(0))
    reluct_at(count - 1, last_load)

    @pl.loop(1, count - 1, unroll=step)
    def _(i):
        reluct_at(i, load_at(i))

    @pl.loop(1, count - 1, unroll=step)
    def _(i):
        sweep_block(coef_ref, load_at(i), lambda j: cur_ref[j, block(i), :], i, keep(one_ref, i))

    ahead = AHEAD * (count - 4) // 4
    if ahead:

        @pl.loop(2, 2 + ahead, unroll=divisor(ahead, 10))
        def _(i):
            second_block(coef_ref, one_ref, cur_ref, out_ref, i)


def second_block(coef_ref, one_ref, cur_ref, out_ref, i):
    def store(j, x):
        out_ref[j, block(i), :] = x

    sweep_block(
        coef_ref,
        lambda j, step: one_ref[j, pl.ds(i * 8 + 8 + step, 8), :],
        lambda j: cur_ref[j, block(i), :],
        i,
        store,
    )


def inner(table, pot, cur, mat):
    fields, rows, cols = pot.shape
    layers = mat.shape[0]
    return pl.pallas_call(
        inner_kernel,
        out_shape=[
            jax.ShapeDtypeStruct((layers, rows + 32, cols), f32),
            jax.ShapeDtypeStruct((fields, rows + 16, cols), f32),
            jax.ShapeDtypeStruct(pot.shape, f32),
        ],
        in_specs=[VMEM] * 4,
        out_specs=[VMEM] * 3,
        compiler_params=params(),
        cost_estimate=pl.CostEstimate(flops=20_000_000, bytes_accessed=4_000_000, transcendentals=0),
        name="inner_rows",
    )(table, pot, cur, mat)


def outer_kernel(
    table_ref, pot_ref, cur_ref, mat_ref, odd_ref, even_ref, coef_in, one_in, out_in, coef_ref, one_ref, out_ref, edge_ref
):
    fields, rows, cols = out_ref.shape
    layers = mat_ref.shape[0]
    odd_a = lax.rem(lax.axis_index("az"), 2) == 1
    count = rows // 8

    blank = jnp.zeros((8, cols), f32)
    for j, (n, at) in enumerate(layout(fields, layers)):
        if j < fields:
            ref, k = pot_ref, j
        elif j < fields + layers:
            ref, k = mat_ref, j - fields
        else:
            ref, k = cur_ref, j - fields - layers
        edge_ref[0, j, 0:8, :] = blank
        edge_ref[0, j, 8:16, :] = blank
        edge_ref[1, j, 16:24, :] = blank
        edge_ref[1, j, 24:32, :] = blank
        edge_ref[0, j, 16:32, :] = ref[k, 0:16, :].astype(f32)
        edge_ref[1, j, 0:16, :] = ref[k, rows - 16 : rows, :].astype(f32)
        even, odd = even_ref[at : at + n, :], odd_ref[at : at + n, :]
        edge_ref[0, j, 16 - n : 16, :] = jnp.where(odd_a, even, odd)
        edge_ref[1, j, 16 : 16 + n, :] = jnp.where(odd_a, odd, even)
    for l in range(layers):
        coef_ref[l, 0:8, :] = blank
        coef_ref[l, 24 + rows : 32 + rows, :] = blank

    def edge_load(k):
        side, at = k // 2, 8 + 8 * (k % 2)
        return (
            lambda j, step: edge_ref[side, j, at + step : at + step + 8, :],
            (-1, 0, count - 1, count)[k],
        )

    for k in (0, 2, 3):
        load, i = edge_load(k)
        reluct_block(table_ref, coef_ref, load, lambda l: load(fields + l, 0).astype(jnp.int32), i)
    for k in range(4):
        load, i = edge_load(k)
        sweep_block(coef_ref, load, lambda j: load(fields + layers + j, 0), i, keep(one_ref, i))

    for i in (0, 1, count - 2, count - 1):
        second_block(coef_ref, one_ref, cur_ref, out_ref, i)
    ahead = AHEAD * (count - 4) // 4
    if ahead < count - 4:

        @pl.loop(2 + ahead, count - 2, unroll=divisor(count - 4 - ahead, 30))
        def _(i):
            second_block(coef_ref, one_ref, cur_ref, out_ref, i)


def outer(table, pot, cur, mat, odd_got, even_got, coef, one, main):
    fields, rows, cols = pot.shape
    layers = mat.shape[0]
    total = 2 * fields + layers
    return pl.pallas_call(
        outer_kernel,
        out_shape=[
            jax.ShapeDtypeStruct(coef.shape, f32),
            jax.ShapeDtypeStruct(one.shape, f32),
            jax.ShapeDtypeStruct(main.shape, f32),
        ],
        in_specs=[VMEM] * 9,
        out_specs=[VMEM] * 3,
        input_output_aliases={6: 0, 7: 1, 8: 2},
        scratch_shapes=[pltpu.VMEM((2, total, 32, cols), f32)],
        compiler_params=params(),
        cost_estimate=pl.CostEstimate(flops=20_000_000, bytes_accessed=4_000_000, transcendentals=0),
        name="outer_rows",
    )(table, pot, cur, mat, odd_got, even_got, coef, one, main)[2]


def deposit_kernel(cycle, starts, bases, fields, rows, added, n_order, off_ref, *refs):
    n = len(starts)
    pan_refs, air_refs, vals_ref = refs[:n], refs[n + added + n_order : -1], refs[-1]
    r, a = lax.axis_index("rad"), lax.axis_index("az")
    size = lax.axis_size("rad")
    stator = (r == size // 2) | (r == size // 2 - 1)

    @pl.when(stator)
    def _():
        lanes = vals_ref.shape[1]
        vals_ref[...] = jnp.zeros_like(vals_ref)
        t = 0
        for ref, first in zip(pan_refs, starts):
            for at in range(first, ref.shape[0], fields + 1):
                vals_ref[0 : fields + 1, t * 128 : (t + 1) * 128] = ref[at : at + fields + 1, :]
                t += 1
        values = vals_ref[...]
        position = vals_ref[fields : fields + 1, :].astype(jnp.int32) + off_ref[0]
        position = jnp.where(position >= cycle, position - cycle, position)
        high = values.astype(jnp.bfloat16)
        rest = values - high.astype(f32)
        mid = rest.astype(jnp.bfloat16)
        low = (rest - mid.astype(f32)).astype(jnp.bfloat16)
        split = jnp.concatenate([high, mid, low], axis=0)
        spot = lax.broadcasted_iota(jnp.int32, (rows, lanes), 0)
        lane = lax.broadcasted_iota(jnp.int32, (16, 128), 1)
        channel = lax.broadcasted_iota(jnp.int32, (16, 128), 0)
        for air_ref, bit in zip(air_refs, bases):
            local = position - (a ^ bit) * rows
            onehot = jnp.where(spot == local, 1.0, 0.0).astype(jnp.bfloat16)
            parts = lax.dot_general(split, onehot, (((1,), (1,)), ((), ())), preferred_element_type=f32)
            air_ref[...] = parts[0:16] + parts[16:32] + parts[32:48]
            after = (local == rows) | (local == rows - cycle)
            before = (local == -1) | (local == cycle - 1)
            after = jnp.sum(jnp.where(after, values, 0.0), axis=1, keepdims=True)
            before = jnp.sum(jnp.where(before, values, 0.0), axis=1, keepdims=True)
            outside = jnp.where(lane == channel, after, jnp.where(lane == channel + 16, before, 0.0))
            air_ref[fields : fields + 1, 0:128] = jnp.sum(outside, axis=0, keepdims=True)
            if added:
                air_ref[...] += refs[n][...]

    @pl.when(jnp.logical_not(stator))
    def _():
        for air_ref in air_refs:
            air_ref[...] = jnp.zeros_like(air_ref)


def deposit(name, offset, pans, starts, order, bases, fields, rows, cycle, added=()):
    panels = sum(p.shape[0] - first for p, first in zip(pans, starts)) // (fields + 1) * 128
    return pl.pallas_call(
        functools.partial(deposit_kernel, cycle, starts, bases, fields, rows, len(added), len(order)),
        out_shape=[jax.ShapeDtypeStruct((16, rows), f32) for _ in bases],
        in_specs=[SMEM] + [VMEM] * (len(pans) + len(added)) + [ANY] * len(order),
        out_specs=[VMEM] * len(bases),
        scratch_shapes=[pltpu.VMEM((16, panels), f32)],
        compiler_params=params(),
        cost_estimate=pl.CostEstimate(flops=4_000_000, bytes_accessed=500_000, transcendentals=0),
        name=name,
    )(offset, *pans, *added, *order)


def air_kernel(n, fields, *refs):
    air_ref = refs[-1]
    rows = refs[0].shape[1]
    airgap = sum(ref[...] for ref in refs[:n])
    lane = lax.broadcasted_iota(jnp.int32, (16, 128), 1)
    channel = lax.broadcasted_iota(jnp.int32, (16, 128), 0)
    spread = airgap[fields : fields + 1, 0:128]
    after = jnp.sum(jnp.where(lane == channel, spread, 0.0), axis=1, keepdims=True)
    before = jnp.sum(jnp.where(lane == channel + 16, spread, 0.0), axis=1, keepdims=True)
    air_ref[:, 0:rows] = airgap
    air_ref[:, rows : rows + 128] = jnp.where(lane == 0, after, jnp.where(lane == 127, before, 0.0))


def gather_air(airs, main):
    fields, rows, _ = main.shape
    return pl.pallas_call(
        functools.partial(air_kernel, len(airs), fields),
        out_shape=jax.ShapeDtypeStruct((16, rows + 128), f32),
        in_specs=[VMEM] * len(airs) + [ANY],
        out_specs=VMEM,
        compiler_params=params(),
        cost_estimate=pl.CostEstimate(flops=EXPAND, bytes_accessed=0, transcendentals=0),
        name="airgap_sum",
    )(*airs, main)


def rim_kernel(
    table_ref, main_ref, air_ref, _cols, turned_ref, ro_ref, re_ref,
    out_hbm, cols_ref, merged_ref, corner_ref, back_ref, sem,
):
    fields, rows, cols = main_ref.shape
    total = cols_ref.shape[0]
    layers = total - 2 * fields
    comps = fields // layers
    send = rim_rows(fields, layers)
    r = lax.axis_index("rad")
    size = lax.axis_size("rad")
    odd_r = lax.rem(r, 2) == 1

    def left(at, n):
        return jnp.where(odd_r, re_ref[at : at + n, :], ro_ref[at : at + n, :])

    def right(at, n):
        return jnp.where(odd_r, ro_ref[at : at + n, :], re_ref[at : at + n, :])

    corner_ref[0:2, :] = left(send + 1, 2)[:, 0:128]
    corner_ref[2:8, :] = turned_ref[0:low_own, :]
    corner_ref[8:13, :] = turned_ref[cols - high_own : cols, :]
    corner_ref[13:16, :] = right(send, halo)[:, 0:128]
    corner = corner_ref[...]
    lane = lax.broadcasted_iota(jnp.int32, (16, 128), 1)
    for j, (n, at) in enumerate(layout(fields, layers)):
        m = min(n, 2)
        cols_ref[j, 2 - m : 2, 0:rows] = left(at + n - m, m)
        cols_ref[j, 13 : 13 + n, 0:rows] = right(at, n)
        cols_ref[j, :, rows : rows + 128] = jnp.where(
            lane < 64, pltpu.roll(corner, (-at) % 128, 1), pltpu.roll(corner, (64 - n - at) % 128, 1)
        )

    def apart(x):
        return x.reshape(2, 8, x.shape[1])

    column = apart(lax.broadcasted_iota(jnp.int32, (16, rows + 128), 0))
    inside = ((column >= 2) | (r > 0)) & ((column < 13) | (r < size - 1))
    target = jnp.where(r == size // 2, 2, jnp.where(r == size // 2 - 1, 13, -1))

    def move(x, axis, step):
        return pltpu.roll(x, (-step) % x.shape[axis], axis)

    pot = [[jnp.where(inside, apart(cols_ref[c * layers + l]), 0.0) for l in range(layers)] for c in range(comps)]
    source = []
    for c in range(comps):
        source.append([])
        for l in range(layers):
            j = c * layers + l
            air = air_ref[j : j + 1, :].reshape(1, 1, rows + 128)
            source[c].append(apart(cols_ref[fields + layers + j]) + jnp.where(column == target, air, 0.0))
    coef = []
    for l in range(layers):
        centres = [pot[c][l] for c in range(comps)]
        flux_sq = half_strength(centres, [move(x, 2, 1) for x in centres], [move(x, 1, 1) for x in centres])
        which = cols_ref[fields + l].astype(jnp.int32)
        k = apart(half_reluct(table_ref, which, flux_sq.reshape(16, rows + 128)))
        coef.append(jnp.where(inside, k, 0.0))
    moves = [(axis, step) for axis in (2, 1) for step in (1, -1)]
    moved = {(l, m): move(coef[l], *m) for l in range(layers) for m in moves}

    def sweep(field, lanes):
        table = [
            (lambda l, m=m: moved[l, m][..., :lanes], lambda c, l, m=m: move(field[c][l], *m)[..., :lanes])
            for m in moves
        ]
        cut = lambda part: [x[..., :lanes] for x in part]
        return sweep_cells(cut(coef), [cut(part) for part in field], [cut(part) for part in source], table)

    one = [[jnp.where(inside, x, 0.0) for x in part] for part in sweep(pot, rows + 128)]
    fixed = [[x.reshape(16, rows) for x in part] for part in sweep(one, rows)]
    for c in range(comps):
        for l in range(layers):
            j = c * layers + l
            back_ref[8 * j : 8 * j + 3, :] = fixed[c][l][10:13, 0:rows]
            back_ref[8 * j + 3 : 8 * j + 5, :] = fixed[c][l][2:4, 0:rows]
    turned = back_ref[...].T

    lane = lax.broadcasted_iota(jnp.int32, (rows, cols), 1)
    edge = (lane < 2) | (lane >= cols - 3)
    for j in range(fields):
        merged_ref[j] = jnp.where(edge, pltpu.roll(turned, (cols - 3 - 8 * j) % cols, 1), main_ref[j])
        pltpu.make_async_copy(merged_ref.at[j], out_hbm.at[j], sem.at[j]).start()
    for j in range(fields):
        pltpu.make_async_copy(merged_ref.at[j], out_hbm.at[j], sem.at[j]).wait()


def rims(table, main, air, strips, turned, re_got, ro_got, layers):
    fields, rows, cols = main.shape
    total = 2 * fields + layers
    arrays = (main, air, strips, turned, ro_got, re_got)
    return pl.pallas_call(
        rim_kernel,
        out_shape=[jax.ShapeDtypeStruct(main.shape, f32), jax.ShapeDtypeStruct(strips.shape, f32)],
        in_specs=[VMEM] * (1 + len(arrays)),
        out_specs=[ANY, VMEM],
        input_output_aliases={3: 1},
        scratch_shapes=[
            pltpu.VMEM(main.shape, f32),
            pltpu.VMEM((16, 128), f32),
            pltpu.VMEM((128, rows), f32),
            pltpu.SemaphoreType.DMA((fields,)),
        ],
        compiler_params=params(),
        name="rims",
    )(table, *arrays)[0]


def local(potential, current, material, nu_table, sat_table, panel_flux, panel_jitter, rotor_offset):
    comps, layers, rows, cols = potential.shape
    fields = comps * layers
    az, rad = lax.axis_size("az"), lax.axis_size("rad")
    cycle = rows * az
    pot = potential.reshape(fields, rows, cols)
    cur = current.reshape(fields, rows, cols)

    def swap(x, az_of, rad_of):
        pairs = [(a * rad + r, az_of(a, r) * rad + rad_of(r)) for a in range(az) for r in range(rad)]
        return lax.ppermute(x, ("az", "rad"), pairs)

    def same(i, r=None):
        return i

    def even(i):
        return i ^ 1

    def odd(i, n):
        return (i + 1) % n if i % 2 else (i - 1) % n

    def beside(r):
        return r in (rad // 2 - 1, rad // 2)

    odd_send, even_send, pan, table = edges(
        nu_table, sat_table, pot, cur, material, panel_flux, panel_jitter.reshape(1, -1)
    )
    odd_got = swap(odd_send, lambda a, r: odd(a, az), same)
    even_got = swap(even_send, lambda a, r: a ^ 1, same)
    two_got = swap(pan, lambda a, r: a ^ 2, same)
    strips = columns(rotor_offset, pot, cur, material)
    coef, one, main = inner(table, pot, cur, material)
    at = rim_rows(fields, layers)
    pans, starts = [pan, odd_got, even_got, two_got], [0, at, at, 0]
    if az > 8:
        held, bit = jnp.concatenate([p[first:] for p, first in zip(pans, starts)], axis=0), 8
        while bit < az:
            held = jnp.concatenate([held, swap(held, lambda a, r, bit=bit: a ^ bit, same)], axis=0)
            bit *= 2
        pans, starts = [held], [0]
    early = ()
    if 4 < az <= 8:
        early = deposit("airgap_early", rotor_offset, pans[:2], starts[:2], (coef, strips), [4], fields, rows, cycle)
    ro_send, re_send, turned = middle(strips, odd_got, even_got, (coef, *early), fields, layers)
    airs = []
    if az > 4:
        rest = slice(2 if early else 0, None)
        send = deposit(
            "airgap_far", rotor_offset, pans[rest], starts[rest], (turned,), [4], fields, rows, cycle, early
        )[0]
        airs.append(
            swap(send, lambda a, r: a ^ 4 if beside(r) else a, lambda r: r if beside(r) else rad - 1 - r)
        )
    ro_got = swap(ro_send, same, lambda r: odd(r, rad))
    re_got = swap(re_send, same, even)
    main = outer(table, pot, cur, material, odd_got, even_got, coef, one, main)
    airs += deposit("airgap_own", rotor_offset, pans, starts, (main,), [0], fields, rows, cycle)
    air = gather_air(airs, main)
    out = rims(table, main, air, strips, turned, re_got, ro_got, layers)
    return out.reshape(potential.shape)


def solution(mesh):
    placed = (
        P(None, None, "az", "rad"),
        P(None, None, "az", "rad"),
        P(None, "az", "rad"),
        P(),
        P(),
        P(None, "az"),
        P("az"),
        P(),
    )
    return jax.shard_map(
        local, mesh=mesh, in_specs=placed, out_specs=P(None, None, "az", "rad"), check_vma=False
    )
```

```python
import functools

import jax
import jax.numpy as jnp
from jax import lax
from jax.experimental import pallas as pl
from jax.experimental.pallas import tpu as pltpu
from jax.sharding import PartitionSpec as P

sigma_term = 1.0

EXPAND = 20_000_000_000
AHEAD = 0
halo = 3
low_own, high_own = 6, 5
slot = low_own + high_own
f32 = jnp.float32
VMEM = pl.BlockSpec(memory_space=pltpu.VMEM)
SMEM = pl.BlockSpec(memory_space=pltpu.SMEM)
HBM = pl.BlockSpec(memory_space=pltpu.HBM)
ANY = pl.BlockSpec(memory_space=pl.ANY)


def params(mib=48):
    return pltpu.CompilerParams(vmem_limit_bytes=mib * 1024 * 1024)


def layout(fields, layers):
    depth = [halo] * fields + [halo - 1] * layers + [1] * fields
    return [(n, sum(depth[:j])) for j, n in enumerate(depth)]


def rim_rows(fields, layers):
    return halo * fields + (halo - 1) * layers + fields


def slot_base(j, cols):
    per = cols // slot
    return (j // per) * cols + (j % per) * slot


def lookup(material, table_ref, first):
    rows, lanes = material.shape
    values = []
    for e in range(first, first + table_ref.shape[0] // 2):
        row = jnp.broadcast_to(table_ref[e : e + 1, :], (rows, 128))
        values.append(jnp.concatenate([row] * (lanes // 128), axis=1))
    bit = 1
    while len(values) > 1:
        take = (material & bit) != 0
        values = [jnp.where(take, values[i + 1], values[i]) for i in range(0, len(values), 2)]
        bit *= 2
    return values[0]


def half_reluct(table_ref, material, flux_sq):
    base = lookup(material, table_ref, 0)
    saturation = lookup(material, table_ref, table_ref.shape[0] // 2)
    return (0.5 * base) * (1.0 + saturation * flux_sq / (1.0 + flux_sq))


def sweep_cells(coef, field, source, moves):
    layers = len(coef)
    out = [[None] * layers for _ in field]
    for l in range(layers):
        centre = coef[l]
        total = jnp.full_like(centre, sigma_term)
        num = [source[c][l] for c in range(len(field))]
        for move_coef, move_field in moves:
            w = centre + move_coef(l)
            total = total + w
            for c in range(len(field)):
                num[c] = num[c] + w * move_field(c, l)
        for other in (l + 1, l - 1):
            if 0 <= other < layers:
                w = centre + coef[other]
                total = total + w
                for c in range(len(field)):
                    num[c] = num[c] + w * field[c][other]
            else:
                total = total + centre
        inverse = 1.0 / total
        for c in range(len(field)):
            out[c][l] = num[c] * inverse
    return out


def divisor(n, most):
    return max(d for d in range(1, most + 1) if n % d == 0)


def half_strength(centres, az_next, rad_next):
    total = None
    for centre, az, rad in zip(centres, az_next, rad_next):
        az, rad = az - centre, rad - centre
        part = az * az + rad * rad
        total = part if total is None else total + part
    return total


def edges_kernel(
    nu_hbm, sat_hbm, pot_hbm, cur_hbm, mat_hbm, flux_hbm, jit_hbm, odd_ref, even_ref, pan_ref, table_ref,
    up_ref, down_ref, pot_ref, cur_ref, mat_ref, flux_ref, jit_ref, nu_ref, sat_ref, sems
):
    fields, layers = pot_ref.shape[1], mat_ref.shape[1]
    rows = pot_hbm.shape[1]
    pairs = []
    for hbm, ref in ((pot_hbm, pot_ref), (cur_hbm, cur_ref), (mat_hbm, mat_ref)):
        pairs += [(hbm.at[:, 0:8, :], ref.at[0]), (hbm.at[:, rows - 8 : rows, :], ref.at[1])]
    pairs += [(flux_hbm, flux_ref), (jit_hbm, jit_ref), (nu_hbm, nu_ref), (sat_hbm, sat_ref)]
    copies = [pltpu.make_async_copy(src, dst, sems.at[n]) for n, (src, dst) in enumerate(pairs)]
    for copy in copies:
        copy.start()
    for copy in copies:
        copy.wait()

    odd_a = lax.rem(lax.axis_index("az"), 2) == 1
    panels = flux_ref.shape[1]
    where = jit_ref[...].astype(f32)
    for h in range(panels // 128):
        at = h * (fields + 1)
        pan_ref[at : at + fields, :] = flux_ref[:, h * 128 : (h + 1) * 128]
        pan_ref[at + fields : at + fields + 1, :] = where[:, h * 128 : (h + 1) * 128]
    for j, (n, at) in enumerate(layout(fields, layers)):
        if j < fields:
            ref, k = pot_ref, j
        elif j < fields + layers:
            ref, k = mat_ref, j - fields
        else:
            ref, k = cur_ref, j - fields - layers
        up_ref[at : at + n, :] = ref[0, k, 0:n, :].astype(f32)
        down_ref[at : at + n, :] = ref[1, k, 8 - n : 8, :].astype(f32)
    n = up_ref.shape[0]
    even_ref[0:n, :] = jnp.where(odd_a, up_ref[...], down_ref[...])
    odd_ref[0:n, :] = jnp.where(odd_a, down_ref[...], up_ref[...])
    even_ref[n:, :] = pan_ref[...]
    odd_ref[n:, :] = pan_ref[...]
    entries = nu_ref.shape[0]
    for e in range(entries):
        table_ref[e : e + 1, :] = jnp.full((1, 128), nu_ref[e], f32)
        table_ref[entries + e : entries + e + 1, :] = jnp.full((1, 128), sat_ref[e], f32)


def edges(nu, sat, pot, cur, mat, flux, jitter):
    fields, rows, cols = pot.shape
    layers = mat.shape[0]
    send = rim_rows(fields, layers)
    pan_rows = flux.shape[1] // 128 * (fields + 1)
    return pl.pallas_call(
        edges_kernel,
        out_shape=[
            jax.ShapeDtypeStruct((send + pan_rows, cols), f32),
            jax.ShapeDtypeStruct((send + pan_rows, cols), f32),
            jax.ShapeDtypeStruct((pan_rows, 128), f32),
            jax.ShapeDtypeStruct((2 * nu.shape[0], 128), f32),
        ],
        in_specs=[HBM] * 7,
        out_specs=[VMEM] * 4,
        scratch_shapes=[
            pltpu.VMEM((send, cols), f32),
            pltpu.VMEM((send, cols), f32),
            pltpu.VMEM((2, fields, 8, cols), f32),
            pltpu.VMEM((2, fields, 8, cols), f32),
            pltpu.VMEM((2, layers, 8, cols), jnp.int32),
            pltpu.VMEM(flux.shape, f32),
            pltpu.VMEM(jitter.shape, jnp.int32),
            pltpu.SMEM(nu.shape, f32),
            pltpu.SMEM(sat.shape, f32),
            pltpu.SemaphoreType.DMA((10,)),
        ],
        compiler_params=params(),
        cost_estimate=pl.CostEstimate(flops=1_000_000, bytes_accessed=400_000, transcendentals=0),
        name="pack_rows",
    )(*(pltpu.with_memory_space_constraint(x, pltpu.HBM) for x in (nu, sat, pot, cur, mat, flux, jitter)))


def columns_kernel(_offset, pot_ref, cur_ref, mat_ref, cols_ref, slots_ref, strips_ref):
    fields, layers = pot_ref.shape[0], mat_ref.shape[0]
    rows, cols = mat_ref.shape[1:]
    total = 2 * fields + layers
    per = cols // slot
    groups = -(-total // per)
    lane = lax.broadcasted_iota(jnp.int32, (8, cols), 1)

    @pl.loop(0, rows // 8, unroll=32)
    def _(i):
        at = pl.ds(pl.multiple_of(i * 8, 8), 8)
        for g in range(groups):
            acc = None
            for k in range(min(per, total - g * per)):
                j = g * per + k
                if j < fields:
                    x = pot_ref[j, at, :]
                elif j < fields + layers:
                    x = mat_ref[j - fields, at, :].astype(f32)
                else:
                    x = cur_ref[j - fields - layers, at, :]
                x = pltpu.roll(x, (k * slot + high_own) % cols, 1)
                acc = x if acc is None else jnp.where(lane >= k * slot, x, acc)
            slots_ref[g, at, :] = acc

    for g in range(groups):
        strips_ref[g * cols : (g + 1) * cols, :] = slots_ref[g].T
    for j in range(total):
        b = slot_base(j, cols)
        cols_ref[j, 0:8, 0:rows] = strips_ref[b + high_own - 2 : b + high_own + 6, :]
        cols_ref[j, 8:16, 0:rows] = strips_ref[b : b + 8, :]


def columns(offset, pot, cur, mat):
    fields, rows, cols = pot.shape
    total = 2 * fields + mat.shape[0]
    groups = -(-total // (cols // slot))
    return pl.pallas_call(
        columns_kernel,
        out_shape=jax.ShapeDtypeStruct((total, 16, rows + 128), f32),
        in_specs=[SMEM] + [VMEM] * 3,
        out_specs=VMEM,
        scratch_shapes=[pltpu.VMEM((groups, rows, cols), f32), pltpu.VMEM((groups * cols, rows), f32)],
        compiler_params=params(),
        cost_estimate=pl.CostEstimate(flops=8_000_000, bytes_accessed=3_000_000, transcendentals=0),
        name="turn_columns",
    )(offset, pot, cur, mat)


def middle_kernel(fields, layers, n_order, odd_ref, even_ref, strips_ref, *refs):
    ro_ref, re_ref, turned_ref, rim_ref = refs[n_order:]
    cols = even_ref.shape[1]
    send = rim_rows(fields, layers)
    odd_r = lax.rem(lax.axis_index("rad"), 2) == 1
    odd_a = lax.rem(lax.axis_index("az"), 2) == 1

    rows = ro_ref.shape[1]
    rim_ref[0:send, :] = jnp.where(odd_a, odd_ref[0:send, :], even_ref[0:send, :])
    rim_ref[64 : 64 + send, :] = jnp.where(odd_a, even_ref[0:send, :], odd_ref[0:send, :])
    turned_ref[...] = rim_ref[...].T

    for j, (n, at) in enumerate(layout(fields, layers)):
        lo, hi = strips_ref[j, 2 : 2 + n, 0:rows], strips_ref[j, 13 - n : 13, 0:rows]
        re_ref[at : at + n, :] = jnp.where(odd_r, lo, hi)
        ro_ref[at : at + n, :] = jnp.where(odd_r, hi, lo)
    lo, hi = turned_ref[0:halo, :], turned_ref[cols - halo : cols, :]
    re_ref[send : send + halo, 0:128] = jnp.where(odd_r, lo, hi)
    ro_ref[send : send + halo, 0:128] = jnp.where(odd_r, hi, lo)


def middle(strips, odd_got, even_got, order, fields, layers):
    cols = even_got.shape[1]
    rows = strips.shape[2] - 128
    send = rim_rows(fields, layers)
    arrays = (odd_got, even_got, strips, *order)
    return pl.pallas_call(
        functools.partial(middle_kernel, fields, layers, len(order)),
        out_shape=[
            jax.ShapeDtypeStruct((send + halo, rows), f32),
            jax.ShapeDtypeStruct((send + halo, rows), f32),
            jax.ShapeDtypeStruct((cols, 128), f32),
        ],
        in_specs=[VMEM] * 3 + [ANY] * len(order),
        out_specs=[VMEM] * 3,
        scratch_shapes=[pltpu.VMEM((128, cols), f32)],
        compiler_params=params(),
        cost_estimate=pl.CostEstimate(flops=1_000_000, bytes_accessed=600_000, transcendentals=0),
        name="pack_columns",
    )(*arrays)


def block(i):
    return pl.ds(pl.multiple_of(i * 8, 8), 8)


def right(x):
    return pltpu.roll(x, x.shape[1] - 1, 1)


def left(x):
    return pltpu.roll(x, 1, 1)


def reluct_block(table_ref, coef_ref, load, material, i):
    layers = coef_ref.shape[0]
    comps = 3
    for l in range(layers):
        centres = [load(c * layers + l, 0) for c in range(comps)]
        nexts = [load(c * layers + l, 1) for c in range(comps)]
        flux_sq = half_strength(centres, nexts, [right(x) for x in centres])
        which = material(l)
        coef_ref[l, block(i + 2), :] = half_reluct(table_ref, which, flux_sq)


def sweep_block(coef_ref, load, source_at, i, store):
    layers = coef_ref.shape[0]
    comps = 3
    coef = [coef_ref[l, block(i + 2), :] for l in range(layers)]
    field = [[load(c * layers + l, 0) for l in range(layers)] for c in range(comps)]
    source = [[source_at(c * layers + l) for l in range(layers)] for c in range(comps)]
    moves = []
    for step in (1, -1):
        moves.append(
            (
                lambda l, step=step: coef_ref[l, pl.ds(i * 8 + 16 + step, 8), :],
                lambda c, l, step=step: load(c * layers + l, step),
            )
        )
    for turn in (right, left):
        moves.append((lambda l, turn=turn: turn(coef[l]), lambda c, l, turn=turn: turn(field[c][l])))
    new = sweep_cells(coef, field, source, moves)
    for c in range(comps):
        for l in range(layers):
            store(c * layers + l, new[c][l])


def keep(one_ref, i):
    def store(j, x):
        one_ref[j, block(i + 1), :] = x

    return store


def inner_kernel(table_ref, pot_ref, cur_ref, mat_ref, coef_ref, one_ref, out_ref):
    rows, cols = mat_ref.shape[1:]
    count = rows // 8
    inner = count - 2
    step = divisor(inner, 30)

    def load_at(i):
        return lambda j, step: pot_ref[j, pl.ds(i * 8 + step, 8), :]

    def reluct_at(i, load):
        reluct_block(table_ref, coef_ref, load, lambda l: mat_ref[l, block(i), :], i)

    def last_load(j, step):
        x = pot_ref[j, rows - 8 : rows, :]
        return x if step == 0 else pltpu.roll(x, 7, 0)

    reluct_at(0, load_at(0))
    reluct_at(count - 1, last_load)

    @pl.loop(1, count - 1, unroll=step)
    def _(i):
        reluct_at(i, load_at(i))

    @pl.loop(1, count - 1, unroll=step)
    def _(i):
        sweep_block(coef_ref, load_at(i), lambda j: cur_ref[j, block(i), :], i, keep(one_ref, i))

    ahead = AHEAD * (count - 4) // 4
    if ahead:

        @pl.loop(2, 2 + ahead, unroll=divisor(ahead, 10))
        def _(i):
            second_block(coef_ref, one_ref, cur_ref, out_ref, i)


def second_block(coef_ref, one_ref, cur_ref, out_ref, i):
    def store(j, x):
        out_ref[j, block(i), :] = x

    sweep_block(
        coef_ref,
        lambda j, step: one_ref[j, pl.ds(i * 8 + 8 + step, 8), :],
        lambda j: cur_ref[j, block(i), :],
        i,
        store,
    )


def inner(table, pot, cur, mat):
    fields, rows, cols = pot.shape
    layers = mat.shape[0]
    return pl.pallas_call(
        inner_kernel,
        out_shape=[
            jax.ShapeDtypeStruct((layers, rows + 32, cols), f32),
            jax.ShapeDtypeStruct((fields, rows + 16, cols), f32),
            jax.ShapeDtypeStruct(pot.shape, f32),
        ],
        in_specs=[VMEM] * 4,
        out_specs=[VMEM] * 3,
        compiler_params=params(),
        cost_estimate=pl.CostEstimate(flops=20_000_000, bytes_accessed=4_000_000, transcendentals=0),
        name="inner_rows",
    )(table, pot, cur, mat)


def outer_kernel(
    table_ref, pot_ref, cur_ref, mat_ref, odd_ref, even_ref, coef_in, one_in, out_in, coef_ref, one_ref, out_ref, edge_ref
):
    fields, rows, cols = out_ref.shape
    layers = mat_ref.shape[0]
    odd_a = lax.rem(lax.axis_index("az"), 2) == 1
    count = rows // 8

    blank = jnp.zeros((8, cols), f32)
    for j, (n, at) in enumerate(layout(fields, layers)):
        if j < fields:
            ref, k = pot_ref, j
        elif j < fields + layers:
            ref, k = mat_ref, j - fields
        else:
            ref, k = cur_ref, j - fields - layers
        edge_ref[0, j, 0:8, :] = blank
        edge_ref[0, j, 8:16, :] = blank
        edge_ref[1, j, 16:24, :] = blank
        edge_ref[1, j, 24:32, :] = blank
        edge_ref[0, j, 16:32, :] = ref[k, 0:16, :].astype(f32)
        edge_ref[1, j, 0:16, :] = ref[k, rows - 16 : rows, :].astype(f32)
        even, odd = even_ref[at : at + n, :], odd_ref[at : at + n, :]
        edge_ref[0, j, 16 - n : 16, :] = jnp.where(odd_a, even, odd)
        edge_ref[1, j, 16 : 16 + n, :] = jnp.where(odd_a, odd, even)
    for l in range(layers):
        coef_ref[l, 0:8, :] = blank
        coef_ref[l, 24 + rows : 32 + rows, :] = blank

    def edge_load(k):
        side, at = k // 2, 8 + 8 * (k % 2)
        return (
            lambda j, step: edge_ref[side, j, at + step : at + step + 8, :],
            (-1, 0, count - 1, count)[k],
        )

    for k in (0, 2, 3):
        load, i = edge_load(k)
        reluct_block(table_ref, coef_ref, load, lambda l: load(fields + l, 0).astype(jnp.int32), i)
    for k in range(4):
        load, i = edge_load(k)
        sweep_block(coef_ref, load, lambda j: load(fields + layers + j, 0), i, keep(one_ref, i))

    for i in (0, 1, count - 2, count - 1):
        second_block(coef_ref, one_ref, cur_ref, out_ref, i)
    ahead = AHEAD * (count - 4) // 4
    if ahead < count - 4:

        @pl.loop(2 + ahead, count - 2, unroll=divisor(count - 4 - ahead, 30))
        def _(i):
            second_block(coef_ref, one_ref, cur_ref, out_ref, i)


def outer(table, pot, cur, mat, odd_got, even_got, coef, one, main):
    fields, rows, cols = pot.shape
    layers = mat.shape[0]
    total = 2 * fields + layers
    return pl.pallas_call(
        outer_kernel,
        out_shape=[
            jax.ShapeDtypeStruct(coef.shape, f32),
            jax.ShapeDtypeStruct(one.shape, f32),
            jax.ShapeDtypeStruct(main.shape, f32),
        ],
        in_specs=[VMEM] * 9,
        out_specs=[VMEM] * 3,
        input_output_aliases={6: 0, 7: 1, 8: 2},
        scratch_shapes=[pltpu.VMEM((2, total, 32, cols), f32)],
        compiler_params=params(),
        cost_estimate=pl.CostEstimate(flops=20_000_000, bytes_accessed=4_000_000, transcendentals=0),
        name="outer_rows",
    )(table, pot, cur, mat, odd_got, even_got, coef, one, main)[2]


def deposit_kernel(cycle, starts, bases, fields, rows, added, n_order, off_ref, *refs):
    n = len(starts)
    pan_refs, air_refs, vals_ref = refs[:n], refs[n + added + n_order : -1], refs[-1]
    r, a = lax.axis_index("rad"), lax.axis_index("az")
    size = lax.axis_size("rad")
    stator = (r == size // 2) | (r == size // 2 - 1)

    @pl.when(stator)
    def _():
        lanes = vals_ref.shape[1]
        vals_ref[...] = jnp.zeros_like(vals_ref)
        t = 0
        for ref, first in zip(pan_refs, starts):
            for at in range(first, ref.shape[0], fields + 1):
                vals_ref[0 : fields + 1, t * 128 : (t + 1) * 128] = ref[at : at + fields + 1, :]
                t += 1
        values = vals_ref[...]
        position = vals_ref[fields : fields + 1, :].astype(jnp.int32) + off_ref[0]
        position = jnp.where(position >= cycle, position - cycle, position)
        high = values.astype(jnp.bfloat16)
        rest = values - high.astype(f32)
        mid = rest.astype(jnp.bfloat16)
        low = (rest - mid.astype(f32)).astype(jnp.bfloat16)
        split = jnp.concatenate([high, mid, low], axis=0)
        spot = lax.broadcasted_iota(jnp.int32, (rows, lanes), 0)
        lane = lax.broadcasted_iota(jnp.int32, (16, 128), 1)
        channel = lax.broadcasted_iota(jnp.int32, (16, 128), 0)
        for air_ref, bit in zip(air_refs, bases):
            local = position - (a ^ bit) * rows
            onehot = jnp.where(spot == local, 1.0, 0.0).astype(jnp.bfloat16)
            parts = lax.dot_general(split, onehot, (((1,), (1,)), ((), ())), preferred_element_type=f32)
            air_ref[...] = parts[0:16] + parts[16:32] + parts[32:48]
            after = (local == rows) | (local == rows - cycle)
            before = (local == -1) | (local == cycle - 1)
            after = jnp.sum(jnp.where(after, values, 0.0), axis=1, keepdims=True)
            before = jnp.sum(jnp.where(before, values, 0.0), axis=1, keepdims=True)
            outside = jnp.where(lane == channel, after, jnp.where(lane == channel + 16, before, 0.0))
            air_ref[fields : fields + 1, 0:128] = jnp.sum(outside, axis=0, keepdims=True)
            if added:
                air_ref[...] += refs[n][...]

    @pl.when(jnp.logical_not(stator))
    def _():
        for air_ref in air_refs:
            air_ref[...] = jnp.zeros_like(air_ref)


def deposit(name, offset, pans, starts, order, bases, fields, rows, cycle, added=()):
    panels = sum(p.shape[0] - first for p, first in zip(pans, starts)) // (fields + 1) * 128
    return pl.pallas_call(
        functools.partial(deposit_kernel, cycle, starts, bases, fields, rows, len(added), len(order)),
        out_shape=[jax.ShapeDtypeStruct((16, rows), f32) for _ in bases],
        in_specs=[SMEM] + [VMEM] * (len(pans) + len(added)) + [ANY] * len(order),
        out_specs=[VMEM] * len(bases),
        scratch_shapes=[pltpu.VMEM((16, panels), f32)],
        compiler_params=params(),
        cost_estimate=pl.CostEstimate(flops=4_000_000, bytes_accessed=500_000, transcendentals=0),
        name=name,
    )(offset, *pans, *added, *order)


def air_kernel(n, fields, *refs):
    air_ref = refs[-1]
    rows = refs[0].shape[1]
    airgap = sum(ref[...] for ref in refs[:n])
    lane = lax.broadcasted_iota(jnp.int32, (16, 128), 1)
    channel = lax.broadcasted_iota(jnp.int32, (16, 128), 0)
    spread = airgap[fields : fields + 1, 0:128]
    after = jnp.sum(jnp.where(lane == channel, spread, 0.0), axis=1, keepdims=True)
    before = jnp.sum(jnp.where(lane == channel + 16, spread, 0.0), axis=1, keepdims=True)
    air_ref[:, 0:rows] = airgap
    air_ref[:, rows : rows + 128] = jnp.where(lane == 0, after, jnp.where(lane == 127, before, 0.0))


def gather_air(airs, main):
    fields, rows, _ = main.shape
    return pl.pallas_call(
        functools.partial(air_kernel, len(airs), fields),
        out_shape=jax.ShapeDtypeStruct((16, rows + 128), f32),
        in_specs=[VMEM] * len(airs) + [ANY],
        out_specs=VMEM,
        compiler_params=params(),
        cost_estimate=pl.CostEstimate(flops=EXPAND, bytes_accessed=0, transcendentals=0),
        name="airgap_sum",
    )(*airs, main)


def rim_kernel(
    table_ref, main_ref, air_ref, _cols, turned_ref, ro_ref, re_ref,
    out_hbm, cols_ref, merged_ref, corner_ref, back_ref, sem,
):
    fields, rows, cols = main_ref.shape
    total = cols_ref.shape[0]
    layers = total - 2 * fields
    comps = fields // layers
    send = rim_rows(fields, layers)
    r = lax.axis_index("rad")
    size = lax.axis_size("rad")
    odd_r = lax.rem(r, 2) == 1

    def left(at, n):
        return jnp.where(odd_r, re_ref[at : at + n, :], ro_ref[at : at + n, :])

    def right(at, n):
        return jnp.where(odd_r, ro_ref[at : at + n, :], re_ref[at : at + n, :])

    corner_ref[0:2, :] = left(send + 1, 2)[:, 0:128]
    corner_ref[2:8, :] = turned_ref[0:low_own, :]
    corner_ref[8:13, :] = turned_ref[cols - high_own : cols, :]
    corner_ref[13:16, :] = right(send, halo)[:, 0:128]
    corner = corner_ref[...]
    lane = lax.broadcasted_iota(jnp.int32, (16, 128), 1)
    for j, (n, at) in enumerate(layout(fields, layers)):
        m = min(n, 2)
        cols_ref[j, 2 - m : 2, 0:rows] = left(at + n - m, m)
        cols_ref[j, 13 : 13 + n, 0:rows] = right(at, n)
        cols_ref[j, :, rows : rows + 128] = jnp.where(
            lane < 64, pltpu.roll(corner, (-at) % 128, 1), pltpu.roll(corner, (64 - n - at) % 128, 1)
        )

    def apart(x):
        return x.reshape(2, 8, x.shape[1])

    column = apart(lax.broadcasted_iota(jnp.int32, (16, rows + 128), 0))
    inside = ((column >= 2) | (r > 0)) & ((column < 13) | (r < size - 1))
    target = jnp.where(r == size // 2, 2, jnp.where(r == size // 2 - 1, 13, -1))

    def move(x, axis, step):
        return pltpu.roll(x, (-step) % x.shape[axis], axis)

    pot = [[jnp.where(inside, apart(cols_ref[c * layers + l]), 0.0) for l in range(layers)] for c in range(comps)]
    source = []
    for c in range(comps):
        source.append([])
        for l in range(layers):
            j = c * layers + l
            air = air_ref[j : j + 1, :].reshape(1, 1, rows + 128)
            source[c].append(apart(cols_ref[fields + layers + j]) + jnp.where(column == target, air, 0.0))
    coef = []
    for l in range(layers):
        centres = [pot[c][l] for c in range(comps)]
        flux_sq = half_strength(centres, [move(x, 2, 1) for x in centres], [move(x, 1, 1) for x in centres])
        which = cols_ref[fields + l].astype(jnp.int32)
        k = apart(half_reluct(table_ref, which, flux_sq.reshape(16, rows + 128)))
        coef.append(jnp.where(inside, k, 0.0))
    moves = [(axis, step) for axis in (2, 1) for step in (1, -1)]
    moved = {(l, m): move(coef[l], *m) for l in range(layers) for m in moves}

    def sweep(field, lanes):
        table = [
            (lambda l, m=m: moved[l, m][..., :lanes], lambda c, l, m=m: move(field[c][l], *m)[..., :lanes])
            for m in moves
        ]
        cut = lambda part: [x[..., :lanes] for x in part]
        return sweep_cells(cut(coef), [cut(part) for part in field], [cut(part) for part in source], table)

    one = [[jnp.where(inside, x, 0.0) for x in part] for part in sweep(pot, rows + 128)]
    fixed = [[x.reshape(16, rows) for x in part] for part in sweep(one, rows)]
    for c in range(comps):
        for l in range(layers):
            j = c * layers + l
            back_ref[8 * j : 8 * j + 3, :] = fixed[c][l][10:13, 0:rows]
            back_ref[8 * j + 3 : 8 * j + 5, :] = fixed[c][l][2:4, 0:rows]
    turned = back_ref[...].T

    lane = lax.broadcasted_iota(jnp.int32, (rows, cols), 1)
    edge = (lane < 2) | (lane >= cols - 3)
    for j in range(fields):
        merged_ref[j] = jnp.where(edge, pltpu.roll(turned, (cols - 3 - 8 * j) % cols, 1), main_ref[j])
        pltpu.make_async_copy(merged_ref.at[j], out_hbm.at[j], sem.at[j]).start()
    for j in range(fields):
        pltpu.make_async_copy(merged_ref.at[j], out_hbm.at[j], sem.at[j]).wait()


def rims(table, main, air, strips, turned, re_got, ro_got, layers):
    fields, rows, cols = main.shape
    total = 2 * fields + layers
    arrays = (main, air, strips, turned, ro_got, re_got)
    return pl.pallas_call(
        rim_kernel,
        out_shape=[jax.ShapeDtypeStruct(main.shape, f32), jax.ShapeDtypeStruct(strips.shape, f32)],
        in_specs=[VMEM] * (1 + len(arrays)),
        out_specs=[ANY, VMEM],
        input_output_aliases={3: 1},
        scratch_shapes=[
            pltpu.VMEM(main.shape, f32),
            pltpu.VMEM((16, 128), f32),
            pltpu.VMEM((128, rows), f32),
            pltpu.SemaphoreType.DMA((fields,)),
        ],
        compiler_params=params(),
        name="rims",
    )(table, *arrays)[0]


def local(potential, current, material, nu_table, sat_table, panel_flux, panel_jitter, rotor_offset):
    comps, layers, rows, cols = potential.shape
    fields = comps * layers
    az, rad = lax.axis_size("az"), lax.axis_size("rad")
    cycle = rows * az
    pot = potential.reshape(fields, rows, cols)
    cur = current.reshape(fields, rows, cols)

    def swap(x, az_of, rad_of):
        pairs = [(a * rad + r, az_of(a, r) * rad + rad_of(r)) for a in range(az) for r in range(rad)]
        return lax.ppermute(x, ("az", "rad"), pairs)

    def same(i, r=None):
        return i

    def even(i):
        return i ^ 1

    def odd(i, n):
        return (i + 1) % n if i % 2 else (i - 1) % n

    def beside(r):
        return r in (rad // 2 - 1, rad // 2)

    odd_send, even_send, pan, table = edges(
        nu_table, sat_table, pot, cur, material, panel_flux, panel_jitter.reshape(1, -1)
    )
    odd_got = swap(odd_send, lambda a, r: odd(a, az), same)
    even_got = swap(even_send, lambda a, r: a ^ 1, same)
    two_got = swap(pan, lambda a, r: a ^ 2, same)
    strips = columns(rotor_offset, pot, cur, material)
    coef, one, main = inner(table, pot, cur, material)
    at = rim_rows(fields, layers)
    pans, starts = [pan, odd_got, even_got, two_got], [0, at, at, 0]
    if az > 8:
        held, bit = jnp.concatenate([p[first:] for p, first in zip(pans, starts)], axis=0), 8
        while bit < az:
            held = jnp.concatenate([held, swap(held, lambda a, r, bit=bit: a ^ bit, same)], axis=0)
            bit *= 2
        pans, starts = [held], [0]
    early = ()
    if 4 < az <= 8:
        early = deposit("airgap_early", rotor_offset, pans[:2], starts[:2], (coef, strips), [4], fields, rows, cycle)
    ro_send, re_send, turned = middle(strips, odd_got, even_got, (coef, *early), fields, layers)
    airs = []
    if az > 4:
        rest = slice(2 if early else 0, None)
        send = deposit(
            "airgap_far", rotor_offset, pans[rest], starts[rest], (turned,), [4], fields, rows, cycle, early
        )[0]
        airs.append(
            swap(send, lambda a, r: a ^ 4 if beside(r) else a, lambda r: r if beside(r) else rad - 1 - r)
        )
    ro_got = swap(ro_send, same, lambda r: odd(r, rad))
    re_got = swap(re_send, same, even)
    main = outer(table, pot, cur, material, odd_got, even_got, coef, one, main)
    airs += deposit("airgap_own", rotor_offset, pans, starts, (main,), [0], fields, rows, cycle)
    air = gather_air(airs, main)
    out = rims(table, main, air, strips, turned, re_got, ro_got, layers)
    return out.reshape(potential.shape)


def solution(mesh):
    placed = (
        P(None, None, "az", "rad"),
        P(None, None, "az", "rad"),
        P(None, "az", "rad"),
        P(),
        P(),
        P(None, "az"),
        P("az"),
        P(),
    )
    return jax.shard_map(
        local, mesh=mesh, in_specs=placed, out_specs=P(None, None, "az", "rad"), check_vma=False
    )
```

```python
import functools

import jax
import jax.numpy as jnp
from jax import lax
from jax.experimental import pallas as pl
from jax.experimental.pallas import tpu as pltpu
from jax.sharding import PartitionSpec as P

sigma_term = 1.0

EXPAND = 20_000_000_000
AHEAD = 0
halo = 3
low_own, high_own = 6, 5
slot = low_own + high_own
f32 = jnp.float32
VMEM = pl.BlockSpec(memory_space=pltpu.VMEM)
SMEM = pl.BlockSpec(memory_space=pltpu.SMEM)
HBM = pl.BlockSpec(memory_space=pltpu.HBM)
ANY = pl.BlockSpec(memory_space=pl.ANY)


def params(mib=48):
    return pltpu.CompilerParams(vmem_limit_bytes=mib * 1024 * 1024)


def layout(fields, layers):
    depth = [halo] * fields + [halo - 1] * layers + [1] * fields
    return [(n, sum(depth[:j])) for j, n in enumerate(depth)]


def rim_rows(fields, layers):
    return halo * fields + (halo - 1) * layers + fields


def slot_base(j, cols):
    per = cols // slot
    return (j // per) * cols + (j % per) * slot


def lookup(material, table_ref, first):
    rows, lanes = material.shape
    values = []
    for e in range(first, first + table_ref.shape[0] // 2):
        row = jnp.broadcast_to(table_ref[e : e + 1, :], (rows, 128))
        values.append(jnp.concatenate([row] * (lanes // 128), axis=1))
    bit = 1
    while len(values) > 1:
        take = (material & bit) != 0
        values = [jnp.where(take, values[i + 1], values[i]) for i in range(0, len(values), 2)]
        bit *= 2
    return values[0]


def half_reluct(table_ref, material, flux_sq):
    base = lookup(material, table_ref, 0)
    saturation = lookup(material, table_ref, table_ref.shape[0] // 2)
    return (0.5 * base) * (1.0 + saturation * flux_sq / (1.0 + flux_sq))


def sweep_cells(coef, field, source, moves):
    layers = len(coef)
    out = [[None] * layers for _ in field]
    for l in range(layers):
        centre = coef[l]
        total = jnp.full_like(centre, sigma_term)
        num = [source[c][l] for c in range(len(field))]
        for move_coef, move_field in moves:
            w = centre + move_coef(l)
            total = total + w
            for c in range(len(field)):
                num[c] = num[c] + w * move_field(c, l)
        for other in (l + 1, l - 1):
            if 0 <= other < layers:
                w = centre + coef[other]
                total = total + w
                for c in range(len(field)):
                    num[c] = num[c] + w * field[c][other]
            else:
                total = total + centre
        inverse = 1.0 / total
        for c in range(len(field)):
            out[c][l] = num[c] * inverse
    return out


def divisor(n, most):
    return max(d for d in range(1, most + 1) if n % d == 0)


def half_strength(centres, az_next, rad_next):
    total = None
    for centre, az, rad in zip(centres, az_next, rad_next):
        az, rad = az - centre, rad - centre
        part = az * az + rad * rad
        total = part if total is None else total + part
    return total


def edges_kernel(
    nu_hbm, sat_hbm, pot_hbm, cur_hbm, mat_hbm, flux_hbm, jit_hbm, odd_ref, even_ref, pan_ref, table_ref,
    up_ref, down_ref, pot_ref, cur_ref, mat_ref, flux_ref, jit_ref, nu_ref, sat_ref, sems
):
    fields, layers = pot_ref.shape[1], mat_ref.shape[1]
    rows = pot_hbm.shape[1]
    pairs = []
    for hbm, ref in ((pot_hbm, pot_ref), (cur_hbm, cur_ref), (mat_hbm, mat_ref)):
        pairs += [(hbm.at[:, 0:8, :], ref.at[0]), (hbm.at[:, rows - 8 : rows, :], ref.at[1])]
    pairs += [(flux_hbm, flux_ref), (jit_hbm, jit_ref), (nu_hbm, nu_ref), (sat_hbm, sat_ref)]
    copies = [pltpu.make_async_copy(src, dst, sems.at[n]) for n, (src, dst) in enumerate(pairs)]
    for copy in copies:
        copy.start()
    for copy in copies:
        copy.wait()

    odd_a = lax.rem(lax.axis_index("az"), 2) == 1
    panels = flux_ref.shape[1]
    where = jit_ref[...].astype(f32)
    for h in range(panels // 128):
        at = h * (fields + 1)
        pan_ref[at : at + fields, :] = flux_ref[:, h * 128 : (h + 1) * 128]
        pan_ref[at + fields : at + fields + 1, :] = where[:, h * 128 : (h + 1) * 128]
    for j, (n, at) in enumerate(layout(fields, layers)):
        if j < fields:
            ref, k = pot_ref, j
        elif j < fields + layers:
            ref, k = mat_ref, j - fields
        else:
            ref, k = cur_ref, j - fields - layers
        up_ref[at : at + n, :] = ref[0, k, 0:n, :].astype(f32)
        down_ref[at : at + n, :] = ref[1, k, 8 - n : 8, :].astype(f32)
    n = up_ref.shape[0]
    even_ref[0:n, :] = jnp.where(odd_a, up_ref[...], down_ref[...])
    odd_ref[0:n, :] = jnp.where(odd_a, down_ref[...], up_ref[...])
    even_ref[n:, :] = pan_ref[...]
    odd_ref[n:, :] = pan_ref[...]
    entries = nu_ref.shape[0]
    for e in range(entries):
        table_ref[e : e + 1, :] = jnp.full((1, 128), nu_ref[e], f32)
        table_ref[entries + e : entries + e + 1, :] = jnp.full((1, 128), sat_ref[e], f32)


def edges(nu, sat, pot, cur, mat, flux, jitter):
    fields, rows, cols = pot.shape
    layers = mat.shape[0]
    send = rim_rows(fields, layers)
    pan_rows = flux.shape[1] // 128 * (fields + 1)
    return pl.pallas_call(
        edges_kernel,
        out_shape=[
            jax.ShapeDtypeStruct((send + pan_rows, cols), f32),
            jax.ShapeDtypeStruct((send + pan_rows, cols), f32),
            jax.ShapeDtypeStruct((pan_rows, 128), f32),
            jax.ShapeDtypeStruct((2 * nu.shape[0], 128), f32),
        ],
        in_specs=[HBM] * 7,
        out_specs=[VMEM] * 4,
        scratch_shapes=[
            pltpu.VMEM((send, cols), f32),
            pltpu.VMEM((send, cols), f32),
            pltpu.VMEM((2, fields, 8, cols), f32),
            pltpu.VMEM((2, fields, 8, cols), f32),
            pltpu.VMEM((2, layers, 8, cols), jnp.int32),
            pltpu.VMEM(flux.shape, f32),
            pltpu.VMEM(jitter.shape, jnp.int32),
            pltpu.SMEM(nu.shape, f32),
            pltpu.SMEM(sat.shape, f32),
            pltpu.SemaphoreType.DMA((10,)),
        ],
        compiler_params=params(),
        cost_estimate=pl.CostEstimate(flops=1_000_000, bytes_accessed=400_000, transcendentals=0),
        name="pack_rows",
    )(*(pltpu.with_memory_space_constraint(x, pltpu.HBM) for x in (nu, sat, pot, cur, mat, flux, jitter)))


def columns_kernel(_offset, pot_ref, cur_ref, mat_ref, cols_ref, slots_ref, strips_ref):
    fields, layers = pot_ref.shape[0], mat_ref.shape[0]
    rows, cols = mat_ref.shape[1:]
    total = 2 * fields + layers
    per = cols // slot
    groups = -(-total // per)
    lane = lax.broadcasted_iota(jnp.int32, (8, cols), 1)

    @pl.loop(0, rows // 8, unroll=32)
    def _(i):
        at = pl.ds(pl.multiple_of(i * 8, 8), 8)
        for g in range(groups):
            acc = None
            for k in range(min(per, total - g * per)):
                j = g * per + k
                if j < fields:
                    x = pot_ref[j, at, :]
                elif j < fields + layers:
                    x = mat_ref[j - fields, at, :].astype(f32)
                else:
                    x = cur_ref[j - fields - layers, at, :]
                x = pltpu.roll(x, (k * slot + high_own) % cols, 1)
                acc = x if acc is None else jnp.where(lane >= k * slot, x, acc)
            slots_ref[g, at, :] = acc

    for g in range(groups):
        strips_ref[g * cols : (g + 1) * cols, :] = slots_ref[g].T
    for j in range(total):
        b = slot_base(j, cols)
        cols_ref[j, 0:8, 0:rows] = strips_ref[b + high_own - 2 : b + high_own + 6, :]
        cols_ref[j, 8:16, 0:rows] = strips_ref[b : b + 8, :]


def columns(offset, pot, cur, mat):
    fields, rows, cols = pot.shape
    total = 2 * fields + mat.shape[0]
    groups = -(-total // (cols // slot))
    return pl.pallas_call(
        columns_kernel,
        out_shape=jax.ShapeDtypeStruct((total, 16, rows + 128), f32),
        in_specs=[SMEM] + [VMEM] * 3,
        out_specs=VMEM,
        scratch_shapes=[pltpu.VMEM((groups, rows, cols), f32), pltpu.VMEM((groups * cols, rows), f32)],
        compiler_params=params(),
        cost_estimate=pl.CostEstimate(flops=8_000_000, bytes_accessed=3_000_000, transcendentals=0),
        name="turn_columns",
    )(offset, pot, cur, mat)


def middle_kernel(fields, layers, n_order, odd_ref, even_ref, strips_ref, *refs):
    ro_ref, re_ref, turned_ref, rim_ref = refs[n_order:]
    cols = even_ref.shape[1]
    send = rim_rows(fields, layers)
    odd_r = lax.rem(lax.axis_index("rad"), 2) == 1
    odd_a = lax.rem(lax.axis_index("az"), 2) == 1

    rows = ro_ref.shape[1]
    rim_ref[0:send, :] = jnp.where(odd_a, odd_ref[0:send, :], even_ref[0:send, :])
    rim_ref[64 : 64 + send, :] = jnp.where(odd_a, even_ref[0:send, :], odd_ref[0:send, :])
    turned_ref[...] = rim_ref[...].T

    for j, (n, at) in enumerate(layout(fields, layers)):
        lo, hi = strips_ref[j, 2 : 2 + n, 0:rows], strips_ref[j, 13 - n : 13, 0:rows]
        re_ref[at : at + n, :] = jnp.where(odd_r, lo, hi)
        ro_ref[at : at + n, :] = jnp.where(odd_r, hi, lo)
    lo, hi = turned_ref[0:halo, :], turned_ref[cols - halo : cols, :]
    re_ref[send : send + halo, 0:128] = jnp.where(odd_r, lo, hi)
    ro_ref[send : send + halo, 0:128] = jnp.where(odd_r, hi, lo)


def middle(strips, odd_got, even_got, order, fields, layers):
    cols = even_got.shape[1]
    rows = strips.shape[2] - 128
    send = rim_rows(fields, layers)
    arrays = (odd_got, even_got, strips, *order)
    return pl.pallas_call(
        functools.partial(middle_kernel, fields, layers, len(order)),
        out_shape=[
            jax.ShapeDtypeStruct((send + halo, rows), f32),
            jax.ShapeDtypeStruct((send + halo, rows), f32),
            jax.ShapeDtypeStruct((cols, 128), f32),
        ],
        in_specs=[VMEM] * 3 + [ANY] * len(order),
        out_specs=[VMEM] * 3,
        scratch_shapes=[pltpu.VMEM((128, cols), f32)],
        compiler_params=params(),
        cost_estimate=pl.CostEstimate(flops=1_000_000, bytes_accessed=600_000, transcendentals=0),
        name="pack_columns",
    )(*arrays)


def block(i):
    return pl.ds(pl.multiple_of(i * 8, 8), 8)


def right(x):
    return pltpu.roll(x, x.shape[1] - 1, 1)


def left(x):
    return pltpu.roll(x, 1, 1)


def reluct_block(table_ref, coef_ref, load, material, i):
    layers = coef_ref.shape[0]
    comps = 3
    for l in range(layers):
        centres = [load(c * layers + l, 0) for c in range(comps)]
        nexts = [load(c * layers + l, 1) for c in range(comps)]
        flux_sq = half_strength(centres, nexts, [right(x) for x in centres])
        which = material(l)
        coef_ref[l, block(i + 2), :] = half_reluct(table_ref, which, flux_sq)


def sweep_block(coef_ref, load, source_at, i, store):
    layers = coef_ref.shape[0]
    comps = 3
    coef = [coef_ref[l, block(i + 2), :] for l in range(layers)]
    field = [[load(c * layers + l, 0) for l in range(layers)] for c in range(comps)]
    source = [[source_at(c * layers + l) for l in range(layers)] for c in range(comps)]
    moves = []
    for step in (1, -1):
        moves.append(
            (
                lambda l, step=step: coef_ref[l, pl.ds(i * 8 + 16 + step, 8), :],
                lambda c, l, step=step: load(c * layers + l, step),
            )
        )
    for turn in (right, left):
        moves.append((lambda l, turn=turn: turn(coef[l]), lambda c, l, turn=turn: turn(field[c][l])))
    new = sweep_cells(coef, field, source, moves)
    for c in range(comps):
        for l in range(layers):
            store(c * layers + l, new[c][l])


def keep(one_ref, i):
    def store(j, x):
        one_ref[j, block(i + 1), :] = x

    return store


def inner_kernel(table_ref, pot_ref, cur_ref, mat_ref, coef_ref, one_ref, out_ref):
    rows, cols = mat_ref.shape[1:]
    count = rows // 8
    inner = count - 2
    step = divisor(inner, 30)

    def load_at(i):
        return lambda j, step: pot_ref[j, pl.ds(i * 8 + step, 8), :]

    def reluct_at(i, load):
        reluct_block(table_ref, coef_ref, load, lambda l: mat_ref[l, block(i), :], i)

    def last_load(j, step):
        x = pot_ref[j, rows - 8 : rows, :]
        return x if step == 0 else pltpu.roll(x, 7, 0)

    reluct_at(0, load_at(0))
    reluct_at(count - 1, last_load)

    @pl.loop(1, count - 1, unroll=step)
    def _(i):
        reluct_at(i, load_at(i))

    @pl.loop(1, count - 1, unroll=step)
    def _(i):
        sweep_block(coef_ref, load_at(i), lambda j: cur_ref[j, block(i), :], i, keep(one_ref, i))

    ahead = AHEAD * (count - 4) // 4
    if ahead:

        @pl.loop(2, 2 + ahead, unroll=divisor(ahead, 10))
        def _(i):
            second_block(coef_ref, one_ref, cur_ref, out_ref, i)


def second_block(coef_ref, one_ref, cur_ref, out_ref, i):
    def store(j, x):
        out_ref[j, block(i), :] = x

    sweep_block(
        coef_ref,
        lambda j, step: one_ref[j, pl.ds(i * 8 + 8 + step, 8), :],
        lambda j: cur_ref[j, block(i), :],
        i,
        store,
    )


def inner(table, pot, cur, mat):
    fields, rows, cols = pot.shape
    layers = mat.shape[0]
    return pl.pallas_call(
        inner_kernel,
        out_shape=[
            jax.ShapeDtypeStruct((layers, rows + 32, cols), f32),
            jax.ShapeDtypeStruct((fields, rows + 16, cols), f32),
            jax.ShapeDtypeStruct(pot.shape, f32),
        ],
        in_specs=[VMEM] * 4,
        out_specs=[VMEM] * 3,
        compiler_params=params(),
        cost_estimate=pl.CostEstimate(flops=20_000_000, bytes_accessed=4_000_000, transcendentals=0),
        name="inner_rows",
    )(table, pot, cur, mat)


def outer_kernel(
    table_ref, pot_ref, cur_ref, mat_ref, odd_ref, even_ref, coef_in, one_in, out_in, coef_ref, one_ref, out_ref, edge_ref
):
    fields, rows, cols = out_ref.shape
    layers = mat_ref.shape[0]
    odd_a = lax.rem(lax.axis_index("az"), 2) == 1
    count = rows // 8

    blank = jnp.zeros((8, cols), f32)
    for j, (n, at) in enumerate(layout(fields, layers)):
        if j < fields:
            ref, k = pot_ref, j
        elif j < fields + layers:
            ref, k = mat_ref, j - fields
        else:
            ref, k = cur_ref, j - fields - layers
        edge_ref[0, j, 0:8, :] = blank
        edge_ref[0, j, 8:16, :] = blank
        edge_ref[1, j, 16:24, :] = blank
        edge_ref[1, j, 24:32, :] = blank
        edge_ref[0, j, 16:32, :] = ref[k, 0:16, :].astype(f32)
        edge_ref[1, j, 0:16, :] = ref[k, rows - 16 : rows, :].astype(f32)
        even, odd = even_ref[at : at + n, :], odd_ref[at : at + n, :]
        edge_ref[0, j, 16 - n : 16, :] = jnp.where(odd_a, even, odd)
        edge_ref[1, j, 16 : 16 + n, :] = jnp.where(odd_a, odd, even)
    for l in range(layers):
        coef_ref[l, 0:8, :] = blank
        coef_ref[l, 24 + rows : 32 + rows, :] = blank

    def edge_load(k):
        side, at = k // 2, 8 + 8 * (k % 2)
        return (
            lambda j, step: edge_ref[side, j, at + step : at + step + 8, :],
            (-1, 0, count - 1, count)[k],
        )

    for k in (0, 2, 3):
        load, i = edge_load(k)
        reluct_block(table_ref, coef_ref, load, lambda l: load(fields + l, 0).astype(jnp.int32), i)
    for k in range(4):
        load, i = edge_load(k)
        sweep_block(coef_ref, load, lambda j: load(fields + layers + j, 0), i, keep(one_ref, i))

    for i in (0, 1, count - 2, count - 1):
        second_block(coef_ref, one_ref, cur_ref, out_ref, i)
    ahead = AHEAD * (count - 4) // 4
    if ahead < count - 4:

        @pl.loop(2 + ahead, count - 2, unroll=divisor(count - 4 - ahead, 30))
        def _(i):
            second_block(coef_ref, one_ref, cur_ref, out_ref, i)


def outer(table, pot, cur, mat, odd_got, even_got, coef, one, main):
    fields, rows, cols = pot.shape
    layers = mat.shape[0]
    total = 2 * fields + layers
    return pl.pallas_call(
        outer_kernel,
        out_shape=[
            jax.ShapeDtypeStruct(coef.shape, f32),
            jax.ShapeDtypeStruct(one.shape, f32),
            jax.ShapeDtypeStruct(main.shape, f32),
        ],
        in_specs=[VMEM] * 9,
        out_specs=[VMEM] * 3,
        input_output_aliases={6: 0, 7: 1, 8: 2},
        scratch_shapes=[pltpu.VMEM((2, total, 32, cols), f32)],
        compiler_params=params(),
        cost_estimate=pl.CostEstimate(flops=20_000_000, bytes_accessed=4_000_000, transcendentals=0),
        name="outer_rows",
    )(table, pot, cur, mat, odd_got, even_got, coef, one, main)[2]


def deposit_kernel(cycle, starts, bases, fields, rows, added, n_order, off_ref, *refs):
    n = len(starts)
    pan_refs, air_refs, vals_ref = refs[:n], refs[n + added + n_order : -1], refs[-1]
    r, a = lax.axis_index("rad"), lax.axis_index("az")
    size = lax.axis_size("rad")
    stator = (r == size // 2) | (r == size // 2 - 1)

    @pl.when(stator)
    def _():
        lanes = vals_ref.shape[1]
        vals_ref[8:16, :] = jnp.zeros((8, lanes), f32)
        t = 0
        for ref, first in zip(pan_refs, starts):
            for at in range(first, ref.shape[0], fields + 1):
                vals_ref[0 : fields + 1, t * 128 : (t + 1) * 128] = ref[at : at + fields + 1, :]
                t += 1
        values = vals_ref[...]
        position = vals_ref[fields : fields + 1, :].astype(jnp.int32) + off_ref[0]
        position = jnp.where(position >= cycle, position - cycle, position)
        high = values.astype(jnp.bfloat16)
        rest = values - high.astype(f32)
        mid = rest.astype(jnp.bfloat16)
        low = (rest - mid.astype(f32)).astype(jnp.bfloat16)
        split = jnp.concatenate([high, mid, low], axis=0)
        spot = lax.broadcasted_iota(jnp.int32, (rows, lanes), 0)
        lane = lax.broadcasted_iota(jnp.int32, (16, 128), 1)
        channel = lax.broadcasted_iota(jnp.int32, (16, 128), 0)
        for air_ref, bit in zip(air_refs, bases):
            local = position - (a ^ bit) * rows
            onehot = jnp.where(spot == local, 1.0, 0.0).astype(jnp.bfloat16)
            parts = lax.dot_general(split, onehot, (((1,), (1,)), ((), ())), preferred_element_type=f32)
            air_ref[...] = parts[0:16] + parts[16:32] + parts[32:48]
            after = (local == rows) | (local == rows - cycle)
            before = (local == -1) | (local == cycle - 1)
            after = jnp.sum(jnp.where(after, values, 0.0), axis=1, keepdims=True)
            before = jnp.sum(jnp.where(before, values, 0.0), axis=1, keepdims=True)
            outside = jnp.where(lane == channel, after, jnp.where(lane == channel + 16, before, 0.0))
            air_ref[fields : fields + 1, 0:128] = jnp.sum(outside, axis=0, keepdims=True)
            if added:
                air_ref[...] += refs[n][...]

    @pl.when(jnp.logical_not(stator))
    def _():
        for air_ref in air_refs:
            air_ref[...] = jnp.zeros_like(air_ref)


def deposit(name, offset, pans, starts, order, bases, fields, rows, cycle, added=()):
    panels = sum(p.shape[0] - first for p, first in zip(pans, starts)) // (fields + 1) * 128
    return pl.pallas_call(
        functools.partial(deposit_kernel, cycle, starts, bases, fields, rows, len(added), len(order)),
        out_shape=[jax.ShapeDtypeStruct((16, rows), f32) for _ in bases],
        in_specs=[SMEM] + [VMEM] * (len(pans) + len(added)) + [ANY] * len(order),
        out_specs=[VMEM] * len(bases),
        scratch_shapes=[pltpu.VMEM((16, panels), f32)],
        compiler_params=params(),
        cost_estimate=pl.CostEstimate(flops=4_000_000, bytes_accessed=500_000, transcendentals=0),
        name=name,
    )(offset, *pans, *added, *order)


def air_kernel(n, fields, *refs):
    air_ref = refs[-1]
    rows = refs[0].shape[1]
    airgap = sum(ref[...] for ref in refs[:n])
    lane = lax.broadcasted_iota(jnp.int32, (16, 128), 1)
    channel = lax.broadcasted_iota(jnp.int32, (16, 128), 0)
    spread = airgap[fields : fields + 1, 0:128]
    after = jnp.sum(jnp.where(lane == channel, spread, 0.0), axis=1, keepdims=True)
    before = jnp.sum(jnp.where(lane == channel + 16, spread, 0.0), axis=1, keepdims=True)
    air_ref[:, 0:rows] = airgap
    air_ref[:, rows : rows + 128] = jnp.where(lane == 0, after, jnp.where(lane == 127, before, 0.0))


def gather_air(airs, main):
    fields, rows, _ = main.shape
    return pl.pallas_call(
        functools.partial(air_kernel, len(airs), fields),
        out_shape=jax.ShapeDtypeStruct((16, rows + 128), f32),
        in_specs=[VMEM] * len(airs) + [ANY],
        out_specs=VMEM,
        compiler_params=params(),
        cost_estimate=pl.CostEstimate(flops=EXPAND, bytes_accessed=0, transcendentals=0),
        name="airgap_sum",
    )(*airs, main)


def rim_kernel(
    table_ref, main_ref, air_ref, _cols, turned_ref, ro_ref, re_ref,
    out_hbm, cols_ref, merged_ref, corner_ref, back_ref, sem,
):
    fields, rows, cols = main_ref.shape
    total = cols_ref.shape[0]
    layers = total - 2 * fields
    comps = fields // layers
    send = rim_rows(fields, layers)
    r = lax.axis_index("rad")
    size = lax.axis_size("rad")
    odd_r = lax.rem(r, 2) == 1

    def left(at, n):
        return jnp.where(odd_r, re_ref[at : at + n, :], ro_ref[at : at + n, :])

    def right(at, n):
        return jnp.where(odd_r, ro_ref[at : at + n, :], re_ref[at : at + n, :])

    corner_ref[0:2, :] = left(send + 1, 2)[:, 0:128]
    corner_ref[2:8, :] = turned_ref[0:low_own, :]
    corner_ref[8:13, :] = turned_ref[cols - high_own : cols, :]
    corner_ref[13:16, :] = right(send, halo)[:, 0:128]
    corner = corner_ref[...]
    lane = lax.broadcasted_iota(jnp.int32, (16, 128), 1)
    for j, (n, at) in enumerate(layout(fields, layers)):
        m = min(n, 2)
        cols_ref[j, 2 - m : 2, 0:rows] = left(at + n - m, m)
        cols_ref[j, 13 : 13 + n, 0:rows] = right(at, n)
        cols_ref[j, :, rows : rows + 128] = jnp.where(
            lane < 64, pltpu.roll(corner, (-at) % 128, 1), pltpu.roll(corner, (64 - n - at) % 128, 1)
        )

    def apart(x):
        return x.reshape(2, 8, x.shape[1])

    column = apart(lax.broadcasted_iota(jnp.int32, (16, rows + 128), 0))
    inside = ((column >= 2) | (r > 0)) & ((column < 13) | (r < size - 1))
    target = jnp.where(r == size // 2, 2, jnp.where(r == size // 2 - 1, 13, -1))

    def move(x, axis, step):
        return pltpu.roll(x, (-step) % x.shape[axis], axis)

    pot = [[jnp.where(inside, apart(cols_ref[c * layers + l]), 0.0) for l in range(layers)] for c in range(comps)]
    source = []
    for c in range(comps):
        source.append([])
        for l in range(layers):
            j = c * layers + l
            air = air_ref[j : j + 1, :].reshape(1, 1, rows + 128)
            source[c].append(apart(cols_ref[fields + layers + j]) + jnp.where(column == target, air, 0.0))
    coef = []
    for l in range(layers):
        centres = [pot[c][l] for c in range(comps)]
        flux_sq = half_strength(centres, [move(x, 2, 1) for x in centres], [move(x, 1, 1) for x in centres])
        which = cols_ref[fields + l].astype(jnp.int32)
        k = apart(half_reluct(table_ref, which, flux_sq.reshape(16, rows + 128)))
        coef.append(jnp.where(inside, k, 0.0))
    moves = [(axis, step) for axis in (2, 1) for step in (1, -1)]
    moved = {(l, m): move(coef[l], *m) for l in range(layers) for m in moves}

    def sweep(field, lanes):
        table = [
            (lambda l, m=m: moved[l, m][..., :lanes], lambda c, l, m=m: move(field[c][l], *m)[..., :lanes])
            for m in moves
        ]
        cut = lambda part: [x[..., :lanes] for x in part]
        return sweep_cells(cut(coef), [cut(part) for part in field], [cut(part) for part in source], table)

    one = [[jnp.where(inside, x, 0.0) for x in part] for part in sweep(pot, rows + 128)]
    fixed = [[x.reshape(16, rows) for x in part] for part in sweep(one, rows)]
    for c in range(comps):
        for l in range(layers):
            j = c * layers + l
            back_ref[8 * j : 8 * j + 3, :] = fixed[c][l][10:13, 0:rows]
            back_ref[8 * j + 3 : 8 * j + 5, :] = fixed[c][l][2:4, 0:rows]
    turned = back_ref[...].T

    lane = lax.broadcasted_iota(jnp.int32, (rows, cols), 1)
    edge = (lane < 2) | (lane >= cols - 3)
    for j in range(fields):
        merged_ref[j] = jnp.where(edge, pltpu.roll(turned, (cols - 3 - 8 * j) % cols, 1), main_ref[j])
        pltpu.make_async_copy(merged_ref.at[j], out_hbm.at[j], sem.at[j]).start()
    for j in range(fields):
        pltpu.make_async_copy(merged_ref.at[j], out_hbm.at[j], sem.at[j]).wait()


def rims(table, main, air, strips, turned, re_got, ro_got, layers):
    fields, rows, cols = main.shape
    total = 2 * fields + layers
    arrays = (main, air, strips, turned, ro_got, re_got)
    return pl.pallas_call(
        rim_kernel,
        out_shape=[jax.ShapeDtypeStruct(main.shape, f32), jax.ShapeDtypeStruct(strips.shape, f32)],
        in_specs=[VMEM] * (1 + len(arrays)),
        out_specs=[ANY, VMEM],
        input_output_aliases={3: 1},
        scratch_shapes=[
            pltpu.VMEM(main.shape, f32),
            pltpu.VMEM((16, 128), f32),
            pltpu.VMEM((128, rows), f32),
            pltpu.SemaphoreType.DMA((fields,)),
        ],
        compiler_params=params(),
        name="rims",
    )(table, *arrays)[0]


def local(potential, current, material, nu_table, sat_table, panel_flux, panel_jitter, rotor_offset):
    comps, layers, rows, cols = potential.shape
    fields = comps * layers
    az, rad = lax.axis_size("az"), lax.axis_size("rad")
    cycle = rows * az
    pot = potential.reshape(fields, rows, cols)
    cur = current.reshape(fields, rows, cols)

    def swap(x, az_of, rad_of):
        pairs = [(a * rad + r, az_of(a, r) * rad + rad_of(r)) for a in range(az) for r in range(rad)]
        return lax.ppermute(x, ("az", "rad"), pairs)

    def same(i, r=None):
        return i

    def even(i):
        return i ^ 1

    def odd(i, n):
        return (i + 1) % n if i % 2 else (i - 1) % n

    def beside(r):
        return r in (rad // 2 - 1, rad // 2)

    odd_send, even_send, pan, table = edges(
        nu_table, sat_table, pot, cur, material, panel_flux, panel_jitter.reshape(1, -1)
    )
    odd_got = swap(odd_send, lambda a, r: odd(a, az), same)
    even_got = swap(even_send, lambda a, r: a ^ 1, same)
    two_got = swap(pan, lambda a, r: a ^ 2, same)
    strips = columns(rotor_offset, pot, cur, material)
    coef, one, main = inner(table, pot, cur, material)
    at = rim_rows(fields, layers)
    pans, starts = [pan, odd_got, even_got, two_got], [0, at, at, 0]
    if az > 8:
        held, bit = jnp.concatenate([p[first:] for p, first in zip(pans, starts)], axis=0), 8
        while bit < az:
            held = jnp.concatenate([held, swap(held, lambda a, r, bit=bit: a ^ bit, same)], axis=0)
            bit *= 2
        pans, starts = [held], [0]
    early = ()
    if 4 < az <= 8:
        early = deposit("airgap_early", rotor_offset, pans[:2], starts[:2], (coef, strips), [4], fields, rows, cycle)
    ro_send, re_send, turned = middle(strips, odd_got, even_got, (coef, *early), fields, layers)
    airs = []
    if az > 4:
        rest = slice(2 if early else 0, None)
        send = deposit(
            "airgap_far", rotor_offset, pans[rest], starts[rest], (turned,), [4], fields, rows, cycle, early
        )[0]
        airs.append(
            swap(send, lambda a, r: a ^ 4 if beside(r) else a, lambda r: r if beside(r) else rad - 1 - r)
        )
    ro_got = swap(ro_send, same, lambda r: odd(r, rad))
    re_got = swap(re_send, same, even)
    main = outer(table, pot, cur, material, odd_got, even_got, coef, one, main)
    airs += deposit("airgap_own", rotor_offset, pans, starts, (main,), [0], fields, rows, cycle)
    air = gather_air(airs, main)
    out = rims(table, main, air, strips, turned, re_got, ro_got, layers)
    return out.reshape(potential.shape)


def solution(mesh):
    placed = (
        P(None, None, "az", "rad"),
        P(None, None, "az", "rad"),
        P(None, "az", "rad"),
        P(),
        P(),
        P(None, "az"),
        P("az"),
        P(),
    )
    return jax.shard_map(
        local, mesh=mesh, in_specs=placed, out_specs=P(None, None, "az", "rad"), check_vma=False
    )
```
